32 devices in a mesh: hop: 16 (over z, y, x), par: 2 (over core).
Axes of the slice: x: 2, y: 2, z: 4, core: 2. Of those that a mesh axis runs over, the one named last changes fastest.
Arguments:
- child_feats: bfloat16 [16384, 1024], P(('hop', 'par')), may hold values from -6 to 6
- board_mask: int32 [16384], P(('hop', 'par')), may hold values 0 or 1
- importance: float32 [16384], P(('hop', 'par')), may hold values from 0.1 to 1
- parent_slot: int32 [16384], P(('hop', 'par')), may hold values from 0 to 1023
- send_counts: int32 [32, 32], P(('hop', 'par')), may hold values from 1 to 16, as said below
- parent_feats: bfloat16 [32768, 1024], P(('hop', 'par')), may hold values from -6 to 6
- proj_weight: bfloat16 [1024, 1024], replicated, may hold values from -0.1875 to 0.1875
- q_weight: bfloat16 [1024, 1024], replicated, may hold values from -0.1875 to 0.1875
- q_bias: float32 [1024], replicated, may hold values from -1.5 to 1.5
- w_weight: bfloat16 [2048, 1024], replicated, may hold values from -0.125 to 0.125
- w_bias: float32 [1024], replicated, may hold values from -1.5 to 1.5
- emb_cotangent: float32 [32768, 1024], P(('hop', 'par')), may hold values from -6 to 6
Outputs:
- embedding: float32 [32768, 1024], P(('hop', 'par'))
- grad_child: bfloat16 [16384, 1024], P(('hop', 'par'))
- grad_parent: float32 [32768, 1024], P(('hop', 'par'))
- grad_proj: float32 [1024, 1024], replicated
- grad_q: float32 [1024, 1024], replicated
- grad_qbias: float32 [1024], replicated
- grad_w: float32 [2048, 1024], replicated
- grad_wbias: float32 [1024], replicated
The draws below stay inside these ranges and needn't reach their ends.
Inputs may be any that keep to these rules, and one draw needn't show every extreme that they name: `send_counts`: in every draw one parent owner receives 16 live slots from every source device.
All inputs are finite; a program needn't handle non-finite values. No bound on the sum of `board_mask` on one device may be relied on, other than what follows from the above.
Results may differ from the reference program's by a relative error of at most 0.0068.
Values may be sent and summed in bfloat16 or wider, within the bound.
A program may use at most 192 MiB of HBM per device.

```python
import jax
import jax.numpy as jnp
from jax import lax

D = 1024
CH_DEV = 512
P_DEV = 1024
SHARDS = 32
CAP = 16
CHILDREN = 16384
PARENTS = 32768


def draw_send_counts(key, part):
    base_counts = jax.random.randint(jax.random.fold_in(key, 11), (SHARDS, SHARDS), 1, CAP + 1)
    hottest = jax.random.randint(jax.random.fold_in(key, 12), (), 0, SHARDS)
    columns = jnp.arange(SHARDS)[None, :]
    return jnp.where(columns == hottest, CAP, base_counts).astype(jnp.int32)


def plant(values, key, low, top_value):
    spot = [jax.random.randint(jax.random.fold_in(key, axis), (), 0, length) for axis, length in enumerate(values.shape)]
    main_axis = values.shape.index(max(values.shape))
    beside = spot[:main_axis] + [(spot[main_axis] + 1) % values.shape[main_axis]] + spot[main_axis + 1:]
    return values.at[tuple(spot)].set(low).at[tuple(beside)].set(top_value)


def levels(stream_key, extent, split, least, largest):
    loudness = 1.0
    for axis_at, parts in split:
        draws = jax.random.uniform(jax.random.fold_in(jax.random.fold_in(stream_key, 6), axis_at), (parts,), jnp.float32, least / len(split), largest / len(split))
        loudness = loudness * jnp.repeat(jnp.exp(draws), extent[axis_at] // parts).reshape((-1,) + (1,) * (len(extent) - 1 - axis_at))
    return loudness


def normal_values(stream_key, shape, scale, bound, split=(), held_as=jnp.bfloat16):
    values = scale * jax.random.normal(stream_key, shape, jnp.float32)
    if split:
        values = values * levels(stream_key, shape, split, -0.22, 0.18)
    return jnp.clip(values, -bound, bound).astype(held_as)


def setup_inputs(seed: int = 0) -> dict:
    splits = jax.random.split(jax.random.key(seed), 13)
    return {
        "child_feats": normal_values(splits[0], (CHILDREN, D), 1.0, 6.0, ((0, 32),)),
        "board_mask": plant((jax.random.randint(splits[1], (CHILDREN,), 0, 3) < 1).astype(jnp.int32), jax.random.fold_in(splits[1], 1), 0, 1),
        "importance": jnp.clip(0.1 + 0.9 * jax.random.uniform(splits[2], (CHILDREN,), jnp.float32) ** levels(splits[2], (CHILDREN,), ((0, 32),), -0.2, 0.2), 0.1, 1.0),
        "parent_slot": plant(jax.random.randint(splits[3], (CHILDREN,), 0, P_DEV), jax.random.fold_in(splits[3], 1), 0, P_DEV - 1).astype(jnp.int32),
        "send_counts": draw_send_counts(jax.random.fold_in(splits[12], 71), 0),
        "parent_feats": normal_values(splits[5], (PARENTS, D), 1.0, 6.0, ((0, 32),)),
        "proj_weight": normal_values(splits[6], (D, D), D ** -0.5, 0.1875),
        "q_weight": normal_values(splits[7], (D, D), D ** -0.5, 0.1875),
        "q_bias": normal_values(splits[8], (D,), 0.3, 1.5, (), jnp.float32),
        "w_weight": normal_values(splits[9], (2 * D, D), (2 * D) ** -0.5, 0.125),
        "w_bias": normal_values(splits[10], (D,), 0.3, 1.5, (), jnp.float32),
        "emb_cotangent": normal_values(splits[11], (PARENTS, D), 1.0, 6.0, ((0, 32),), jnp.float32),
    }


HIGHEST = lax.Precision.HIGHEST

@jax.custom_vjp
def low(v):
    return lax.optimization_barrier(v.astype(jnp.bfloat16)).astype(jnp.float32)

@jax.custom_vjp
def low_back(v):
    return v

def low_keep(v):
    return (low(v), None)

def low_pass(kept, grad):
    return (grad,)

def back_keep(v):
    return (v, None)

def back_low(kept, grad):
    return (low(grad),)
low.defvjp(low_keep, low_pass)
low_back.defvjp(back_keep, back_low)

def child_block(block_feats, block_board, block_weight, proj_weight, q_weight, q_bias):
    projected = low_back(jnp.dot(block_feats, proj_weight, precision=HIGHEST))
    merged = low(jnp.where(block_board[:, None] == 1, projected, block_feats))
    pre_act = low_back(jnp.dot(merged, q_weight, precision=HIGHEST) + q_bias)
    activation = jax.nn.silu(pre_act)
    return low_back(low(block_weight[:, None] * activation))

def reference(child_feats, board_mask, importance, parent_slot, send_counts, parent_feats, proj_weight, q_weight, q_bias, w_weight, w_bias, emb_cotangent):
    positions = jnp.arange(CAP, dtype=jnp.int32)
    live_slots = (positions[None, None, :] < send_counts[:, :, None]).astype(jnp.float32).reshape(SHARDS, CH_DEV)
    weight_live = importance.reshape(SHARDS, CH_DEV) * live_slots
    destination = (jnp.arange(CH_DEV, dtype=jnp.int32) // CAP).astype(jnp.int32)
    global_ids = (destination[None, :] * P_DEV + parent_slot.reshape(SHARDS, CH_DEV)).astype(jnp.int32)
    weight_sum = jax.ops.segment_sum(weight_live.reshape(-1), global_ids.reshape(-1), num_segments=PARENTS)
    divisor = jnp.maximum(weight_sum, 1.0)
    child_all = child_feats.astype(jnp.float32).reshape(SHARDS, CH_DEV, D)
    board_all = board_mask.reshape(SHARDS, CH_DEV)

    def forward(child_in, parent_in, proj_in, q_in, qb_in, w_in, wb_in):
        checked_block = jax.checkpoint(child_block)

        def advance(running, scan_items):
            block_feats, block_board, block_weight, block_ids = scan_items
            message = checked_block(block_feats, block_board, block_weight, proj_in, q_in, qb_in)
            return (running + jax.ops.segment_sum(message, block_ids, num_segments=PARENTS), None)
        running, _ = lax.scan(advance, jnp.zeros((PARENTS, D), jnp.float32), (child_in, board_all, weight_live, global_ids))
        neighbor_mean = low(running / divisor[:, None])
        joined = jnp.concatenate([parent_in, neighbor_mean], axis=1)
        pre_norm = low_back(jnp.dot(joined, w_in, precision=HIGHEST) + wb_in)
        act_out = jax.nn.silu(pre_norm)
        return act_out * lax.rsqrt(lax.optimization_barrier(jnp.sum(act_out * act_out, axis=1, keepdims=True)) + 1e-06)
    embedding, pullback = jax.vjp(forward, child_all, parent_feats.astype(jnp.float32), proj_weight.astype(jnp.float32), q_weight.astype(jnp.float32), q_bias, w_weight.astype(jnp.float32), w_bias)
    gradients = pullback(emb_cotangent)
    grad_child = gradients[0].reshape(CHILDREN, D).astype(jnp.bfloat16)
    return (embedding, grad_child, gradients[1], gradients[2], gradients[3], gradients[4], gradients[5], gradients[6])
```

```python
import functools

import jax
import jax.numpy as jnp
from jax import lax
from jax.experimental import pallas as pl
from jax.experimental.pallas import tpu as pltpu
from jax.sharding import PartitionSpec as P

MESH = pl.DeviceIdType.MESH
CORE = -1


def times_transpose(left, right):
    return lax.dot_general(
        left, right, (((1,), (1,)), ((), ())), preferred_element_type=jnp.float32
    )


def contract_rows(left, right):
    return lax.dot_general(
        left, right, (((0,), (0,)), ((), ())), preferred_element_type=jnp.float32
    )


def silu_slope(value):
    sigma = jax.nn.sigmoid(value)
    return sigma * (1.0 + value * (1.0 - sigma))


def send_rows(payload, hop_count, par_count, slot_cap, feature_width):
    parcel = payload.reshape(hop_count * par_count, slot_cap, feature_width)
    arrived = lax.all_to_all(parcel, ("hop", "par"), split_axis=0, concat_axis=0, tiled=True)
    return arrived.reshape(payload.shape)


def halving_orders(hop_count, rows):
    bits = hop_count.bit_length() - 1
    if bits == 4:
        x, y, z0, z1 = range(4)
        base = [[x, y, z0, z1], [y, x, z0, z1], [z0, x, y, z1], [x, y, z0, z1]]
        base += [[y, x, z0, z1], [z0, y, x, z1], [x, y, z0, z1], [y, x, z0, z1]]
    else:
        base = [[(first + k) % bits for k in range(bits)] for first in range(0, bits, 2)]
    groups = 1
    while groups * 2 <= len(base) and rows // (groups * 2) // (hop_count * 2) >= 16:
        groups *= 2
    return [[CORE] + order for order in base[:groups]]


def own_bit(hop, core, bit):
    return core if bit == CORE else lax.rem(hop // (1 << bit), 2)


def partner(hop, core, bit):
    if bit == CORE:
        return (hop, 1 - core)
    return (hop + (1 - 2 * own_bit(hop, core, bit)) * (1 << bit), core)


def sum_kernel(orders, part_ref, sum_ref, held, inbox, send_sem, recv_sem, out_sem, in_sem):
    hop, core = lax.axis_index("hop"), lax.axis_index("par")
    groups, levels = len(orders), len(orders[0])
    rows = part_ref.shape[0] // groups
    barrier = pltpu.get_barrier_semaphore()
    for bit in range(CORE, levels - 1):
        pl.semaphore_signal(barrier, inc=1, device_id=partner(hop, core, bit), device_id_type=MESH)
    held[...] = part_ref[...]
    pl.semaphore_wait(barrier, levels)

    start = [jnp.int32(group * rows) for group in range(groups)]
    kept = [[None] * levels for _ in range(groups)]
    places = [rows - (rows >> level) for level in range(levels)]
    down, up = {}, {}

    def halve(group, level):
        bit = orders[group][level]
        half = rows >> (level + 1)
        mine = own_bit(hop, core, bit)
        away = pl.multiple_of(start[group] + (1 - mine) * half, half)
        copy = pltpu.make_async_remote_copy(
            src_ref=held.at[pl.ds(away, half)],
            dst_ref=inbox.at[group, pl.ds(places[level], half)],
            send_sem=send_sem.at[group, level],
            recv_sem=recv_sem.at[group, level],
            device_id=partner(hop, core, bit),
            device_id_type=MESH,
        )
        copy.start()
        down[group, level] = copy
        start[group] = start[group] + mine * half
        kept[group][level] = start[group]

    def double(group, level):
        half = rows >> (level + 1)
        part = pl.ds(pl.multiple_of(kept[group][level], half), half)
        copy = pltpu.make_async_remote_copy(
            src_ref=sum_ref.at[part],
            dst_ref=sum_ref.at[part],
            send_sem=out_sem.at[group, level],
            recv_sem=in_sem.at[group, level],
            device_id=partner(hop, core, orders[group][level]),
            device_id_type=MESH,
        )
        copy.start()
        up[group, level] = copy

    for group in range(groups):
        halve(group, 0)
    for level in range(levels):
        for group in range(groups):
            half = rows >> (level + 1)
            part = pl.ds(pl.multiple_of(kept[group][level], half), half)
            down[group, level].wait_recv()
            total = held[part] + inbox[group, pl.ds(places[level], half)]
            if level < levels - 1:
                held[part] = total
                halve(group, level + 1)
            else:
                sum_ref[part] = total
                double(group, level)
    for level in range(levels - 1, -1, -1):
        for group in range(groups):
            up[group, level].wait_recv()
            if level > 0:
                double(group, level - 1)
    for level in range(levels):
        for group in range(groups):
            down[group, level].wait_send()
            up[group, level].wait_send()


def sum_over_devices(part, hop_count):
    rows, columns = part.shape
    orders = halving_orders(hop_count, rows)
    groups, levels = len(orders), len(orders[0])
    semaphores = pltpu.SemaphoreType.DMA((groups, levels))
    return pl.pallas_call(
        functools.partial(sum_kernel, orders),
        name="weight_gradient_sum",
        out_shape=jax.ShapeDtypeStruct((rows, columns), part.dtype),
        in_specs=[pl.BlockSpec(memory_space=pltpu.VMEM)],
        out_specs=pl.BlockSpec(memory_space=pltpu.VMEM),
        scratch_shapes=[
            pltpu.VMEM((rows, columns), part.dtype),
            pltpu.VMEM((groups, rows // groups, columns), part.dtype),
            semaphores,
            semaphores,
            semaphores,
            semaphores,
        ],
        compiler_params=pltpu.CompilerParams(
            collective_id=0, has_side_effects=True, vmem_limit_bytes=48 << 20
        ),
    )(part)


def body(
    child_feats,
    board_mask,
    importance,
    parent_slot,
    send_counts,
    parent_feats,
    proj_weight,
    q_weight,
    q_bias,
    w_weight,
    w_bias,
    emb_cotangent,
):
    slot_rows, feature_width = child_feats.shape
    hop_count = lax.axis_size("hop")
    par_count = lax.axis_size("par")
    shard_count = hop_count * par_count
    slot_cap = slot_rows // shard_count
    live_slots = (
        (jnp.arange(slot_cap)[None, :] < send_counts[0][:, None])
        .astype(jnp.float32)
        .reshape(slot_rows)
    )
    weight_live = importance * live_slots
    is_board = board_mask[:, None] == 1
    projected = jnp.dot(child_feats, proj_weight, preferred_element_type=jnp.float32)
    merged = jnp.where(is_board, projected, child_feats.astype(jnp.float32)).astype(jnp.bfloat16)
    pre_act = jnp.dot(merged, q_weight, preferred_element_type=jnp.float32) + q_bias
    message = (weight_live[:, None] * jax.nn.silu(pre_act)).astype(jnp.bfloat16)
    edge_info = jnp.stack([weight_live, parent_slot.astype(jnp.float32)]).reshape(
        2, shard_count, slot_cap
    )
    got_info = lax.all_to_all(edge_info, ("hop", "par"), split_axis=1, concat_axis=1, tiled=True)
    got_weight = got_info[0].reshape(slot_rows)
    got_slot = got_info[1].reshape(slot_rows).astype(jnp.int32)
    arrived = send_rows(message, hop_count, par_count, slot_cap, feature_width)
    parent_rows = parent_feats.shape[0]
    owner_table = got_slot[None, :] == jnp.arange(parent_rows, dtype=jnp.int32)[:, None]
    gathered = jnp.dot(
        owner_table.astype(jnp.bfloat16), arrived, preferred_element_type=jnp.float32
    )
    weight_sum = jnp.sum(jnp.where(owner_table, got_weight[None, :], 0.0), axis=1)
    divisor = jnp.maximum(weight_sum, 1.0)
    neighbor_mean = (gathered / divisor[:, None]).astype(jnp.bfloat16)
    joined = jnp.concatenate([parent_feats, neighbor_mean], axis=1)
    pre_norm = jnp.dot(joined, w_weight, preferred_element_type=jnp.float32) + w_bias
    act_out = jax.nn.silu(pre_norm)
    inv_norm = lax.rsqrt(jnp.sum(act_out * act_out, axis=1, keepdims=True) + 1e-06)
    embedding = act_out * inv_norm
    grad_emb = inv_norm * (
        emb_cotangent - embedding * jnp.sum(emb_cotangent * embedding, axis=1, keepdims=True)
    )
    grad_pre = (grad_emb * silu_slope(pre_norm)).astype(jnp.bfloat16)
    grad_w = contract_rows(joined, grad_pre)
    grad_wbias = jnp.sum(grad_pre.astype(jnp.float32), axis=0)
    grad_cat = times_transpose(grad_pre, w_weight)
    grad_parent = grad_cat[:, :feature_width]
    grad_mean = grad_cat[:, feature_width:] / divisor[:, None]
    return_rows = jnp.take(grad_mean, got_slot, axis=0).astype(jnp.bfloat16)
    grad_message = send_rows(return_rows, hop_count, par_count, slot_cap, feature_width)
    grad_act = weight_live[:, None] * grad_message.astype(jnp.float32)
    grad_preact = (grad_act * silu_slope(pre_act)).astype(jnp.bfloat16)
    grad_q = contract_rows(merged, grad_preact)
    grad_qbias = jnp.sum(grad_preact.astype(jnp.float32), axis=0)
    grad_merged = times_transpose(grad_preact, q_weight)
    grad_board = jnp.where(is_board, grad_merged, 0.0).astype(jnp.bfloat16)
    grad_proj = contract_rows(child_feats, grad_board)
    grad_child = (
        jnp.where(is_board, 0.0, grad_merged) + times_transpose(grad_board, proj_weight)
    ).astype(jnp.bfloat16)
    part = jnp.concatenate([grad_w, grad_q, grad_proj]).astype(jnp.bfloat16)
    summed = sum_over_devices(part, hop_count)
    summed = summed.astype(jnp.float32)
    grad_qbias, grad_wbias = lax.psum((grad_qbias, grad_wbias), ("hop", "par"))
    w_rows, q_rows = grad_w.shape[0], grad_q.shape[0]
    return (
        embedding,
        grad_child,
        grad_parent,
        summed[w_rows + q_rows :],
        summed[w_rows : w_rows + q_rows],
        grad_qbias,
        summed[:w_rows],
        grad_wbias,
    )


def solution(mesh):
    rows = P(("hop", "par"), None)
    flat = P(("hop", "par"))
    return jax.shard_map(
        body,
        mesh=mesh,
        in_specs=(rows, flat, flat, flat, rows, rows, P(), P(), P(), P(), P(), rows),
        out_specs=(rows, rows, rows, P(), P(), P(), P(), P()),
        check_vma=False,
    )
```

```python
import functools

import jax
import jax.numpy as jnp
from jax import lax
from jax.experimental import pallas as pl
from jax.experimental.pallas import tpu as pltpu
from jax.sharding import PartitionSpec as P

MESH = pl.DeviceIdType.MESH
CORE = -1


def times_transpose(left, right):
    return lax.dot_general(
        left, right, (((1,), (1,)), ((), ())), preferred_element_type=jnp.float32
    )


def contract_rows(left, right):
    return lax.dot_general(
        left, right, (((0,), (0,)), ((), ())), preferred_element_type=jnp.float32
    )


def silu_slope(value):
    sigma = jax.nn.sigmoid(value)
    return sigma * (1.0 + value * (1.0 - sigma))


def send_rows(payload, hop_count, par_count, slot_cap, feature_width):
    parcel = payload.reshape(hop_count * par_count, slot_cap, feature_width)
    arrived = lax.all_to_all(parcel, ("hop", "par"), split_axis=0, concat_axis=0, tiled=True)
    return arrived.reshape(payload.shape)


def halving_orders(hop_count, rows):
    bits = hop_count.bit_length() - 1
    if bits == 4:
        x, y, z0, z1 = range(4)
        base = [[x, y, z0, z1], [y, x, z0, z1], [z0, x, y, z1], [x, y, z0, z1]]
        base += [[y, x, z0, z1], [z0, y, x, z1], [x, y, z0, z1], [y, x, z0, z1]]
    else:
        base = [[(first + k) % bits for k in range(bits)] for first in range(0, bits, 2)]
    groups = 1
    while groups * 2 <= len(base) and rows // (groups * 2) // (hop_count * 2) >= 16:
        groups *= 2
    return [[CORE] + order for order in base[:groups]]


def own_bit(hop, core, bit):
    return core if bit == CORE else lax.rem(hop // (1 << bit), 2)


def partner(hop, core, bit):
    if bit == CORE:
        return (hop, 1 - core)
    return (hop + (1 - 2 * own_bit(hop, core, bit)) * (1 << bit), core)


def sum_kernel(orders, part_ref, sum_ref, held, inbox, send_sem, recv_sem, out_sem, in_sem):
    hop, core = lax.axis_index("hop"), lax.axis_index("par")
    groups, levels = len(orders), len(orders[0])
    rows = part_ref.shape[0] // groups
    barrier = pltpu.get_barrier_semaphore()
    for bit in range(CORE, levels - 1):
        pl.semaphore_signal(barrier, inc=1, device_id=partner(hop, core, bit), device_id_type=MESH)
    held[...] = part_ref[...]
    pl.semaphore_wait(barrier, levels)

    start = [jnp.int32(group * rows) for group in range(groups)]
    kept = [[None] * levels for _ in range(groups)]
    places = [rows - (rows >> level) for level in range(levels)]
    down, up = {}, {}

    def halve(group, level):
        bit = orders[group][level]
        half = rows >> (level + 1)
        mine = own_bit(hop, core, bit)
        away = pl.multiple_of(start[group] + (1 - mine) * half, half)
        copy = pltpu.make_async_remote_copy(
            src_ref=held.at[pl.ds(away, half)],
            dst_ref=inbox.at[group, pl.ds(places[level], half)],
            send_sem=send_sem.at[group, level],
            recv_sem=recv_sem.at[group, level],
            device_id=partner(hop, core, bit),
            device_id_type=MESH,
        )
        copy.start()
        down[group, level] = copy
        start[group] = start[group] + mine * half
        kept[group][level] = start[group]

    def double(group, level):
        half = rows >> (level + 1)
        part = pl.ds(pl.multiple_of(kept[group][level], half), half)
        copy = pltpu.make_async_remote_copy(
            src_ref=sum_ref.at[part],
            dst_ref=sum_ref.at[part],
            send_sem=out_sem.at[group, level],
            recv_sem=in_sem.at[group, level],
            device_id=partner(hop, core, orders[group][level]),
            device_id_type=MESH,
        )
        copy.start()
        up[group, level] = copy

    for group in range(groups):
        halve(group, 0)
    for level in range(levels):
        for group in range(groups):
            half = rows >> (level + 1)
            part = pl.ds(pl.multiple_of(kept[group][level], half), half)
            down[group, level].wait_recv()
            total = held[part] + inbox[group, pl.ds(places[level], half)]
            if level < levels - 1:
                held[part] = total
                halve(group, level + 1)
            else:
                sum_ref[part] = total
                double(group, level)
    for level in range(levels - 1, -1, -1):
        for group in range(groups):
            up[group, level].wait_recv()
            if level > 0:
                double(group, level - 1)
    for level in range(levels):
        for group in range(groups):
            down[group, level].wait_send()
            up[group, level].wait_send()


def sum_over_devices(part, hop_count):
    rows, columns = part.shape
    orders = halving_orders(hop_count, rows)
    groups, levels = len(orders), len(orders[0])
    semaphores = pltpu.SemaphoreType.DMA((groups, levels))
    return pl.pallas_call(
        functools.partial(sum_kernel, orders),
        name="weight_gradient_sum",
        out_shape=jax.ShapeDtypeStruct((rows, columns), part.dtype),
        in_specs=[pl.BlockSpec(memory_space=pltpu.VMEM)],
        out_specs=pl.BlockSpec(memory_space=pltpu.VMEM),
        scratch_shapes=[
            pltpu.VMEM((rows, columns), part.dtype),
            pltpu.VMEM((groups, rows // groups, columns), part.dtype),
            semaphores,
            semaphores,
            semaphores,
            semaphores,
        ],
        compiler_params=pltpu.CompilerParams(
            collective_id=0, has_side_effects=True, vmem_limit_bytes=48 << 20
        ),
    )(part)


def plain_body(
    child_feats,
    board_mask,
    importance,
    parent_slot,
    send_counts,
    parent_feats,
    proj_weight,
    q_weight,
    q_bias,
    w_weight,
    w_bias,
    emb_cotangent,
):
    slot_rows, feature_width = child_feats.shape
    hop_count = lax.axis_size("hop")
    par_count = lax.axis_size("par")
    shard_count = hop_count * par_count
    slot_cap = slot_rows // shard_count
    live_slots = (
        (jnp.arange(slot_cap)[None, :] < send_counts[0][:, None])
        .astype(jnp.float32)
        .reshape(slot_rows)
    )
    weight_live = importance * live_slots
    is_board = board_mask[:, None] == 1
    projected = jnp.dot(child_feats, proj_weight, preferred_element_type=jnp.float32)
    merged = jnp.where(is_board, projected, child_feats.astype(jnp.float32)).astype(jnp.bfloat16)
    pre_act = jnp.dot(merged, q_weight, preferred_element_type=jnp.float32) + q_bias
    message = (weight_live[:, None] * jax.nn.silu(pre_act)).astype(jnp.bfloat16)
    edge_info = jnp.stack([weight_live, parent_slot.astype(jnp.float32)]).reshape(
        2, shard_count, slot_cap
    )
    got_info = lax.all_to_all(edge_info, ("hop", "par"), split_axis=1, concat_axis=1, tiled=True)
    got_weight = got_info[0].reshape(slot_rows)
    got_slot = got_info[1].reshape(slot_rows).astype(jnp.int32)
    arrived = send_rows(message, hop_count, par_count, slot_cap, feature_width)
    parent_rows = parent_feats.shape[0]
    owner_table = got_slot[None, :] == jnp.arange(parent_rows, dtype=jnp.int32)[:, None]
    gathered = jnp.dot(
        owner_table.astype(jnp.bfloat16), arrived, preferred_element_type=jnp.float32
    )
    weight_sum = jnp.sum(jnp.where(owner_table, got_weight[None, :], 0.0), axis=1)
    divisor = jnp.maximum(weight_sum, 1.0)
    neighbor_mean = (gathered / divisor[:, None]).astype(jnp.bfloat16)
    joined = jnp.concatenate([parent_feats, neighbor_mean], axis=1)
    pre_norm = jnp.dot(joined, w_weight, preferred_element_type=jnp.float32) + w_bias
    act_out = jax.nn.silu(pre_norm)
    inv_norm = lax.rsqrt(jnp.sum(act_out * act_out, axis=1, keepdims=True) + 1e-06)
    embedding = act_out * inv_norm
    grad_emb = inv_norm * (
        emb_cotangent - embedding * jnp.sum(emb_cotangent * embedding, axis=1, keepdims=True)
    )
    grad_pre = (grad_emb * silu_slope(pre_norm)).astype(jnp.bfloat16)
    grad_w = contract_rows(joined, grad_pre)
    grad_wbias = jnp.sum(grad_pre.astype(jnp.float32), axis=0)
    grad_cat = times_transpose(grad_pre, w_weight)
    grad_parent = grad_cat[:, :feature_width]
    grad_mean = grad_cat[:, feature_width:] / divisor[:, None]
    return_rows = jnp.take(grad_mean, got_slot, axis=0).astype(jnp.bfloat16)
    grad_message = send_rows(return_rows, hop_count, par_count, slot_cap, feature_width)
    grad_act = weight_live[:, None] * grad_message.astype(jnp.float32)
    grad_preact = (grad_act * silu_slope(pre_act)).astype(jnp.bfloat16)
    grad_q = contract_rows(merged, grad_preact)
    grad_qbias = jnp.sum(grad_preact.astype(jnp.float32), axis=0)
    grad_merged = times_transpose(grad_preact, q_weight)
    grad_board = jnp.where(is_board, grad_merged, 0.0).astype(jnp.bfloat16)
    grad_proj = contract_rows(child_feats, grad_board)
    grad_child = (
        jnp.where(is_board, 0.0, grad_merged) + times_transpose(grad_board, proj_weight)
    ).astype(jnp.bfloat16)
    part = jnp.concatenate([grad_w, grad_q, grad_proj]).astype(jnp.bfloat16)
    summed = sum_over_devices(part, hop_count)
    summed = summed.astype(jnp.float32)
    grad_qbias, grad_wbias = lax.psum((grad_qbias, grad_wbias), ("hop", "par"))
    w_rows, q_rows = grad_w.shape[0], grad_q.shape[0]
    return (
        embedding,
        grad_child,
        grad_parent,
        summed[w_rows + q_rows :],
        summed[w_rows : w_rows + q_rows],
        grad_qbias,
        summed[:w_rows],
        grad_wbias,
    )


TILE = 256
BLOCK = 16


def columns(index, width=TILE):
    return pl.ds(pl.multiple_of(index * width, width), width)


def mm(left, right):
    return jnp.dot(left, right, preferred_element_type=jnp.float32)


def sigmoid(value):
    return 0.5 * jnp.tanh(0.5 * value) + 0.5


def spread(column, width):
    return jnp.concatenate([column] * (width // column.shape[1]), axis=1)


class Sums:
    def __init__(self, hop, core, groups, held, inbox, total, sems):
        self.hop, self.core, self.groups = hop, core, groups
        self.held, self.inbox, self.total = held, inbox, total
        self.send, self.recv, self.out, self.into, self.own = sems
        self.start = [jnp.int32(first) for first, _, _ in groups]
        self.kept, self.down, self.up, self.local = {}, {}, {}, {}
        self.levels = len(groups[0][2])

    def halve(self, group, level):
        first, rows, order = self.groups[group]
        bit, half = order[level], rows >> (level + 1)
        mine = own_bit(self.hop, self.core, bit)
        away = pl.multiple_of(self.start[group] + (1 - mine) * half, half)
        place = first + rows - (rows >> level)
        copy = pltpu.make_async_remote_copy(
            src_ref=self.held.at[pl.ds(away, half)],
            dst_ref=self.inbox.at[pl.ds(place, half)],
            send_sem=self.send.at[group, level],
            recv_sem=self.recv.at[group, level],
            device_id=partner(self.hop, self.core, bit),
            device_id_type=MESH,
        )
        copy.start()
        self.down[group, level] = copy
        self.start[group] = self.start[group] + mine * half
        self.kept[group, level] = self.start[group]

    def fold(self, group, level):
        first, rows, _ = self.groups[group]
        half = rows >> (level + 1)
        part = pl.ds(pl.multiple_of(self.kept[group, level], half), half)
        place = first + rows - (rows >> level)
        self.down[group, level].wait_recv()
        self.held[part] = self.held[part] + self.inbox[pl.ds(place, half)]
        if level < self.levels - 1:
            self.halve(group, level + 1)
        else:
            copy = pltpu.make_async_copy(self.held.at[part], self.total.at[part], self.own.at[group])
            copy.start()
            self.local[group] = copy
            self.double(group, level, self.held)

    def double(self, group, level, source):
        _, rows, order = self.groups[group]
        half = rows >> (level + 1)
        part = pl.ds(pl.multiple_of(self.kept[group, level], half), half)
        copy = pltpu.make_async_remote_copy(
            src_ref=source.at[part],
            dst_ref=self.total.at[part],
            send_sem=self.out.at[group, level],
            recv_sem=self.into.at[group, level],
            device_id=partner(self.hop, self.core, order[level]),
            device_id_type=MESH,
        )
        copy.start()
        self.up[group, level] = copy

    def gather(self, group, level):
        if level == self.levels - 1:
            self.local[group].wait()
        self.up[group, level].wait_recv()
        if level > 0:
            self.double(group, level - 1, self.total)

    def finish(self):
        for group in range(len(self.groups)):
            for level in range(self.levels):
                self.down[group, level].wait_send()
                self.up[group, level].wait_send()


def layer_kernel(
    groups,
    child_in,
    importance,
    board,
    slot,
    counts,
    parent_in,
    proj_in,
    q_in,
    q_bias,
    w_in,
    w_bias,
    cot_in,
    emb_out,
    child_out,
    parent_out,
    total,
    bias_out,
    child,
    proj,
    q,
    w,
    parent,
    cot,
    merged,
    scaled_slope,
    message,
    arrived,
    moved,
    pre,
    table,
    table_rows,
    grad_pre,
    grad_moved,
    back_out,
    back_in,
    child_t,
    merged_t,
    parent_t,
    held,
    inbox,
    emb,
    weight_col,
    board_col,
    shrink,
    slot_shrink,
    got_weight,
    got_slot,
    info_out,
    info_in,
    bias_held,
    bias_in,
    load_sem,
    store_sem,
    info_sem,
    msg_sem,
    back_sem,
    bias_sem,
    sum_send,
    sum_recv,
    sum_out,
    sum_in,
    sum_own,
):
    hop, core = lax.axis_index("hop"), lax.axis_index("par")
    me = hop * 2 + core
    slots, width = child.shape
    parents = parent.shape[0]
    devices = counts.shape[1]
    cap = slots // devices
    half = slots // 2
    levels = len(groups[0][2])
    tiles = width // TILE
    upper = own_bit(hop, core, levels - 2)
    sides = (1 - upper, upper)
    f32, bf16 = jnp.float32, jnp.bfloat16

    def target(rel):
        to_hop = hop
        for bit in range(levels - 1):
            if (rel >> (bit + 1)) & 1:
                to_hop = to_hop + (1 - 2 * own_bit(hop, core, bit)) * (1 << bit)
        to_core = 1 - core if rel & 1 else core
        return to_hop, to_core

    def rows_of(device):
        return pl.ds(pl.multiple_of(device * cap, cap), cap)

    def side_rows(side):
        return pl.ds(pl.multiple_of(side * half, half), half)

    loads = []
    for index, (source, place) in enumerate(
        ((child_in, child), (proj_in, proj), (q_in, q), (parent_in, parent), (w_in, w), (cot_in, cot))
    ):
        copy = pltpu.make_async_copy(source, place, load_sem.at[index])
        copy.start()
        loads.append(copy)

    barrier = pltpu.get_barrier_semaphore()
    for rel in range(1, devices):
        pl.semaphore_signal(barrier, inc=1, device_id=target(rel), device_id_type=MESH)

    lane = lax.broadcasted_iota(jnp.int32, (128, 128), 1)
    down = lax.broadcasted_iota(jnp.int32, (128, 128), 0)
    eye = lane == down
    place = lax.rem(down, cap)

    def column(row):
        return jnp.sum(jnp.where(eye, jnp.broadcast_to(row, (128, 128)), 0.0), axis=1, keepdims=True)

    count_row = counts[...].astype(f32)
    for part in range(slots // 128):
        owner = lax.broadcasted_iota(jnp.int32, (128, devices), 0) // cap + part * (128 // cap)
        is_owner = owner == lax.broadcasted_iota(jnp.int32, (128, devices), 1)
        live = jnp.sum(
            jnp.where(is_owner, jnp.broadcast_to(count_row, (128, devices)), 0.0), axis=1, keepdims=True
        )
        weight = jnp.broadcast_to(column(importance[part : part + 1, :]), (128, 128))
        weight = jnp.where(place.astype(f32) < live, weight, 0.0)
        slot_at = jnp.broadcast_to(column(slot[part : part + 1, :].astype(f32)), (128, 128))
        at = slice(part * 128, (part + 1) * 128)
        weight_col[at, :] = weight
        board_col[at, :] = jnp.broadcast_to(column(board[part : part + 1, :].astype(f32)), (128, 128))
        info = jnp.where(lane == place, weight, 0.0) + jnp.where(lane == place + cap, slot_at, 0.0)
        for owner_at in range(128 // cap):
            info_out[part * (128 // cap) + owner_at] = jnp.sum(
                info[owner_at * cap : (owner_at + 1) * cap, :], axis=0, keepdims=True
            )

    pl.semaphore_wait(barrier, devices - 1)

    for rel in range(devices - 1, 0, -1):
        to_hop, to_core = target(rel)
        pltpu.make_async_remote_copy(
            src_ref=info_out.at[to_hop * 2 + to_core],
            dst_ref=info_in.at[me],
            send_sem=info_sem.at[0],
            recv_sem=info_sem.at[1],
            device_id=(to_hop, to_core),
            device_id_type=MESH,
        ).start()
    pltpu.make_async_copy(info_out.at[me], info_in.at[me], info_sem.at[1]).start()

    def send_side(source, place_ref, sem, side_index):
        first = devices // 2 if side_index == 0 else 0
        rels = sorted(range(first, first + devices // 2), key=lambda rel: (rel & 1, -rel))
        for rel in rels:
            if rel == 0:
                pltpu.make_async_copy(
                    source.at[rows_of(me)], place_ref.at[rows_of(me)], sem.at[1, side_index]
                ).start()
                continue
            to_hop, to_core = target(rel)
            pltpu.make_async_remote_copy(
                src_ref=source.at[rows_of(to_hop * 2 + to_core)],
                dst_ref=place_ref.at[rows_of(me)],
                send_sem=sem.at[0, side_index],
                recv_sem=sem.at[1, side_index],
                device_id=(to_hop, to_core),
                device_id_type=MESH,
            ).start()

    def wait_side(place_ref, sem, side_index):
        rows = side_rows(sides[side_index])
        pltpu.make_async_copy(place_ref.at[rows], place_ref.at[rows], sem.at[1, side_index]).wait()

    def wait_sent(source, sem):
        for side_index, rows in ((0, half), (1, half - cap)):
            part = source.at[pl.ds(0, rows)]
            pltpu.make_async_copy(part, part, sem.at[0, side_index]).wait()

    loads[0].wait()
    loads[1].wait()
    for side_index, side in enumerate(sides):
        rows = side_rows(side)
        boards = spread(board_col[rows, :], TILE) == 1.0

        @pl.loop(0, tiles)
        def _(tile):
            projected = mm(child[rows, :], proj[:, columns(tile)])
            raw = child[rows, columns(tile)]
            merged[rows, columns(tile)] = jnp.where(boards, projected, raw.astype(f32)).astype(bf16)

        if side_index == 0:
            loads[2].wait()
        weights = spread(weight_col[rows, :], TILE)

        @pl.loop(0, tiles)
        def _(tile):
            value = mm(merged[rows, :], q[:, columns(tile)]) + q_bias[:, columns(tile)]
            gate = sigmoid(value)
            act = value * gate
            message[rows, columns(tile)] = (weights * act).astype(bf16)
            scaled_slope[rows, columns(tile)] = weights * (gate + act * (1.0 - gate))

        send_side(message, arrived, msg_sem, side_index)

    loads[3].wait()
    loads[4].wait()

    @pl.loop(0, tiles)
    def _(tile):
        @pl.loop(0, parents // 512)
        def _(block):
            pre[columns(block, 512), columns(tile)] = (
                mm(parent[columns(block, 512), :], w[pl.ds(0, width), columns(tile)])
                + w_bias[:, columns(tile)]
            )

    info_all = pltpu.make_async_copy(info_in, info_in, info_sem.at[1])
    info_all.wait()
    lane16 = lax.broadcasted_iota(jnp.int32, (cap, 128), 1)
    down16 = lax.broadcasted_iota(jnp.int32, (cap, 128), 0)
    for device in range(devices):
        got = jnp.broadcast_to(info_in[device], (cap, 128))
        at = slice(device * cap, (device + 1) * cap)
        got_weight[at, :] = jnp.broadcast_to(
            jnp.sum(jnp.where(lane16 == down16, got, 0.0), axis=1, keepdims=True), (cap, 128)
        )
        got_slot[at, :] = jnp.broadcast_to(
            jnp.sum(jnp.where(lane16 == down16 + cap, got, 0.0), axis=1, keepdims=True), (cap, 128)
        )

    for part in range(parents // 128):
        want = (lax.broadcasted_iota(jnp.int32, (128, 128), 1) + part * 128).astype(f32)
        weight_sum = jnp.zeros((1, 128), f32)
        for block in range(slots // 128):
            at = slice(block * 128, (block + 1) * 128)
            hit = got_slot[at, :] == want
            table_rows[at, part * 128 : (part + 1) * 128] = jnp.where(hit, 1.0, 0.0).astype(bf16)
            weight_sum = weight_sum + jnp.sum(jnp.where(hit, got_weight[at, :], 0.0), axis=0, keepdims=True)
        inverse = 1.0 / jnp.maximum(weight_sum, 1.0)
        shrink[part * 128 : (part + 1) * 128, :] = jnp.broadcast_to(column(inverse), (128, 128))
        for block in range(slots // 128):
            at = slice(block * 128, (block + 1) * 128)
            hit = got_slot[at, :] == want
            term = jnp.where(hit, jnp.broadcast_to(inverse, (128, 128)), 0.0)
            if part == 0:
                slot_shrink[at, :] = term
            else:
                slot_shrink[at, :] = slot_shrink[at, :] + term
    for block in range(slots // 128):
        at = slice(block * 128, (block + 1) * 128)
        slot_shrink[at, :] = jnp.broadcast_to(
            jnp.sum(slot_shrink[at, :], axis=1, keepdims=True), (128, 128)
        )

    def transpose_into(place_ref, source, blocks):
        for block in range(blocks):

            @pl.loop(0, source.shape[1] // TILE)
            def _(tile):
                part = source[block * TILE : (block + 1) * TILE, columns(tile)]
                place_ref[block, columns(tile), :] = part.T

    transpose_into(table, table_rows, slots // TILE)
    transpose_into(child_t, child, slots // TILE)
    transpose_into(merged_t, merged, slots // TILE)
    transpose_into(parent_t, parent, parents // TILE)

    def add_messages(side_index):
        side = sides[side_index]
        rows = side_rows(side)

        @pl.loop(0, tiles)
        def _(tile):
            moved[rows, columns(tile)] = mm(arrived[rows, :], w[pl.ds(width, width), columns(tile)]).astype(bf16)

        @pl.loop(0, tiles)
        def _(tile):
            @pl.loop(0, parents // 512)
            def _(block):
                at = columns(block, 512)
                pre[at, columns(tile)] = pre[at, columns(tile)] + spread(shrink[at, :], TILE) * mm(
                    table[side, at, :], moved[rows, columns(tile)]
                )

    wait_side(arrived, msg_sem, 1)
    add_messages(1)
    loads[5].wait()
    wait_side(arrived, msg_sem, 0)
    add_messages(0)

    @pl.loop(0, parents // BLOCK)
    def _(block):
        at = columns(block, BLOCK)
        value = pre[at, :]
        turn = cot[at, :]
        gate = sigmoid(value)
        act = value * gate
        inv = lax.rsqrt(jnp.sum(act * act, axis=1, keepdims=True) + 1e-06)
        share = jnp.sum(turn * act, axis=1, keepdims=True) * (inv * inv * inv)
        emb[at, :] = (act * inv).astype(bf16)
        grad_pre[at, :] = ((turn * inv - act * share) * (gate + act * (1.0 - gate))).astype(bf16)

    stores = [pltpu.make_async_copy(emb, emb_out, store_sem.at[0])]
    stores[0].start()

    for side_index, side in enumerate(sides):
        rows = side_rows(side)
        shrinks = spread(slot_shrink[rows, :], TILE)

        @pl.loop(0, tiles)
        def _(tile):
            grad_moved[rows, columns(tile)] = (
                shrinks * mm(table_rows[rows, :], grad_pre[:, columns(tile)])
            ).astype(bf16)

        @pl.loop(0, tiles)
        def _(tile):
            turned = w[pl.ds(pl.multiple_of(width + tile * TILE, TILE), TILE), :]
            back_out[rows, columns(tile)] = times_transpose(grad_moved[rows, :], turned).astype(bf16)

        send_side(back_out, back_in, back_sem, side_index)

    sums = Sums(hop, core, groups, held, inbox, total, (sum_send, sum_recv, sum_out, sum_in, sum_own))
    w_groups = [g for g, (first, _, _) in enumerate(groups) if first < 2 * width]
    q_groups = [g for g, (first, _, _) in enumerate(groups) if 2 * width <= first < 3 * width]
    p_groups = [g for g, (first, _, _) in enumerate(groups) if first >= 3 * width]

    @pl.loop(0, tiles)
    def _(tile):
        @pl.loop(0, tiles)
        def _(block):
            total_part = jnp.zeros((TILE, TILE), f32)
            for part in range(parents // TILE):
                total_part = total_part + mm(
                    parent_t[part, columns(block), :],
                    grad_pre[part * TILE : (part + 1) * TILE, columns(tile)],
                )
            held[columns(block), columns(tile)] = total_part.astype(bf16)

    for group in w_groups[: len(w_groups) // 2]:
        sums.halve(group, 0)
    transpose_into(table, arrived, slots // TILE)

    @pl.loop(0, tiles)
    def _(tile):
        @pl.loop(0, tiles)
        def _(block):
            total_part = jnp.zeros((TILE, TILE), f32)
            for part in range(slots // TILE):
                total_part = total_part + mm(
                    table[part, columns(block), :],
                    grad_moved[part * TILE : (part + 1) * TILE, columns(tile)],
                )
            at = pl.ds(pl.multiple_of(width + block * TILE, TILE), TILE)
            held[at, columns(tile)] = total_part.astype(bf16)

    for group in w_groups[len(w_groups) // 2 :]:
        sums.halve(group, 0)
    bias_held[0] = jnp.zeros(bias_held.shape[1:], f32)
    bias_held[0, 0:1, :] = mm(jnp.ones((16, parents), bf16), grad_pre[...])[0:1, :]

    for group in w_groups:
        sums.fold(group, 0)

    @pl.loop(0, tiles)
    def _(tile):
        @pl.loop(0, parents // 512)
        def _(block):
            parent[columns(block, 512), columns(tile)] = times_transpose(
                grad_pre[columns(block, 512), :], w[columns(tile), :]
            ).astype(bf16)

    stores.append(pltpu.make_async_copy(parent, parent_out, store_sem.at[1]))
    stores[1].start()
    wait_sent(message, msg_sem)

    def child_front(side_index):
        rows = side_rows(sides[side_index])

        @pl.loop(0, tiles)
        def _(tile):
            grad_moved[rows, columns(tile)] = (
                scaled_slope[rows, columns(tile)] * back_in[rows, columns(tile)].astype(f32)
            ).astype(bf16)

    def weight_sums(side_index, turned, grads, partial, base):
        side = sides[side_index]
        rows = side_rows(side)

        @pl.loop(0, tiles)
        def _(tile):
            @pl.loop(0, width // 512)
            def _(block):
                at = columns(block, 512)
                value = mm(turned[side, at, :], grads[rows, columns(tile)])
                if side_index == 1:
                    partial[at, columns(tile)] = value
                else:
                    place_at = pl.ds(pl.multiple_of(base + block * 512, 512), 512)
                    held[place_at, columns(tile)] = (value + partial[at, columns(tile)]).astype(bf16)

    def child_middle(side_index):
        rows = side_rows(sides[side_index])
        boards = spread(board_col[rows, :], TILE) == 1.0

        @pl.loop(0, tiles)
        def _(tile):
            value = times_transpose(grad_moved[rows, :], q[columns(tile), :])
            moved[rows, columns(tile)] = jnp.where(boards, value, 0.0).astype(bf16)
            scaled_slope[rows, columns(tile)] = jnp.where(boards, 0.0, value)

    def child_end(side_index):
        rows = side_rows(sides[side_index])

        @pl.loop(0, tiles)
        def _(tile):
            value = times_transpose(moved[rows, :], proj[columns(tile), :])
            message[rows, columns(tile)] = (scaled_slope[rows, columns(tile)] + value).astype(bf16)

    wait_side(back_in, back_sem, 1)
    child_front(1)
    weight_sums(1, merged_t, grad_moved, pre, 2 * width)
    child_middle(1)
    weight_sums(1, child_t, moved, cot, 3 * width)
    child_end(1)

    for group in w_groups:
        sums.fold(group, 1)

    wait_side(back_in, back_sem, 0)
    child_front(0)
    weight_sums(0, merged_t, grad_moved, pre, 2 * width)
    for group in q_groups:
        sums.halve(group, 0)
    child_middle(0)
    weight_sums(0, child_t, moved, cot, 3 * width)
    for group in p_groups:
        sums.halve(group, 0)

    bias_held[0, 1:2, :] = mm(jnp.ones((16, slots), bf16), grad_moved[...])[0:1, :]
    bias_copies = []

    def send_bias(level):
        copy = pltpu.make_async_remote_copy(
            src_ref=bias_held.at[level],
            dst_ref=bias_in.at[level],
            send_sem=bias_sem.at[0, level],
            recv_sem=bias_sem.at[1, level],
            device_id=partner(hop, core, groups[0][2][level]),
            device_id_type=MESH,
        )
        copy.start()
        bias_copies.append(copy)

    def fold_bias(level):
        bias_copies[level].wait_recv()
        both = bias_held[level] + bias_in[level]
        if level < levels - 1:
            bias_held[level + 1] = both
            send_bias(level + 1)
        else:
            bias_out[...] = both

    send_bias(0)
    child_end(0)
    stores.append(pltpu.make_async_copy(message, child_out, store_sem.at[2]))
    stores[2].start()

    late = q_groups + p_groups
    plan = [("late", 0), ("w", 2), ("late", 1), ("w", 3), ("late", 2), ("w", 4), ("late", 3), ("w_up", 4)]
    plan += [("late", 4), ("w_up", 3), ("late_up", 4), ("w_up", 2), ("late_up", 3), ("w_up", 1)]
    plan += [("late_up", 2), ("w_up", 0), ("late_up", 1), ("late_up", 0)]
    for what, level in plan:
        for group in w_groups if what[0] == "w" else late:
            (sums.gather if what.endswith("up") else sums.fold)(group, level)
        if what == "late":
            fold_bias(level)

    sums.finish()
    for copy in bias_copies:
        copy.wait_send()
    wait_sent(back_out, back_sem)
    sent = info_out.at[pl.ds(0, devices - 1)]
    pltpu.make_async_copy(sent, sent, info_sem.at[0]).wait()
    for copy in stores:
        copy.wait()


def sum_groups(width):
    x, y, z0, z1 = range(4)
    orders = [[x, y, z0, z1], [y, x, z0, z1], [x, z0, y, z1], [y, z0, x, z1]]
    orders += [[x, y, z0, z1], [y, x, z0, z1], [z0, x, y, z1], [z0, y, x, z1]]
    rows = 4 * width // len(orders)
    return [(index * rows, rows, [CORE] + order) for index, order in enumerate(orders)]


def fused_body(
    child_feats,
    board_mask,
    importance,
    parent_slot,
    send_counts,
    parent_feats,
    proj_weight,
    q_weight,
    q_bias,
    w_weight,
    w_bias,
    emb_cotangent,
):
    slots, width = child_feats.shape
    parents = parent_feats.shape[0]
    devices = send_counts.shape[1]
    groups = sum_groups(width)
    levels = len(groups[0][2])
    f32, bf16 = jnp.float32, jnp.bfloat16
    half = slots // 2
    vmem = pl.BlockSpec(memory_space=pltpu.VMEM)
    hbm = pl.BlockSpec(memory_space=pl.ANY)
    dma = pltpu.SemaphoreType.DMA
    shape = jax.ShapeDtypeStruct
    emb, grad_child, grad_parent, total, biases = pl.pallas_call(
        functools.partial(layer_kernel, groups),
        name="layer",
        out_shape=(
            shape((parents, width), bf16),
            shape((slots, width), bf16),
            shape((parents, width), bf16),
            shape((4 * width, width), bf16),
            shape((8, width), f32),
        ),
        in_specs=[hbm, vmem, vmem, vmem, vmem, hbm, hbm, hbm, vmem, hbm, vmem, hbm],
        out_specs=(hbm, hbm, hbm, hbm, vmem),
        scratch_shapes=[
            pltpu.VMEM((slots, width), bf16),
            pltpu.VMEM((width, width), bf16),
            pltpu.VMEM((width, width), bf16),
            pltpu.VMEM((2 * width, width), bf16),
            pltpu.VMEM((parents, width), bf16),
            pltpu.VMEM((parents, width), f32),
            pltpu.VMEM((slots, width), bf16),
            pltpu.VMEM((slots, width), f32),
            pltpu.VMEM((slots, width), bf16),
            pltpu.VMEM((slots, width), bf16),
            pltpu.VMEM((slots, width), bf16),
            pltpu.VMEM((parents, width), f32),
            pltpu.VMEM((2, parents, half), bf16),
            pltpu.VMEM((slots, parents), bf16),
            pltpu.VMEM((parents, width), bf16),
            pltpu.VMEM((slots, width), bf16),
            pltpu.VMEM((slots, width), bf16),
            pltpu.VMEM((slots, width), bf16),
            pltpu.VMEM((2, width, half), bf16),
            pltpu.VMEM((2, width, half), bf16),
            pltpu.VMEM((parents // TILE, width, TILE), bf16),
            pltpu.VMEM((4 * width, width), bf16),
            pltpu.VMEM((4 * width, width), bf16),
            pltpu.VMEM((parents, width), bf16),
            pltpu.VMEM((slots, 128), f32),
            pltpu.VMEM((slots, 128), f32),
            pltpu.VMEM((parents, 128), f32),
            pltpu.VMEM((slots, 128), f32),
            pltpu.VMEM((slots, 128), f32),
            pltpu.VMEM((slots, 128), f32),
            pltpu.VMEM((devices, 1, 128), f32),
            pltpu.VMEM((devices, 1, 128), f32),
            pltpu.VMEM((levels, 8, width), f32),
            pltpu.VMEM((levels, 8, width), f32),
            dma((6,)),
            dma((3,)),
            dma((2,)),
            dma((2, 2)),
            dma((2, 2)),
            dma((2, levels)),
        ]
        + [dma((len(groups), levels))] * 4
        + [dma((len(groups),))],
        compiler_params=pltpu.CompilerParams(
            collective_id=1, has_side_effects=True, vmem_limit_bytes=62 << 20
        ),
        cost_estimate=pl.CostEstimate(
            flops=36 * slots * width * width, bytes_accessed=40 << 20, transcendentals=3 * parents * width
        ),
    )(
        child_feats,
        importance.reshape(-1, 128),
        board_mask.reshape(-1, 128),
        parent_slot.reshape(-1, 128),
        send_counts,
        parent_feats,
        proj_weight,
        q_weight,
        q_bias.reshape(1, -1),
        w_weight,
        w_bias.reshape(1, -1),
        emb_cotangent,
    )
    return (
        emb.astype(f32),
        grad_child,
        grad_parent.astype(f32),
        total[3 * width :].astype(f32),
        total[2 * width : 3 * width].astype(f32),
        biases[1],
        total[: 2 * width].astype(f32),
        biases[0],
    )


def solution(mesh):
    rows = P(("hop", "par"), None)
    flat = P(("hop", "par"))
    fused = mesh.shape["hop"] == 16 and mesh.shape["par"] == 2
    return jax.shard_map(
        fused_body if fused else plain_body,
        mesh=mesh,
        in_specs=(rows, flat, flat, flat, rows, rows, P(), P(), P(), P(), P(), rows),
        out_specs=(rows, rows, rows, P(), P(), P(), P(), P()),
        check_vma=False,
    )
```

```python
import functools

import jax
import jax.numpy as jnp
from jax import lax
from jax.experimental import pallas as pl
from jax.experimental.pallas import tpu as pltpu
from jax.sharding import PartitionSpec as P

MESH = pl.DeviceIdType.MESH
CORE = -1


def times_transpose(left, right):
    return lax.dot_general(
        left, right, (((1,), (1,)), ((), ())), preferred_element_type=jnp.float32
    )


def contract_rows(left, right):
    return lax.dot_general(
        left, right, (((0,), (0,)), ((), ())), preferred_element_type=jnp.float32
    )


def silu_slope(value):
    sigma = jax.nn.sigmoid(value)
    return sigma * (1.0 + value * (1.0 - sigma))


def send_rows(payload, hop_count, par_count, slot_cap, feature_width):
    parcel = payload.reshape(hop_count * par_count, slot_cap, feature_width)
    arrived = lax.all_to_all(parcel, ("hop", "par"), split_axis=0, concat_axis=0, tiled=True)
    return arrived.reshape(payload.shape)


def halving_orders(hop_count, rows):
    bits = hop_count.bit_length() - 1
    if bits == 4:
        x, y, z0, z1 = range(4)
        base = [[x, y, z0, z1], [y, x, z0, z1], [z0, x, y, z1], [x, y, z0, z1]]
        base += [[y, x, z0, z1], [z0, y, x, z1], [x, y, z0, z1], [y, x, z0, z1]]
    else:
        base = [[(first + k) % bits for k in range(bits)] for first in range(0, bits, 2)]
    groups = 1
    while groups * 2 <= len(base) and rows // (groups * 2) // (hop_count * 2) >= 16:
        groups *= 2
    return [[CORE] + order for order in base[:groups]]


def own_bit(hop, core, bit):
    return core if bit == CORE else lax.rem(hop // (1 << bit), 2)


def partner(hop, core, bit):
    if bit == CORE:
        return (hop, 1 - core)
    return (hop + (1 - 2 * own_bit(hop, core, bit)) * (1 << bit), core)


def sum_kernel(orders, part_ref, sum_ref, held, inbox, send_sem, recv_sem, out_sem, in_sem):
    hop, core = lax.axis_index("hop"), lax.axis_index("par")
    groups, levels = len(orders), len(orders[0])
    rows = part_ref.shape[0] // groups
    barrier = pltpu.get_barrier_semaphore()
    for bit in range(CORE, levels - 1):
        pl.semaphore_signal(barrier, inc=1, device_id=partner(hop, core, bit), device_id_type=MESH)
    held[...] = part_ref[...]
    pl.semaphore_wait(barrier, levels)

    start = [jnp.int32(group * rows) for group in range(groups)]
    kept = [[None] * levels for _ in range(groups)]
    places = [rows - (rows >> level) for level in range(levels)]
    down, up = {}, {}

    def halve(group, level):
        bit = orders[group][level]
        half = rows >> (level + 1)
        mine = own_bit(hop, core, bit)
        away = pl.multiple_of(start[group] + (1 - mine) * half, half)
        copy = pltpu.make_async_remote_copy(
            src_ref=held.at[pl.ds(away, half)],
            dst_ref=inbox.at[group, pl.ds(places[level], half)],
            send_sem=send_sem.at[group, level],
            recv_sem=recv_sem.at[group, level],
            device_id=partner(hop, core, bit),
            device_id_type=MESH,
        )
        copy.start()
        down[group, level] = copy
        start[group] = start[group] + mine * half
        kept[group][level] = start[group]

    def double(group, level):
        half = rows >> (level + 1)
        part = pl.ds(pl.multiple_of(kept[group][level], half), half)
        copy = pltpu.make_async_remote_copy(
            src_ref=sum_ref.at[part],
            dst_ref=sum_ref.at[part],
            send_sem=out_sem.at[group, level],
            recv_sem=in_sem.at[group, level],
            device_id=partner(hop, core, orders[group][level]),
            device_id_type=MESH,
        )
        copy.start()
        up[group, level] = copy

    for group in range(groups):
        halve(group, 0)
    for level in range(levels):
        for group in range(groups):
            half = rows >> (level + 1)
            part = pl.ds(pl.multiple_of(kept[group][level], half), half)
            down[group, level].wait_recv()
            total = held[part] + inbox[group, pl.ds(places[level], half)]
            if level < levels - 1:
                held[part] = total
                halve(group, level + 1)
            else:
                sum_ref[part] = total
                double(group, level)
    for level in range(levels - 1, -1, -1):
        for group in range(groups):
            up[group, level].wait_recv()
            if level > 0:
                double(group, level - 1)
    for level in range(levels):
        for group in range(groups):
            down[group, level].wait_send()
            up[group, level].wait_send()


def sum_over_devices(part, hop_count):
    rows, columns = part.shape
    orders = halving_orders(hop_count, rows)
    groups, levels = len(orders), len(orders[0])
    semaphores = pltpu.SemaphoreType.DMA((groups, levels))
    return pl.pallas_call(
        functools.partial(sum_kernel, orders),
        name="weight_gradient_sum",
        out_shape=jax.ShapeDtypeStruct((rows, columns), part.dtype),
        in_specs=[pl.BlockSpec(memory_space=pltpu.VMEM)],
        out_specs=pl.BlockSpec(memory_space=pltpu.VMEM),
        scratch_shapes=[
            pltpu.VMEM((rows, columns), part.dtype),
            pltpu.VMEM((groups, rows // groups, columns), part.dtype),
            semaphores,
            semaphores,
            semaphores,
            semaphores,
        ],
        compiler_params=pltpu.CompilerParams(
            collective_id=0, has_side_effects=True, vmem_limit_bytes=48 << 20
        ),
    )(part)


def plain_body(
    child_feats,
    board_mask,
    importance,
    parent_slot,
    send_counts,
    parent_feats,
    proj_weight,
    q_weight,
    q_bias,
    w_weight,
    w_bias,
    emb_cotangent,
):
    slot_rows, feature_width = child_feats.shape
    hop_count = lax.axis_size("hop")
    par_count = lax.axis_size("par")
    shard_count = hop_count * par_count
    slot_cap = slot_rows // shard_count
    live_slots = (
        (jnp.arange(slot_cap)[None, :] < send_counts[0][:, None])
        .astype(jnp.float32)
        .reshape(slot_rows)
    )
    weight_live = importance * live_slots
    is_board = board_mask[:, None] == 1
    projected = jnp.dot(child_feats, proj_weight, preferred_element_type=jnp.float32)
    merged = jnp.where(is_board, projected, child_feats.astype(jnp.float32)).astype(jnp.bfloat16)
    pre_act = jnp.dot(merged, q_weight, preferred_element_type=jnp.float32) + q_bias
    message = (weight_live[:, None] * jax.nn.silu(pre_act)).astype(jnp.bfloat16)
    edge_info = jnp.stack([weight_live, parent_slot.astype(jnp.float32)]).reshape(
        2, shard_count, slot_cap
    )
    got_info = lax.all_to_all(edge_info, ("hop", "par"), split_axis=1, concat_axis=1, tiled=True)
    got_weight = got_info[0].reshape(slot_rows)
    got_slot = got_info[1].reshape(slot_rows).astype(jnp.int32)
    arrived = send_rows(message, hop_count, par_count, slot_cap, feature_width)
    parent_rows = parent_feats.shape[0]
    owner_table = got_slot[None, :] == jnp.arange(parent_rows, dtype=jnp.int32)[:, None]
    gathered = jnp.dot(
        owner_table.astype(jnp.bfloat16), arrived, preferred_element_type=jnp.float32
    )
    weight_sum = jnp.sum(jnp.where(owner_table, got_weight[None, :], 0.0), axis=1)
    divisor = jnp.maximum(weight_sum, 1.0)
    neighbor_mean = (gathered / divisor[:, None]).astype(jnp.bfloat16)
    joined = jnp.concatenate([parent_feats, neighbor_mean], axis=1)
    pre_norm = jnp.dot(joined, w_weight, preferred_element_type=jnp.float32) + w_bias
    act_out = jax.nn.silu(pre_norm)
    inv_norm = lax.rsqrt(jnp.sum(act_out * act_out, axis=1, keepdims=True) + 1e-06)
    embedding = act_out * inv_norm
    grad_emb = inv_norm * (
        emb_cotangent - embedding * jnp.sum(emb_cotangent * embedding, axis=1, keepdims=True)
    )
    grad_pre = (grad_emb * silu_slope(pre_norm)).astype(jnp.bfloat16)
    grad_w = contract_rows(joined, grad_pre)
    grad_wbias = jnp.sum(grad_pre.astype(jnp.float32), axis=0)
    grad_cat = times_transpose(grad_pre, w_weight)
    grad_parent = grad_cat[:, :feature_width]
    grad_mean = grad_cat[:, feature_width:] / divisor[:, None]
    return_rows = jnp.take(grad_mean, got_slot, axis=0).astype(jnp.bfloat16)
    grad_message = send_rows(return_rows, hop_count, par_count, slot_cap, feature_width)
    grad_act = weight_live[:, None] * grad_message.astype(jnp.float32)
    grad_preact = (grad_act * silu_slope(pre_act)).astype(jnp.bfloat16)
    grad_q = contract_rows(merged, grad_preact)
    grad_qbias = jnp.sum(grad_preact.astype(jnp.float32), axis=0)
    grad_merged = times_transpose(grad_preact, q_weight)
    grad_board = jnp.where(is_board, grad_merged, 0.0).astype(jnp.bfloat16)
    grad_proj = contract_rows(child_feats, grad_board)
    grad_child = (
        jnp.where(is_board, 0.0, grad_merged) + times_transpose(grad_board, proj_weight)
    ).astype(jnp.bfloat16)
    part = jnp.concatenate([grad_w, grad_q, grad_proj]).astype(jnp.bfloat16)
    summed = sum_over_devices(part, hop_count)
    summed = summed.astype(jnp.float32)
    grad_qbias, grad_wbias = lax.psum((grad_qbias, grad_wbias), ("hop", "par"))
    w_rows, q_rows = grad_w.shape[0], grad_q.shape[0]
    return (
        embedding,
        grad_child,
        grad_parent,
        summed[w_rows + q_rows :],
        summed[w_rows : w_rows + q_rows],
        grad_qbias,
        summed[:w_rows],
        grad_wbias,
    )


TILE = 512
BLOCK = 128


def columns(index, width=TILE):
    return pl.ds(pl.multiple_of(index * width, width), width)


def mm(left, right):
    return jnp.dot(left, right, preferred_element_type=jnp.float32)


def sigmoid(value):
    return 0.5 * jnp.tanh(0.5 * value) + 0.5


def spread(column, width):
    return jnp.concatenate([column] * (width // column.shape[1]), axis=1)


class Sums:
    def __init__(self, hop, core, groups, held, inbox, total, sems):
        self.hop, self.core, self.groups = hop, core, groups
        self.held, self.inbox, self.total = held, inbox, total
        self.send, self.recv, self.out, self.into, self.own = sems
        self.levels = len(groups[0][2])
        low, high = own_bit(hop, core, 2), own_bit(hop, core, 3)
        self.is_inner = low != high
        self.high = high
        place = 0
        self.plans = []
        for first, rows, order in groups:
            start, size, inner, steps = jnp.int32(first), rows, False, []
            for kind in order:
                if kind == "i":
                    step = (kind, start, start, size, place, inner)
                    inner = True
                else:
                    size //= 2
                    mine = high if kind == "m" else own_bit(hop, core, "cxypq".index(kind) - 1)
                    step = (kind, start + (1 - mine) * size, start + mine * size, size, place, inner)
                    start = start + mine * size
                    inner = inner or kind == "m"
                steps.append(step)
                place += size
            self.plans.append(steps)

    def other(self, kind):
        if kind == "m":
            return (self.hop + (1 - 2 * self.high) * 4, self.core)
        return partner(self.hop, self.core, "cxypq".index(kind.replace("i", "p")) - 1)

    def when(self, role, what):
        if role is None:
            what()
        else:
            pl.when(self.is_inner if role == "inner" else jnp.logical_not(self.is_inner))(what)

    def roles(self, group, level, upward):
        kind, _, _, _, _, inner = self.plans[group][level]
        if kind == "i":
            return ("inner", "outer") if upward else ("outer", "inner")
        role = "inner" if inner or kind == "m" else None
        return role, role

    def rows(self, start, size):
        return pl.ds(pl.multiple_of(start, size), size)

    def down(self, group, level):
        kind, away, _, size, place, _ = self.plans[group][level]
        return pltpu.make_async_remote_copy(
            src_ref=self.held.at[self.rows(away, size)],
            dst_ref=self.inbox.at[pl.ds(place, size)],
            send_sem=self.send.at[group, level],
            recv_sem=self.recv.at[group, level],
            device_id=self.other(kind),
            device_id_type=MESH,
        )

    def up(self, group, level):
        kind, _, kept, size, _, _ = self.plans[group][level]
        source = self.held if level == self.levels - 1 else self.total
        part = self.rows(kept, size)
        return pltpu.make_async_remote_copy(
            src_ref=source.at[part],
            dst_ref=self.total.at[part],
            send_sem=self.out.at[group, level],
            recv_sem=self.into.at[group, level],
            device_id=self.other(kind),
            device_id_type=MESH,
        )

    def own_copy(self, group):
        _, _, kept, size, _, _ = self.plans[group][-1]
        part = self.rows(kept, size)
        return pltpu.make_async_copy(self.held.at[part], self.total.at[part], self.own.at[group])

    def halve(self, group, level):
        self.when(self.roles(group, level, False)[0], lambda: self.down(group, level).start())

    def double(self, group, level):
        self.when(self.roles(group, level, True)[0], lambda: self.up(group, level).start())

    def fold(self, group, level):
        _, _, kept, size, place, _ = self.plans[group][level]

        def add():
            self.down(group, level).wait_recv()
            part = self.rows(kept, size)
            self.held[part] = self.held[part] + self.inbox[pl.ds(place, size)]
            if level == self.levels - 1:
                self.own_copy(group).start()
                self.up(group, level).start()

        self.when(self.roles(group, level, False)[1], add)
        if level < self.levels - 1:
            self.halve(group, level + 1)

    def gather(self, group, level):
        def take():
            if level == self.levels - 1:
                self.own_copy(group).wait()
            self.up(group, level).wait_recv()

        self.when(self.roles(group, level, True)[1], take)
        if level > 0:
            self.double(group, level - 1)

    def finish(self):
        for group in range(len(self.groups)):
            for level in range(self.levels):
                self.when(
                    self.roles(group, level, False)[0], lambda: self.down(group, level).wait_send()
                )
                self.when(self.roles(group, level, True)[0], lambda: self.up(group, level).wait_send())


def layer_kernel(
    groups,
    child_in,
    importance,
    board,
    slot,
    counts,
    parent_in,
    proj_in,
    q_in,
    q_bias,
    w_in,
    w_bias,
    cot_in,
    emb_out,
    child_out,
    parent_out,
    total,
    bias_out,
    child,
    proj,
    q,
    w,
    parent,
    cot,
    merged,
    scaled_slope,
    message,
    arrived,
    moved,
    pre,
    table_rows,
    grad_pre,
    grad_moved,
    back_out,
    back_in,
    held,
    inbox,
    emb,
    weight_col,
    board_col,
    shrink,
    slot_shrink,
    got_weight,
    got_slot,
    info_out,
    info_in,
    bias_held,
    bias_in,
    load_sem,
    store_sem,
    info_sem,
    msg_sem,
    back_sem,
    bias_sem,
    sum_send,
    sum_recv,
    sum_out,
    sum_in,
    sum_own,
):
    hop, core = lax.axis_index("hop"), lax.axis_index("par")
    me = hop * 2 + core
    slots, width = child.shape
    parents = parent.shape[0]
    devices = counts.shape[1]
    cap = slots // devices
    half = slots // 2
    levels = bias_held.shape[0]
    tiles = width // TILE
    upper = own_bit(hop, core, levels - 2)
    sides = (1 - upper, upper)
    f32, bf16 = jnp.float32, jnp.bfloat16

    def other_hop(flips):
        to_hop = hop
        for bit in range(levels - 1):
            if (flips >> bit) & 1:
                to_hop = to_hop + (1 - 2 * own_bit(hop, core, bit)) * (1 << bit)
        return to_hop

    def targets(first, last):
        away = [(other_hop(flips), to_core) for to_core in range(2) for flips in range(last - 1, max(first, 1) - 1, -1)]
        return away + ([(hop, 1 - core)] if first == 0 else [])

    def rows_of(device):
        return pl.ds(pl.multiple_of(device * cap, cap), cap)

    def side_rows(side):
        return pl.ds(pl.multiple_of(side * half, half), half)

    loads = []
    for index, (source, place) in enumerate(
        ((child_in, child), (proj_in, proj), (q_in, q), (parent_in, parent), (w_in, w), (cot_in, cot))
    ):
        loads.append(pltpu.make_async_copy(source, place, load_sem.at[index]))
    for copy in loads[:3]:
        copy.start()

    barrier = pltpu.get_barrier_semaphore()
    for to in targets(0, devices // 2):
        pl.semaphore_signal(barrier, inc=1, device_id=to, device_id_type=MESH)

    lane = lax.broadcasted_iota(jnp.int32, (128, 128), 1)
    down = lax.broadcasted_iota(jnp.int32, (128, 128), 0)
    eye = lane == down
    place = lax.rem(down, cap)

    def column(row):
        return jnp.sum(jnp.where(eye, jnp.broadcast_to(row, (128, 128)), 0.0), axis=1, keepdims=True)

    count_row = counts[...].astype(f32)
    for part in range(slots // 128):
        owner = lax.broadcasted_iota(jnp.int32, (128, devices), 0) // cap + part * (128 // cap)
        is_owner = owner == lax.broadcasted_iota(jnp.int32, (128, devices), 1)
        live = jnp.sum(
            jnp.where(is_owner, jnp.broadcast_to(count_row, (128, devices)), 0.0), axis=1, keepdims=True
        )
        weight = jnp.broadcast_to(column(importance[part : part + 1, :]), (128, 128))
        weight = jnp.where(place.astype(f32) < live, weight, 0.0)
        slot_at = jnp.broadcast_to(column(slot[part : part + 1, :].astype(f32)), (128, 128))
        at = slice(part * 128, (part + 1) * 128)
        weight_col[at, :] = weight
        board_col[at, :] = jnp.broadcast_to(column(board[part : part + 1, :].astype(f32)), (128, 128))
        info = jnp.where(lane == place, weight, 0.0) + jnp.where(lane == place + cap, slot_at, 0.0)
        for owner_at in range(128 // cap):
            info_out[part * (128 // cap) + owner_at] = jnp.sum(
                info[owner_at * cap : (owner_at + 1) * cap, :], axis=0, keepdims=True
            )

    def send_info():
        pl.semaphore_wait(barrier, devices - 1)

        for to_hop, to_core in targets(0, devices // 2):
            pltpu.make_async_remote_copy(
                src_ref=info_out.at[to_hop * 2 + to_core],
                dst_ref=info_in.at[me],
                send_sem=info_sem.at[0],
                recv_sem=info_sem.at[1],
                device_id=(to_hop, to_core),
                device_id_type=MESH,
            ).start()
        pltpu.make_async_copy(info_out.at[me], info_in.at[me], info_sem.at[1]).start()

    def send_side(source, place_ref, sem, side_index):
        quarter = devices // 4
        for to_hop, to_core in targets(quarter, 2 * quarter) if side_index == 0 else targets(0, quarter):
            pltpu.make_async_remote_copy(
                src_ref=source.at[rows_of(to_hop * 2 + to_core)],
                dst_ref=place_ref.at[rows_of(me)],
                send_sem=sem.at[0, side_index],
                recv_sem=sem.at[1, side_index],
                device_id=(to_hop, to_core),
                device_id_type=MESH,
            ).start()
        if side_index == 1:
            pltpu.make_async_copy(
                source.at[rows_of(me)], place_ref.at[rows_of(me)], sem.at[1, side_index]
            ).start()

    def wait_side(place_ref, sem, side_index):
        rows = side_rows(sides[side_index])
        pltpu.make_async_copy(place_ref.at[rows], place_ref.at[rows], sem.at[1, side_index]).wait()

    def wait_sent(source, sem):
        for side_index, rows in ((0, half), (1, half - cap)):
            part = source.at[pl.ds(0, rows)]
            pltpu.make_async_copy(part, part, sem.at[0, side_index]).wait()

    loads[0].wait()
    loads[1].wait()
    for side_index, side in enumerate(sides):
        rows = side_rows(side)
        boards = spread(board_col[rows, :], TILE) == 1.0

        @pl.loop(0, tiles)
        def _(tile):
            projected = mm(child[rows, :], proj[:, columns(tile)])
            raw = child[rows, columns(tile)]
            merged[rows, columns(tile)] = jnp.where(boards, projected, raw.astype(f32)).astype(bf16)

        if side_index == 0:
            loads[2].wait()
            for copy in loads[3:]:
                copy.start()
        weights = spread(weight_col[rows, :], TILE)

        @pl.loop(0, tiles)
        def _(tile):
            value = mm(merged[rows, :], q[:, columns(tile)]) + q_bias[:, columns(tile)]
            gate = sigmoid(value)
            act = value * gate
            message[rows, columns(tile)] = (weights * act).astype(bf16)
            scaled_slope[rows, columns(tile)] = weights * (gate + act * (1.0 - gate))

        if side_index == 0:
            send_info()
        send_side(message, arrived, msg_sem, side_index)

    loads[3].wait()
    loads[4].wait()

    @pl.loop(0, tiles)
    def _(tile):
        pre[:, columns(tile)] = mm(parent[...], w[pl.ds(0, width), columns(tile)]) + w_bias[:, columns(tile)]

    info_all = pltpu.make_async_copy(info_in, info_in, info_sem.at[1])
    info_all.wait()
    lane16 = lax.broadcasted_iota(jnp.int32, (cap, 128), 1)
    down16 = lax.broadcasted_iota(jnp.int32, (cap, 128), 0)
    for device in range(devices):
        got = jnp.broadcast_to(info_in[device], (cap, 128))
        at = slice(device * cap, (device + 1) * cap)
        got_weight[at, :] = jnp.broadcast_to(
            jnp.sum(jnp.where(lane16 == down16, got, 0.0), axis=1, keepdims=True), (cap, 128)
        )
        got_slot[at, :] = jnp.broadcast_to(
            jnp.sum(jnp.where(lane16 == down16 + cap, got, 0.0), axis=1, keepdims=True), (cap, 128)
        )

    for part in range(parents // 128):
        want = (lax.broadcasted_iota(jnp.int32, (128, 128), 1) + part * 128).astype(f32)
        weight_sum = jnp.zeros((1, 128), f32)
        for block in range(slots // 128):
            at = slice(block * 128, (block + 1) * 128)
            hit = got_slot[at, :] == want
            table_rows[at, part * 128 : (part + 1) * 128] = jnp.where(hit, 1.0, 0.0).astype(bf16)
            weight_sum = weight_sum + jnp.sum(jnp.where(hit, got_weight[at, :], 0.0), axis=0, keepdims=True)
        inverse = 1.0 / jnp.maximum(weight_sum, 1.0)
        shrink[part * 128 : (part + 1) * 128, :] = jnp.broadcast_to(column(inverse), (128, 128))
        for block in range(slots // 128):
            at = slice(block * 128, (block + 1) * 128)
            hit = got_slot[at, :] == want
            term = jnp.where(hit, jnp.broadcast_to(inverse, (128, 128)), 0.0)
            if part == 0:
                slot_shrink[at, :] = term
            else:
                slot_shrink[at, :] = slot_shrink[at, :] + term
    for block in range(slots // 128):
        at = slice(block * 128, (block + 1) * 128)
        slot_shrink[at, :] = jnp.broadcast_to(
            jnp.sum(slot_shrink[at, :], axis=1, keepdims=True), (128, 128)
        )

    def add_messages(side_index):
        rows = side_rows(sides[side_index])

        @pl.loop(0, tiles)
        def _(tile):
            moved[rows, columns(tile)] = mm(arrived[rows, :], w[pl.ds(width, width), columns(tile)]).astype(bf16)

        @pl.loop(0, tiles)
        def _(tile):
            pre[:, columns(tile)] = pre[:, columns(tile)] + spread(shrink[...], TILE) * contract_rows(
                table_rows[rows, :], moved[rows, columns(tile)]
            )

    wait_side(arrived, msg_sem, 1)
    add_messages(1)
    loads[5].wait()
    wait_side(arrived, msg_sem, 0)
    add_messages(0)

    @pl.loop(0, parents // BLOCK)
    def _(block):
        at = columns(block, BLOCK)
        value = pre[at, :]
        turn = cot[at, :]
        gate = sigmoid(value)
        act = value * gate
        inv = lax.rsqrt(jnp.sum(act * act, axis=1, keepdims=True) + 1e-06)
        share = jnp.sum(turn * act, axis=1, keepdims=True) * (inv * inv * inv)
        emb[at, :] = (act * inv).astype(bf16)
        grad_pre[at, :] = ((turn * inv - act * share) * (gate + act * (1.0 - gate))).astype(bf16)

    stores = [pltpu.make_async_copy(emb, emb_out, store_sem.at[0])]
    stores[0].start()

    for side_index, side in enumerate(sides):
        rows = side_rows(side)
        shrinks = spread(slot_shrink[rows, :], TILE)

        @pl.loop(0, tiles)
        def _(tile):
            grad_moved[rows, columns(tile)] = (
                shrinks * mm(table_rows[rows, :], grad_pre[:, columns(tile)])
            ).astype(bf16)

        @pl.loop(0, tiles)
        def _(tile):
            turned = w[pl.ds(pl.multiple_of(width + tile * TILE, TILE), TILE), :]
            back_out[rows, columns(tile)] = times_transpose(grad_moved[rows, :], turned).astype(bf16)

        send_side(back_out, back_in, back_sem, side_index)

    sums = Sums(hop, core, groups, held, inbox, total, (sum_send, sum_recv, sum_out, sum_in, sum_own))
    w_groups = [g for g, (first, _, _) in enumerate(groups) if first < 2 * width]
    q_groups = [g for g, (first, _, _) in enumerate(groups) if 2 * width <= first < 3 * width]
    p_groups = [g for g, (first, _, _) in enumerate(groups) if first >= 3 * width]

    @pl.loop(0, tiles)
    def _(tile):
        held[pl.ds(0, width), columns(tile)] = contract_rows(parent[...], grad_pre[:, columns(tile)]).astype(bf16)

    for group in w_groups[: len(w_groups) // 2]:
        sums.halve(group, 0)

    @pl.loop(0, tiles)
    def _(tile):
        held[pl.ds(width, width), columns(tile)] = contract_rows(
            arrived[...], grad_moved[:, columns(tile)]
        ).astype(bf16)

    for group in w_groups[len(w_groups) // 2 :]:
        sums.halve(group, 0)
    bias_held[0] = jnp.zeros(bias_held.shape[1:], f32)
    bias_held[0, 0:1, :] = mm(jnp.ones((16, parents), bf16), grad_pre[...])[0:1, :]

    def parent_gradient():
        @pl.loop(0, tiles)
        def _(tile):
            parent[:, columns(tile)] = times_transpose(grad_pre[...], w[columns(tile), :]).astype(bf16)

        stores.append(pltpu.make_async_copy(parent, parent_out, store_sem.at[1]))
        stores[1].start()
        wait_sent(message, msg_sem)

    def child_front(side_index):
        rows = side_rows(sides[side_index])

        @pl.loop(0, tiles)
        def _(tile):
            grad_moved[rows, columns(tile)] = (
                scaled_slope[rows, columns(tile)] * back_in[rows, columns(tile)].astype(f32)
            ).astype(bf16)

    def weight_sums(side_index, left, grads, partial, base):
        rows = side_rows(sides[side_index])

        @pl.loop(0, tiles)
        def _(tile):
            value = contract_rows(left[rows, :], grads[rows, columns(tile)])
            if side_index == 1:
                partial[:, columns(tile)] = value
            else:
                held[pl.ds(base, width), columns(tile)] = (value + partial[:, columns(tile)]).astype(bf16)

    def child_middle(side_index):
        rows = side_rows(sides[side_index])
        boards = spread(board_col[rows, :], TILE) == 1.0

        @pl.loop(0, tiles)
        def _(tile):
            value = times_transpose(grad_moved[rows, :], q[columns(tile), :])
            moved[rows, columns(tile)] = jnp.where(boards, value, 0.0).astype(bf16)
            scaled_slope[rows, columns(tile)] = jnp.where(boards, 0.0, value)

    def child_end(side_index):
        rows = side_rows(sides[side_index])

        @pl.loop(0, tiles)
        def _(tile):
            value = times_transpose(moved[rows, :], proj[columns(tile), :])
            message[rows, columns(tile)] = (scaled_slope[rows, columns(tile)] + value).astype(bf16)

    bias_copies = []

    def send_bias(level):
        copy = pltpu.make_async_remote_copy(
            src_ref=bias_held.at[level],
            dst_ref=bias_in.at[level],
            send_sem=bias_sem.at[0, level],
            recv_sem=bias_sem.at[1, level],
            device_id=partner(hop, core, level - 1),
            device_id_type=MESH,
        )
        copy.start()
        bias_copies.append(copy)

    def fold_bias(level):
        bias_copies[level].wait_recv()
        both = bias_held[level] + bias_in[level]
        if level < levels - 1:
            bias_held[level + 1] = both
            send_bias(level + 1)
        else:
            bias_out[...] = both

    def near_children():
        child_front(1)
        weight_sums(1, merged, grad_moved, pre, 2 * width)
        child_middle(1)
        weight_sums(1, child, moved, cot, 3 * width)
        child_end(1)

    def far_q():
        child_front(0)
        weight_sums(0, merged, grad_moved, pre, 2 * width)

    def far_p():
        child_middle(0)
        weight_sums(0, child, moved, cot, 3 * width)

    def far_end():
        bias_held[0, 1:2, :] = mm(jnp.ones((16, slots), bf16), grad_moved[...])[0:1, :]
        send_bias(0)
        child_end(0)
        stores.append(pltpu.make_async_copy(message, child_out, store_sem.at[2]))
        stores[2].start()

    main = [
        parent_gradient,
        lambda: wait_side(back_in, back_sem, 1),
        near_children,
        lambda: wait_side(back_in, back_sem, 0),
        far_q,
        lambda: [sums.halve(group, 0) for group in q_groups],
        far_p,
        lambda: [sums.halve(group, 0) for group in p_groups],
        far_end,
    ] + [functools.partial(fold_bias, level) for level in range(levels)]
    done = [0] * (len(groups) + 1)
    for turn in SCHEDULE:
        at = done[turn]
        done[turn] += 1
        if turn == 0:
            main[at]()
        elif at < sums.levels:
            sums.fold(turn - 1, at)
        else:
            sums.gather(turn - 1, 2 * sums.levels - 1 - at)

    sums.finish()
    for copy in bias_copies:
        copy.wait_send()
    wait_sent(back_out, back_sem)
    sent = info_out.at[pl.ds(0, devices - 1)]
    pltpu.make_async_copy(sent, sent, info_sem.at[0]).wait()
    for copy in stores:
        copy.wait()


ORDERS = ["cxyim", "cyxim", "cxyim", "cyxim", "cxyim", "cyxim", "cxyim", "cyxim"]
SCHEDULE = [
    3, 0, 4, 1, 3, 0, 0, 4, 1, 2, 0, 0, 0, 0, 0, 4, 1, 2, 1, 7, 3, 8, 4, 1, 2, 3, 4, 2, 7, 8, 3, 5, 6, 3, 7, 4,
    8, 2, 1, 7, 5, 6, 2, 3, 4, 1, 7, 8, 2, 6, 5, 4, 8, 7, 0, 6, 1, 7, 2, 0, 5, 8, 8, 6, 0, 5, 6, 5, 1, 0, 4, 7,
    6, 5, 0, 8, 5, 6, 3, 0, 7, 2, 5, 8, 2, 6, 5, 3, 1, 8, 6, 4, 7, 3,
]


def sum_groups(width):
    rows = 4 * width // len(ORDERS)
    return [(index * rows, rows, order) for index, order in enumerate(ORDERS)]


def inbox_rows(groups):
    total = 0
    for _, size, order in groups:
        for kind in order:
            size = size if kind == "i" else size // 2
            total += size
    return total


def widen_kernel(
    emb,
    child,
    parent,
    total,
    biases,
    emb_out,
    child_out,
    parent_out,
    proj_out,
    q_out,
    q_bias_out,
    w_out,
    w_bias_out,
    narrow,
    wide,
    through,
    read_sem,
    write_sem,
    child_sem,
):
    slots, rows, width = narrow.shape
    through_in = pltpu.make_async_copy(child, through, child_sem.at[0])
    through_out = pltpu.make_async_copy(through, child_out, child_sem.at[1])
    pieces = []
    base = 0
    for place in (w_out, q_out, proj_out):
        for first in range(0, place.shape[0], rows):
            pieces.append((total, base + first, place, first))
        base += place.shape[0]
    for source, place in ((parent, parent_out), (emb, emb_out)):
        for first in range(0, place.shape[0], rows):
            pieces.append((source, first, place, first))

    def read(index):
        source, first, _, _ = pieces[index]
        slot = index % slots
        return pltpu.make_async_copy(source.at[pl.ds(first, rows)], narrow.at[slot], read_sem.at[slot])

    def write(index):
        _, _, place, first = pieces[index]
        slot = index % slots
        return pltpu.make_async_copy(wide.at[slot], place.at[pl.ds(first, rows)], write_sem.at[slot])

    for index in range(slots):
        read(index).start()
    through_in.start()
    w_bias_out[...] = biases[0, :]
    q_bias_out[...] = biases[1, :]
    for index in range(len(pieces)):
        read(index).wait()
        if index >= slots:
            write(index - slots).wait()
        wide[index % slots] = narrow[index % slots].astype(jnp.float32)
        write(index).start()
        if index + slots < len(pieces):
            read(index + slots).start()
        if index == slots:
            through_in.wait()
            through_out.start()
    for index in range(len(pieces) - slots, len(pieces)):
        write(index).wait()
    through_out.wait()


def widen(emb, child, parent, total, biases):
    width = emb.shape[1]
    slots, rows = 4, 512
    shape, f32 = jax.ShapeDtypeStruct, jnp.float32
    hbm = pl.BlockSpec(memory_space=pl.ANY)
    vmem = pl.BlockSpec(memory_space=pltpu.VMEM)
    return pl.pallas_call(
        widen_kernel,
        name="widen",
        out_shape=(
            shape(emb.shape, f32),
            shape(child.shape, child.dtype),
            shape(parent.shape, f32),
            shape((width, width), f32),
            shape((width, width), f32),
            shape((width,), f32),
            shape((2 * width, width), f32),
            shape((width,), f32),
        ),
        in_specs=[hbm, hbm, hbm, hbm, vmem],
        out_specs=(hbm, hbm, hbm, hbm, hbm, vmem, hbm, vmem),
        scratch_shapes=[
            pltpu.VMEM((slots, rows, width), child.dtype),
            pltpu.VMEM((slots, rows, width), f32),
            pltpu.VMEM(child.shape, child.dtype),
            pltpu.SemaphoreType.DMA((slots,)),
            pltpu.SemaphoreType.DMA((slots,)),
            pltpu.SemaphoreType.DMA((2,)),
        ],
        compiler_params=pltpu.CompilerParams(vmem_limit_bytes=62 << 20),
    )(emb, child, parent, total, biases)


def fused_body(
    child_feats,
    board_mask,
    importance,
    parent_slot,
    send_counts,
    parent_feats,
    proj_weight,
    q_weight,
    q_bias,
    w_weight,
    w_bias,
    emb_cotangent,
):
    slots, width = child_feats.shape
    parents = parent_feats.shape[0]
    devices = send_counts.shape[1]
    groups = sum_groups(width)
    levels = devices.bit_length() - 1
    f32, bf16 = jnp.float32, jnp.bfloat16
    vmem = pl.BlockSpec(memory_space=pltpu.VMEM)
    hbm = pl.BlockSpec(memory_space=pl.ANY)
    dma = pltpu.SemaphoreType.DMA
    shape = jax.ShapeDtypeStruct
    emb, grad_child, grad_parent, total, biases = pl.pallas_call(
        functools.partial(layer_kernel, groups),
        name="layer",
        out_shape=(
            shape((parents, width), bf16),
            shape((slots, width), bf16),
            shape((parents, width), bf16),
            shape((4 * width, width), bf16),
            shape((8, width), f32),
        ),
        in_specs=[hbm, vmem, vmem, vmem, vmem, hbm, hbm, hbm, vmem, hbm, vmem, hbm],
        out_specs=(hbm, hbm, hbm, hbm, vmem),
        scratch_shapes=[
            pltpu.VMEM((slots, width), bf16),
            pltpu.VMEM((width, width), bf16),
            pltpu.VMEM((width, width), bf16),
            pltpu.VMEM((2 * width, width), bf16),
            pltpu.VMEM((parents, width), bf16),
            pltpu.VMEM((parents, width), f32),
            pltpu.VMEM((slots, width), bf16),
            pltpu.VMEM((slots, width), f32),
            pltpu.VMEM((slots, width), bf16),
            pltpu.VMEM((slots, width), bf16),
            pltpu.VMEM((slots, width), bf16),
            pltpu.VMEM((parents, width), f32),
            pltpu.VMEM((slots, parents), bf16),
            pltpu.VMEM((parents, width), bf16),
            pltpu.VMEM((slots, width), bf16),
            pltpu.VMEM((slots, width), bf16),
            pltpu.VMEM((slots, width), bf16),
            pltpu.VMEM((4 * width, width), bf16),
            pltpu.VMEM((inbox_rows(groups), width), bf16),
            pltpu.VMEM((parents, width), bf16),
            pltpu.VMEM((slots, 128), f32),
            pltpu.VMEM((slots, 128), f32),
            pltpu.VMEM((parents, 128), f32),
            pltpu.VMEM((slots, 128), f32),
            pltpu.VMEM((slots, 128), f32),
            pltpu.VMEM((slots, 128), f32),
            pltpu.VMEM((devices, 1, 128), f32),
            pltpu.VMEM((devices, 1, 128), f32),
            pltpu.VMEM((levels, 8, width), f32),
            pltpu.VMEM((levels, 8, width), f32),
            dma((6,)),
            dma((3,)),
            dma((2,)),
            dma((2, 2)),
            dma((2, 2)),
            dma((2, levels)),
        ]
        + [dma((len(groups), len(groups[0][2])))] * 4
        + [dma((len(groups),))],
        compiler_params=pltpu.CompilerParams(
            collective_id=1, has_side_effects=True, vmem_limit_bytes=62 << 20
        ),
        cost_estimate=pl.CostEstimate(
            flops=36 * slots * width * width, bytes_accessed=40 << 20, transcendentals=3 * parents * width
        ),
    )(
        child_feats,
        importance.reshape(-1, 128),
        board_mask.reshape(-1, 128),
        parent_slot.reshape(-1, 128),
        send_counts,
        parent_feats,
        proj_weight,
        q_weight,
        q_bias.reshape(1, -1),
        w_weight,
        w_bias.reshape(1, -1),
        emb_cotangent,
    )
    return widen(emb, grad_child, grad_parent, total, biases)


def solution(mesh):
    rows = P(("hop", "par"), None)
    flat = P(("hop", "par"))
    fused = mesh.shape["hop"] == 16 and mesh.shape["par"] == 2
    return jax.shard_map(
        fused_body if fused else plain_body,
        mesh=mesh,
        in_specs=(rows, flat, flat, flat, rows, rows, P(), P(), P(), P(), P(), rows),
        out_specs=(rows, rows, rows, P(), P(), P(), P(), P()),
        check_vma=False,
    )
```

```python
import functools

import jax
import jax.numpy as jnp
from jax import lax
from jax.experimental import pallas as pl
from jax.experimental.pallas import tpu as pltpu
from jax.sharding import PartitionSpec as P

MESH = pl.DeviceIdType.MESH
CORE = -1


def times_transpose(left, right):
    return lax.dot_general(
        left, right, (((1,), (1,)), ((), ())), preferred_element_type=jnp.float32
    )


def contract_rows(left, right):
    return lax.dot_general(
        left, right, (((0,), (0,)), ((), ())), preferred_element_type=jnp.float32
    )


def silu_slope(value):
    sigma = jax.nn.sigmoid(value)
    return sigma * (1.0 + value * (1.0 - sigma))


def send_rows(payload, hop_count, par_count, slot_cap, feature_width):
    parcel = payload.reshape(hop_count * par_count, slot_cap, feature_width)
    arrived = lax.all_to_all(parcel, ("hop", "par"), split_axis=0, concat_axis=0, tiled=True)
    return arrived.reshape(payload.shape)


def halving_orders(hop_count, rows):
    bits = hop_count.bit_length() - 1
    if bits == 4:
        x, y, z0, z1 = range(4)
        base = [[x, y, z0, z1], [y, x, z0, z1], [z0, x, y, z1], [x, y, z0, z1]]
        base += [[y, x, z0, z1], [z0, y, x, z1], [x, y, z0, z1], [y, x, z0, z1]]
    else:
        base = [[(first + k) % bits for k in range(bits)] for first in range(0, bits, 2)]
    groups = 1
    while groups * 2 <= len(base) and rows // (groups * 2) // (hop_count * 2) >= 16:
        groups *= 2
    return [[CORE] + order for order in base[:groups]]


def own_bit(hop, core, bit):
    return core if bit == CORE else lax.rem(hop // (1 << bit), 2)


def partner(hop, core, bit):
    if bit == CORE:
        return (hop, 1 - core)
    return (hop + (1 - 2 * own_bit(hop, core, bit)) * (1 << bit), core)


def sum_kernel(orders, part_ref, sum_ref, held, inbox, send_sem, recv_sem, out_sem, in_sem):
    hop, core = lax.axis_index("hop"), lax.axis_index("par")
    groups, levels = len(orders), len(orders[0])
    rows = part_ref.shape[0] // groups
    barrier = pltpu.get_barrier_semaphore()
    for bit in range(CORE, levels - 1):
        pl.semaphore_signal(barrier, inc=1, device_id=partner(hop, core, bit), device_id_type=MESH)
    held[...] = part_ref[...]
    pl.semaphore_wait(barrier, levels)

    start = [jnp.int32(group * rows) for group in range(groups)]
    kept = [[None] * levels for _ in range(groups)]
    places = [rows - (rows >> level) for level in range(levels)]
    down, up = {}, {}

    def halve(group, level):
        bit = orders[group][level]
        half = rows >> (level + 1)
        mine = own_bit(hop, core, bit)
        away = pl.multiple_of(start[group] + (1 - mine) * half, half)
        copy = pltpu.make_async_remote_copy(
            src_ref=held.at[pl.ds(away, half)],
            dst_ref=inbox.at[group, pl.ds(places[level], half)],
            send_sem=send_sem.at[group, level],
            recv_sem=recv_sem.at[group, level],
            device_id=partner(hop, core, bit),
            device_id_type=MESH,
        )
        copy.start()
        down[group, level] = copy
        start[group] = start[group] + mine * half
        kept[group][level] = start[group]

    def double(group, level):
        half = rows >> (level + 1)
        part = pl.ds(pl.multiple_of(kept[group][level], half), half)
        copy = pltpu.make_async_remote_copy(
            src_ref=sum_ref.at[part],
            dst_ref=sum_ref.at[part],
            send_sem=out_sem.at[group, level],
            recv_sem=in_sem.at[group, level],
            device_id=partner(hop, core, orders[group][level]),
            device_id_type=MESH,
        )
        copy.start()
        up[group, level] = copy

    for group in range(groups):
        halve(group, 0)
    for level in range(levels):
        for group in range(groups):
            half = rows >> (level + 1)
            part = pl.ds(pl.multiple_of(kept[group][level], half), half)
            down[group, level].wait_recv()
            total = held[part] + inbox[group, pl.ds(places[level], half)]
            if level < levels - 1:
                held[part] = total
                halve(group, level + 1)
            else:
                sum_ref[part] = total
                double(group, level)
    for level in range(levels - 1, -1, -1):
        for group in range(groups):
            up[group, level].wait_recv()
            if level > 0:
                double(group, level - 1)
    for level in range(levels):
        for group in range(groups):
            down[group, level].wait_send()
            up[group, level].wait_send()


def sum_over_devices(part, hop_count):
    rows, columns = part.shape
    orders = halving_orders(hop_count, rows)
    groups, levels = len(orders), len(orders[0])
    semaphores = pltpu.SemaphoreType.DMA((groups, levels))
    return pl.pallas_call(
        functools.partial(sum_kernel, orders),
        name="weight_gradient_sum",
        out_shape=jax.ShapeDtypeStruct((rows, columns), part.dtype),
        in_specs=[pl.BlockSpec(memory_space=pltpu.VMEM)],
        out_specs=pl.BlockSpec(memory_space=pltpu.VMEM),
        scratch_shapes=[
            pltpu.VMEM((rows, columns), part.dtype),
            pltpu.VMEM((groups, rows // groups, columns), part.dtype),
            semaphores,
            semaphores,
            semaphores,
            semaphores,
        ],
        compiler_params=pltpu.CompilerParams(
            collective_id=0, has_side_effects=True, vmem_limit_bytes=48 << 20
        ),
    )(part)


def plain_body(
    child_feats,
    board_mask,
    importance,
    parent_slot,
    send_counts,
    parent_feats,
    proj_weight,
    q_weight,
    q_bias,
    w_weight,
    w_bias,
    emb_cotangent,
):
    slot_rows, feature_width = child_feats.shape
    hop_count = lax.axis_size("hop")
    par_count = lax.axis_size("par")
    shard_count = hop_count * par_count
    slot_cap = slot_rows // shard_count
    live_slots = (
        (jnp.arange(slot_cap)[None, :] < send_counts[0][:, None])
        .astype(jnp.float32)
        .reshape(slot_rows)
    )
    weight_live = importance * live_slots
    is_board = board_mask[:, None] == 1
    projected = jnp.dot(child_feats, proj_weight, preferred_element_type=jnp.float32)
    merged = jnp.where(is_board, projected, child_feats.astype(jnp.float32)).astype(jnp.bfloat16)
    pre_act = jnp.dot(merged, q_weight, preferred_element_type=jnp.float32) + q_bias
    message = (weight_live[:, None] * jax.nn.silu(pre_act)).astype(jnp.bfloat16)
    edge_info = jnp.stack([weight_live, parent_slot.astype(jnp.float32)]).reshape(
        2, shard_count, slot_cap
    )
    got_info = lax.all_to_all(edge_info, ("hop", "par"), split_axis=1, concat_axis=1, tiled=True)
    got_weight = got_info[0].reshape(slot_rows)
    got_slot = got_info[1].reshape(slot_rows).astype(jnp.int32)
    arrived = send_rows(message, hop_count, par_count, slot_cap, feature_width)
    parent_rows = parent_feats.shape[0]
    owner_table = got_slot[None, :] == jnp.arange(parent_rows, dtype=jnp.int32)[:, None]
    gathered = jnp.dot(
        owner_table.astype(jnp.bfloat16), arrived, preferred_element_type=jnp.float32
    )
    weight_sum = jnp.sum(jnp.where(owner_table, got_weight[None, :], 0.0), axis=1)
    divisor = jnp.maximum(weight_sum, 1.0)
    neighbor_mean = (gathered / divisor[:, None]).astype(jnp.bfloat16)
    joined = jnp.concatenate([parent_feats, neighbor_mean], axis=1)
    pre_norm = jnp.dot(joined, w_weight, preferred_element_type=jnp.float32) + w_bias
    act_out = jax.nn.silu(pre_norm)
    inv_norm = lax.rsqrt(jnp.sum(act_out * act_out, axis=1, keepdims=True) + 1e-06)
    embedding = act_out * inv_norm
    grad_emb = inv_norm * (
        emb_cotangent - embedding * jnp.sum(emb_cotangent * embedding, axis=1, keepdims=True)
    )
    grad_pre = (grad_emb * silu_slope(pre_norm)).astype(jnp.bfloat16)
    grad_w = contract_rows(joined, grad_pre)
    grad_wbias = jnp.sum(grad_pre.astype(jnp.float32), axis=0)
    grad_cat = times_transpose(grad_pre, w_weight)
    grad_parent = grad_cat[:, :feature_width]
    grad_mean = grad_cat[:, feature_width:] / divisor[:, None]
    return_rows = jnp.take(grad_mean, got_slot, axis=0).astype(jnp.bfloat16)
    grad_message = send_rows(return_rows, hop_count, par_count, slot_cap, feature_width)
    grad_act = weight_live[:, None] * grad_message.astype(jnp.float32)
    grad_preact = (grad_act * silu_slope(pre_act)).astype(jnp.bfloat16)
    grad_q = contract_rows(merged, grad_preact)
    grad_qbias = jnp.sum(grad_preact.astype(jnp.float32), axis=0)
    grad_merged = times_transpose(grad_preact, q_weight)
    grad_board = jnp.where(is_board, grad_merged, 0.0).astype(jnp.bfloat16)
    grad_proj = contract_rows(child_feats, grad_board)
    grad_child = (
        jnp.where(is_board, 0.0, grad_merged) + times_transpose(grad_board, proj_weight)
    ).astype(jnp.bfloat16)
    part = jnp.concatenate([grad_w, grad_q, grad_proj]).astype(jnp.bfloat16)
    summed = sum_over_devices(part, hop_count)
    summed = summed.astype(jnp.float32)
    grad_qbias, grad_wbias = lax.psum((grad_qbias, grad_wbias), ("hop", "par"))
    w_rows, q_rows = grad_w.shape[0], grad_q.shape[0]
    return (
        embedding,
        grad_child,
        grad_parent,
        summed[w_rows + q_rows :],
        summed[w_rows : w_rows + q_rows],
        grad_qbias,
        summed[:w_rows],
        grad_wbias,
    )


TILE = 512
BLOCK = 128


def columns(index, width=TILE):
    return pl.ds(pl.multiple_of(index * width, width), width)


def mm(left, right):
    return jnp.dot(left, right, preferred_element_type=jnp.float32)


def sigmoid(value):
    return 0.5 * jnp.tanh(0.5 * value) + 0.5


def spread(column, width):
    return jnp.concatenate([column] * (width // column.shape[1]), axis=1)


class Sums:
    def __init__(self, hop, core, groups, held, inbox, total, sems):
        self.hop, self.core, self.groups = hop, core, groups
        self.held, self.inbox, self.total = held, inbox, total
        self.send, self.recv, self.out, self.into, self.own = sems
        self.levels = len(groups[0][2])
        low, high = own_bit(hop, core, 2), own_bit(hop, core, 3)
        self.is_inner = low != high
        self.high = high
        place = 0
        self.plans = []
        for first, rows, order in groups:
            start, size, inner, steps = jnp.int32(first), rows, False, []
            for kind in order:
                if kind == "i":
                    step = (kind, start, start, size, place, inner)
                    inner = True
                else:
                    size //= 2
                    mine = high if kind == "m" else own_bit(hop, core, "cxypq".index(kind) - 1)
                    step = (kind, start + (1 - mine) * size, start + mine * size, size, place, inner)
                    start = start + mine * size
                    inner = inner or kind == "m"
                steps.append(step)
                place += size
            self.plans.append(steps)

    def other(self, kind):
        if kind == "m":
            return (self.hop + (1 - 2 * self.high) * 4, self.core)
        return partner(self.hop, self.core, "cxypq".index(kind.replace("i", "p")) - 1)

    def when(self, role, what):
        if role is None:
            what()
        else:
            pl.when(self.is_inner if role == "inner" else jnp.logical_not(self.is_inner))(what)

    def roles(self, group, level, upward):
        kind, _, _, _, _, inner = self.plans[group][level]
        if kind == "i":
            return ("inner", "outer") if upward else ("outer", "inner")
        role = "inner" if inner or kind == "m" else None
        return role, role

    def rows(self, start, size):
        return pl.ds(pl.multiple_of(start, size), size)

    def down(self, group, level):
        kind, away, _, size, place, _ = self.plans[group][level]
        return pltpu.make_async_remote_copy(
            src_ref=self.held.at[self.rows(away, size)],
            dst_ref=self.inbox.at[pl.ds(place, size)],
            send_sem=self.send.at[group, level],
            recv_sem=self.recv.at[group, level],
            device_id=self.other(kind),
            device_id_type=MESH,
        )

    def up(self, group, level):
        kind, _, kept, size, _, _ = self.plans[group][level]
        source = self.held if level == self.levels - 1 else self.total
        part = self.rows(kept, size)
        return pltpu.make_async_remote_copy(
            src_ref=source.at[part],
            dst_ref=self.total.at[part],
            send_sem=self.out.at[group, level],
            recv_sem=self.into.at[group, level],
            device_id=self.other(kind),
            device_id_type=MESH,
        )

    def own_copy(self, group):
        _, _, kept, size, _, _ = self.plans[group][-1]
        part = self.rows(kept, size)
        return pltpu.make_async_copy(self.held.at[part], self.total.at[part], self.own.at[group])

    def halve(self, group, level):
        self.when(self.roles(group, level, False)[0], lambda: self.down(group, level).start())

    def double(self, group, level):
        self.when(self.roles(group, level, True)[0], lambda: self.up(group, level).start())

    def fold(self, group, level):
        _, _, kept, size, place, _ = self.plans[group][level]

        def add():
            self.down(group, level).wait_recv()
            part = self.rows(kept, size)
            self.held[part] = self.held[part] + self.inbox[pl.ds(place, size)]
            if level == self.levels - 1:
                self.own_copy(group).start()
                self.up(group, level).start()

        self.when(self.roles(group, level, False)[1], add)
        if level < self.levels - 1:
            self.halve(group, level + 1)

    def gather(self, group, level):
        def take():
            if level == self.levels - 1:
                self.own_copy(group).wait()
            self.up(group, level).wait_recv()

        self.when(self.roles(group, level, True)[1], take)
        if level > 0:
            self.double(group, level - 1)

    def finish(self):
        for group in range(len(self.groups)):
            for level in range(self.levels):
                self.when(
                    self.roles(group, level, False)[0], lambda: self.down(group, level).wait_send()
                )
                self.when(self.roles(group, level, True)[0], lambda: self.up(group, level).wait_send())


def layer_kernel(
    groups,
    child_in,
    importance,
    board,
    slot,
    counts,
    parent_in,
    proj_in,
    q_in,
    q_bias,
    w_in,
    w_bias,
    cot_in,
    emb_out,
    child_out,
    parent_out,
    total,
    bias_out,
    child,
    proj,
    q,
    w,
    parent,
    cot,
    merged,
    scaled_slope,
    message,
    arrived,
    moved,
    pre,
    table_rows,
    grad_pre,
    grad_moved,
    back_out,
    back_in,
    held,
    inbox,
    emb,
    weight_col,
    board_col,
    shrink,
    slot_shrink,
    got_weight,
    got_slot,
    info_out,
    info_in,
    bias_held,
    bias_in,
    load_sem,
    store_sem,
    info_sem,
    msg_sem,
    back_sem,
    bias_sem,
    sum_send,
    sum_recv,
    sum_out,
    sum_in,
    sum_own,
):
    hop, core = lax.axis_index("hop"), lax.axis_index("par")
    me = hop * 2 + core
    slots, width = child.shape
    parents = parent.shape[0]
    devices = counts.shape[1]
    cap = slots // devices
    half = slots // 2
    levels = bias_held.shape[0]
    tiles = width // TILE
    upper = own_bit(hop, core, levels - 2)
    sides = (1 - upper, upper)
    f32, bf16 = jnp.float32, jnp.bfloat16

    def other_hop(flips):
        to_hop = hop
        for bit in range(levels - 1):
            if (flips >> bit) & 1:
                to_hop = to_hop + (1 - 2 * own_bit(hop, core, bit)) * (1 << bit)
        return to_hop

    def targets(first, last):
        away = [(other_hop(flips), to_core) for to_core in range(2) for flips in range(last - 1, max(first, 1) - 1, -1)]
        return away + ([(hop, 1 - core)] if first == 0 else [])

    def rows_of(device):
        return pl.ds(pl.multiple_of(device * cap, cap), cap)

    def side_rows(side):
        return pl.ds(pl.multiple_of(side * half, half), half)

    loads = []
    for index, (source, place) in enumerate(
        ((child_in, child), (proj_in, proj), (q_in, q), (parent_in, parent), (w_in, w), (cot_in, cot))
    ):
        loads.append(pltpu.make_async_copy(source, place, load_sem.at[index]))
    for copy in loads[:3]:
        copy.start()

    barrier = pltpu.get_barrier_semaphore()
    for to in targets(0, devices // 2):
        pl.semaphore_signal(barrier, inc=1, device_id=to, device_id_type=MESH)

    lane = lax.broadcasted_iota(jnp.int32, (128, 128), 1)
    down = lax.broadcasted_iota(jnp.int32, (128, 128), 0)
    eye = lane == down
    place = lax.rem(down, cap)

    def column(row):
        return jnp.sum(jnp.where(eye, jnp.broadcast_to(row, (128, 128)), 0.0), axis=1, keepdims=True)

    count_row = counts[...].astype(f32)
    for part in range(slots // 128):
        owner = lax.broadcasted_iota(jnp.int32, (128, devices), 0) // cap + part * (128 // cap)
        is_owner = owner == lax.broadcasted_iota(jnp.int32, (128, devices), 1)
        live = jnp.sum(
            jnp.where(is_owner, jnp.broadcast_to(count_row, (128, devices)), 0.0), axis=1, keepdims=True
        )
        weight = jnp.broadcast_to(column(importance[part : part + 1, :]), (128, 128))
        weight = jnp.where(place.astype(f32) < live, weight, 0.0)
        slot_at = jnp.broadcast_to(column(slot[part : part + 1, :].astype(f32)), (128, 128))
        at = slice(part * 128, (part + 1) * 128)
        weight_col[at, :] = weight
        board_col[at, :] = jnp.broadcast_to(column(board[part : part + 1, :].astype(f32)), (128, 128))
        info = jnp.where(lane == place, weight, 0.0) + jnp.where(lane == place + cap, slot_at, 0.0)
        for owner_at in range(128 // cap):
            info_out[part * (128 // cap) + owner_at] = jnp.sum(
                info[owner_at * cap : (owner_at + 1) * cap, :], axis=0, keepdims=True
            )

    def send_info():
        pl.semaphore_wait(barrier, devices - 1)

        for to_hop, to_core in targets(0, devices // 2):
            pltpu.make_async_remote_copy(
                src_ref=info_out.at[to_hop * 2 + to_core],
                dst_ref=info_in.at[me],
                send_sem=info_sem.at[0],
                recv_sem=info_sem.at[1],
                device_id=(to_hop, to_core),
                device_id_type=MESH,
            ).start()
        pltpu.make_async_copy(info_out.at[me], info_in.at[me], info_sem.at[1]).start()

    def send_side(source, place_ref, sem, side_index):
        quarter = devices // 4
        for to_hop, to_core in targets(quarter, 2 * quarter) if side_index == 0 else targets(0, quarter):
            pltpu.make_async_remote_copy(
                src_ref=source.at[rows_of(to_hop * 2 + to_core)],
                dst_ref=place_ref.at[rows_of(me)],
                send_sem=sem.at[0, side_index],
                recv_sem=sem.at[1, side_index],
                device_id=(to_hop, to_core),
                device_id_type=MESH,
            ).start()
        if side_index == 1:
            pltpu.make_async_copy(
                source.at[rows_of(me)], place_ref.at[rows_of(me)], sem.at[1, side_index]
            ).start()

    def wait_side(place_ref, sem, side_index):
        rows = side_rows(sides[side_index])
        pltpu.make_async_copy(place_ref.at[rows], place_ref.at[rows], sem.at[1, side_index]).wait()

    def wait_sent(source, sem):
        for side_index, rows in ((0, half), (1, half - cap)):
            part = source.at[pl.ds(0, rows)]
            pltpu.make_async_copy(part, part, sem.at[0, side_index]).wait()

    loads[0].wait()
    loads[1].wait()
    for side_index, side in enumerate(sides):
        rows = side_rows(side)
        boards = spread(board_col[rows, :], TILE) == 1.0

        @pl.loop(0, tiles)
        def _(tile):
            projected = mm(child[rows, :], proj[:, columns(tile)])
            raw = child[rows, columns(tile)]
            merged[rows, columns(tile)] = jnp.where(boards, projected, raw.astype(f32)).astype(bf16)

        if side_index == 0:
            loads[2].wait()
            for copy in loads[3:]:
                copy.start()
        weights = spread(weight_col[rows, :], TILE)

        @pl.loop(0, tiles)
        def _(tile):
            value = mm(merged[rows, :], q[:, columns(tile)]) + q_bias[:, columns(tile)]
            gate = sigmoid(value)
            act = value * gate
            message[rows, columns(tile)] = (weights * act).astype(bf16)
            scaled_slope[rows, columns(tile)] = weights * (gate + act * (1.0 - gate))

        if side_index == 0:
            send_info()
        send_side(message, arrived, msg_sem, side_index)

    loads[3].wait()
    loads[4].wait()

    @pl.loop(0, tiles)
    def _(tile):
        pre[:, columns(tile)] = mm(parent[...], w[pl.ds(0, width), columns(tile)]) + w_bias[:, columns(tile)]

    info_all = pltpu.make_async_copy(info_in, info_in, info_sem.at[1])
    info_all.wait()
    lane16 = lax.broadcasted_iota(jnp.int32, (cap, 128), 1)
    down16 = lax.broadcasted_iota(jnp.int32, (cap, 128), 0)
    for device in range(devices):
        got = jnp.broadcast_to(info_in[device], (cap, 128))
        at = slice(device * cap, (device + 1) * cap)
        got_weight[at, :] = jnp.broadcast_to(
            jnp.sum(jnp.where(lane16 == down16, got, 0.0), axis=1, keepdims=True), (cap, 128)
        )
        got_slot[at, :] = jnp.broadcast_to(
            jnp.sum(jnp.where(lane16 == down16 + cap, got, 0.0), axis=1, keepdims=True), (cap, 128)
        )

    for part in range(parents // 128):
        want = (lax.broadcasted_iota(jnp.int32, (128, 128), 1) + part * 128).astype(f32)
        weight_sum = jnp.zeros((1, 128), f32)
        for block in range(slots // 128):
            at = slice(block * 128, (block + 1) * 128)
            hit = got_slot[at, :] == want
            table_rows[at, part * 128 : (part + 1) * 128] = jnp.where(hit, 1.0, 0.0).astype(bf16)
            weight_sum = weight_sum + jnp.sum(jnp.where(hit, got_weight[at, :], 0.0), axis=0, keepdims=True)
        inverse = 1.0 / jnp.maximum(weight_sum, 1.0)
        shrink[part * 128 : (part + 1) * 128, :] = jnp.broadcast_to(column(inverse), (128, 128))
        for block in range(slots // 128):
            at = slice(block * 128, (block + 1) * 128)
            hit = got_slot[at, :] == want
            term = jnp.where(hit, jnp.broadcast_to(inverse, (128, 128)), 0.0)
            if part == 0:
                slot_shrink[at, :] = term
            else:
                slot_shrink[at, :] = slot_shrink[at, :] + term
    for block in range(slots // 128):
        at = slice(block * 128, (block + 1) * 128)
        slot_shrink[at, :] = jnp.broadcast_to(
            jnp.sum(slot_shrink[at, :], axis=1, keepdims=True), (128, 128)
        )

    def add_messages(side_index):
        rows = side_rows(sides[side_index])

        @pl.loop(0, tiles)
        def _(tile):
            moved[rows, columns(tile)] = mm(arrived[rows, :], w[pl.ds(width, width), columns(tile)]).astype(bf16)

        @pl.loop(0, tiles)
        def _(tile):
            pre[:, columns(tile)] = pre[:, columns(tile)] + spread(shrink[...], TILE) * contract_rows(
                table_rows[rows, :], moved[rows, columns(tile)]
            )

    wait_side(arrived, msg_sem, 1)
    add_messages(1)
    loads[5].wait()
    wait_side(arrived, msg_sem, 0)
    add_messages(0)

    @pl.loop(0, parents // BLOCK)
    def _(block):
        at = columns(block, BLOCK)
        value = pre[at, :]
        turn = cot[at, :]
        gate = sigmoid(value)
        act = value * gate
        inv = lax.rsqrt(jnp.sum(act * act, axis=1, keepdims=True) + 1e-06)
        share = jnp.sum(turn * act, axis=1, keepdims=True) * (inv * inv * inv)
        emb[at, :] = (act * inv).astype(bf16)
        grad_pre[at, :] = ((turn * inv - act * share) * (gate + act * (1.0 - gate))).astype(bf16)

    stores = [pltpu.make_async_copy(emb, emb_out, store_sem.at[0])]
    stores[0].start()

    for side_index, side in enumerate(sides):
        rows = side_rows(side)
        shrinks = spread(slot_shrink[rows, :], TILE)

        @pl.loop(0, tiles)
        def _(tile):
            grad_moved[rows, columns(tile)] = (
                shrinks * mm(table_rows[rows, :], grad_pre[:, columns(tile)])
            ).astype(bf16)

        @pl.loop(0, tiles)
        def _(tile):
            turned = w[pl.ds(pl.multiple_of(width + tile * TILE, TILE), TILE), :]
            back_out[rows, columns(tile)] = times_transpose(grad_moved[rows, :], turned).astype(bf16)

        send_side(back_out, back_in, back_sem, side_index)

    sums = Sums(hop, core, groups, held, inbox, total, (sum_send, sum_recv, sum_out, sum_in, sum_own))
    w_groups = [g for g, (first, _, _) in enumerate(groups) if first < 2 * width]
    q_groups = [g for g, (first, _, _) in enumerate(groups) if 2 * width <= first < 3 * width]
    p_groups = [g for g, (first, _, _) in enumerate(groups) if first >= 3 * width]

    @pl.loop(0, tiles)
    def _(tile):
        held[pl.ds(0, width), columns(tile)] = contract_rows(parent[...], grad_pre[:, columns(tile)]).astype(bf16)

    for group in w_groups[: len(w_groups) // 2]:
        sums.halve(group, 0)

    @pl.loop(0, tiles)
    def _(tile):
        held[pl.ds(width, width), columns(tile)] = contract_rows(
            arrived[...], grad_moved[:, columns(tile)]
        ).astype(bf16)

    for group in w_groups[len(w_groups) // 2 :]:
        sums.halve(group, 0)
    bias_held[0, 0:1, :] = mm(jnp.ones((16, parents), bf16), grad_pre[...])[0:1, :]

    def parent_gradient():
        @pl.loop(0, tiles)
        def _(tile):
            parent[:, columns(tile)] = times_transpose(grad_pre[...], w[columns(tile), :]).astype(bf16)

        stores.append(pltpu.make_async_copy(parent, parent_out, store_sem.at[1]))
        stores[1].start()
        wait_sent(message, msg_sem)

    def child_front(side_index):
        rows = side_rows(sides[side_index])

        @pl.loop(0, tiles)
        def _(tile):
            grad_moved[rows, columns(tile)] = (
                scaled_slope[rows, columns(tile)] * back_in[rows, columns(tile)].astype(f32)
            ).astype(bf16)

    def weight_sums(side_index, left, grads, partial, base):
        rows = side_rows(sides[side_index])

        @pl.loop(0, tiles)
        def _(tile):
            value = contract_rows(left[rows, :], grads[rows, columns(tile)])
            if side_index == 1:
                partial[:, columns(tile)] = value
            else:
                held[pl.ds(base, width), columns(tile)] = (value + partial[:, columns(tile)]).astype(bf16)

    def child_middle(side_index):
        rows = side_rows(sides[side_index])
        boards = spread(board_col[rows, :], TILE) == 1.0

        @pl.loop(0, tiles)
        def _(tile):
            value = times_transpose(grad_moved[rows, :], q[columns(tile), :])
            moved[rows, columns(tile)] = jnp.where(boards, value, 0.0).astype(bf16)
            scaled_slope[rows, columns(tile)] = jnp.where(boards, 0.0, value)

    def child_end(side_index):
        rows = side_rows(sides[side_index])

        @pl.loop(0, tiles)
        def _(tile):
            value = times_transpose(moved[rows, :], proj[columns(tile), :])
            message[rows, columns(tile)] = (scaled_slope[rows, columns(tile)] + value).astype(bf16)

    bias_copies = []

    def send_bias(level):
        copy = pltpu.make_async_remote_copy(
            src_ref=bias_held.at[level],
            dst_ref=bias_in.at[level],
            send_sem=bias_sem.at[0, level],
            recv_sem=bias_sem.at[1, level],
            device_id=partner(hop, core, level - 1),
            device_id_type=MESH,
        )
        copy.start()
        bias_copies.append(copy)

    def fold_bias(level):
        bias_copies[level].wait_recv()
        both = bias_held[level] + bias_in[level]
        if level < levels - 1:
            bias_held[level + 1] = both
            send_bias(level + 1)
        else:
            bias_out[...] = both

    def near_children():
        child_front(1)
        weight_sums(1, merged, grad_moved, pre, 2 * width)
        child_middle(1)
        weight_sums(1, child, moved, cot, 3 * width)
        child_end(1)

    def far_q():
        child_front(0)
        weight_sums(0, merged, grad_moved, pre, 2 * width)

    def far_p():
        child_middle(0)
        weight_sums(0, child, moved, cot, 3 * width)

    def send_q():
        for group in q_groups:
            sums.halve(group, 0)
        bias_held[0, 1:2, :] = mm(jnp.ones((16, slots), bf16), grad_moved[...])[0:1, :]
        send_bias(0)

    def far_end():
        child_end(0)
        stores.append(pltpu.make_async_copy(message, child_out, store_sem.at[2]))
        stores[2].start()

    main = [
        parent_gradient,
        lambda: wait_side(back_in, back_sem, 1),
        near_children,
        lambda: wait_side(back_in, back_sem, 0),
        far_q,
        send_q,
        far_p,
        lambda: [sums.halve(group, 0) for group in p_groups],
        far_end,
    ]
    done = [0] * (len(groups) + 1)
    for turn in SCHEDULE:
        at = done[turn]
        done[turn] += 1
        if turn == 0:
            main[at]()
        elif at < sums.levels:
            sums.fold(turn - 1, at)
            if turn - 1 == q_groups[0]:
                fold_bias(at)
        else:
            sums.gather(turn - 1, 2 * sums.levels - 1 - at)

    sums.finish()
    for copy in bias_copies:
        copy.wait_send()
    wait_sent(back_out, back_sem)
    sent = info_out.at[pl.ds(0, devices - 1)]
    pltpu.make_async_copy(sent, sent, info_sem.at[0]).wait()
    for copy in stores:
        copy.wait()


GROUPS = [("cxyim", 2), ("cyxim", 2), ("cxyim", 2), ("cyxim", 2), ("cxyim", 4), ("cyxim", 4), ("cxyim", 4), ("cyxim", 4), ("cxyim", 4), ("cyxim", 4), ("cxyim", 4), ("cyxim", 4)]
SCHEDULE = [
    3, 4, 0, 1, 2, 0, 0, 3, 4, 0, 0, 0, 1, 2, 3, 4, 0, 5, 6, 0, 11, 12, 9, 10, 3, 4, 0, 1, 2, 7, 8, 3, 4, 5, 6, 1,
    2, 11, 12, 3, 4, 9, 10, 5, 6, 1, 2, 7, 8, 11, 12, 3, 4, 9, 10, 7, 8, 5, 6, 1, 2, 3, 4, 11, 12, 1, 2, 9, 10, 5, 6, 7,
    8, 5, 6, 11, 12, 1, 2, 5, 6, 9, 10, 11, 12, 7, 8, 9, 10, 11, 12, 3, 4, 9, 10, 7, 8, 7, 8, 5, 6, 11, 12, 1, 2, 9, 10, 5,
    6, 7, 8, 3, 4, 11, 12, 9, 10, 7, 8, 5, 6, 1, 2, 11, 12, 9, 10, 7, 8,
]


def sum_groups(width):
    groups, first = [], 0
    for order, share in GROUPS:
        groups.append((first, width // share, order))
        first += width // share
    return groups


def inbox_rows(groups):
    total = 0
    for _, size, order in groups:
        for kind in order:
            size = size if kind == "i" else size // 2
            total += size
    return total


def widen_kernel(
    emb,
    child,
    parent,
    total,
    biases,
    emb_out,
    child_out,
    parent_out,
    proj_out,
    q_out,
    q_bias_out,
    w_out,
    w_bias_out,
    narrow,
    wide,
    through,
    read_sem,
    write_sem,
    child_sem,
):
    slots, rows, width = narrow.shape
    through_in = pltpu.make_async_copy(child, through, child_sem.at[0])
    through_out = pltpu.make_async_copy(through, child_out, child_sem.at[1])
    pieces = []
    base = 0
    for place in (w_out, q_out, proj_out):
        for first in range(0, place.shape[0], rows):
            pieces.append((total, base + first, place, first))
        base += place.shape[0]
    for source, place in ((parent, parent_out), (emb, emb_out)):
        for first in range(0, place.shape[0], rows):
            pieces.append((source, first, place, first))

    def read(index):
        source, first, _, _ = pieces[index]
        slot = index % slots
        return pltpu.make_async_copy(source.at[pl.ds(first, rows)], narrow.at[slot], read_sem.at[slot])

    def write(index):
        _, _, place, first = pieces[index]
        slot = index % slots
        return pltpu.make_async_copy(wide.at[slot], place.at[pl.ds(first, rows)], write_sem.at[slot])

    for index in range(slots):
        read(index).start()
    through_in.start()
    w_bias_out[...] = biases[0, :]
    q_bias_out[...] = biases[1, :]
    for index in range(len(pieces)):
        read(index).wait()
        if index >= slots:
            write(index - slots).wait()
        wide[index % slots] = narrow[index % slots].astype(jnp.float32)
        write(index).start()
        if index + slots < len(pieces):
            read(index + slots).start()
        if index == slots:
            through_in.wait()
            through_out.start()
    for index in range(len(pieces) - slots, len(pieces)):
        write(index).wait()
    through_out.wait()


def widen(emb, child, parent, total, biases):
    width = emb.shape[1]
    slots, rows = 4, 512
    shape, f32 = jax.ShapeDtypeStruct, jnp.float32
    hbm = pl.BlockSpec(memory_space=pl.ANY)
    vmem = pl.BlockSpec(memory_space=pltpu.VMEM)
    return pl.pallas_call(
        widen_kernel,
        name="widen",
        out_shape=(
            shape(emb.shape, f32),
            shape(child.shape, child.dtype),
            shape(parent.shape, f32),
            shape((width, width), f32),
            shape((width, width), f32),
            shape((width,), f32),
            shape((2 * width, width), f32),
            shape((width,), f32),
        ),
        in_specs=[hbm, hbm, hbm, hbm, vmem],
        out_specs=(hbm, hbm, hbm, hbm, hbm, vmem, hbm, vmem),
        scratch_shapes=[
            pltpu.VMEM((slots, rows, width), child.dtype),
            pltpu.VMEM((slots, rows, width), f32),
            pltpu.VMEM(child.shape, child.dtype),
            pltpu.SemaphoreType.DMA((slots,)),
            pltpu.SemaphoreType.DMA((slots,)),
            pltpu.SemaphoreType.DMA((2,)),
        ],
        compiler_params=pltpu.CompilerParams(vmem_limit_bytes=62 << 20),
    )(emb, child, parent, total, biases)


def fused_body(
    child_feats,
    board_mask,
    importance,
    parent_slot,
    send_counts,
    parent_feats,
    proj_weight,
    q_weight,
    q_bias,
    w_weight,
    w_bias,
    emb_cotangent,
):
    slots, width = child_feats.shape
    parents = parent_feats.shape[0]
    devices = send_counts.shape[1]
    groups = sum_groups(width)
    levels = devices.bit_length() - 1
    f32, bf16 = jnp.float32, jnp.bfloat16
    vmem = pl.BlockSpec(memory_space=pltpu.VMEM)
    hbm = pl.BlockSpec(memory_space=pl.ANY)
    dma = pltpu.SemaphoreType.DMA
    shape = jax.ShapeDtypeStruct
    emb, grad_child, grad_parent, total, biases = pl.pallas_call(
        functools.partial(layer_kernel, groups),
        name="layer",
        out_shape=(
            shape((parents, width), bf16),
            shape((slots, width), bf16),
            shape((parents, width), bf16),
            shape((4 * width, width), bf16),
            shape((2, width), f32),
        ),
        in_specs=[hbm, vmem, vmem, vmem, vmem, hbm, hbm, hbm, vmem, hbm, vmem, hbm],
        out_specs=(hbm, hbm, hbm, hbm, vmem),
        scratch_shapes=[
            pltpu.VMEM((slots, width), bf16),
            pltpu.VMEM((width, width), bf16),
            pltpu.VMEM((width, width), bf16),
            pltpu.VMEM((2 * width, width), bf16),
            pltpu.VMEM((parents, width), bf16),
            pltpu.VMEM((parents, width), f32),
            pltpu.VMEM((slots, width), bf16),
            pltpu.VMEM((slots, width), f32),
            pltpu.VMEM((slots, width), bf16),
            pltpu.VMEM((slots, width), bf16),
            pltpu.VMEM((slots, width), bf16),
            pltpu.VMEM((parents, width), f32),
            pltpu.VMEM((slots, parents), bf16),
            pltpu.VMEM((parents, width), bf16),
            pltpu.VMEM((slots, width), bf16),
            pltpu.VMEM((slots, width), bf16),
            pltpu.VMEM((slots, width), bf16),
            pltpu.VMEM((4 * width, width), bf16),
            pltpu.VMEM((inbox_rows(groups), width), bf16),
            pltpu.VMEM((parents, width), bf16),
            pltpu.VMEM((slots, 128), f32),
            pltpu.VMEM((slots, 128), f32),
            pltpu.VMEM((parents, 128), f32),
            pltpu.VMEM((slots, 128), f32),
            pltpu.VMEM((slots, 128), f32),
            pltpu.VMEM((slots, 128), f32),
            pltpu.VMEM((devices, 1, 128), f32),
            pltpu.VMEM((devices, 1, 128), f32),
            pltpu.VMEM((levels, 2, width), f32),
            pltpu.VMEM((levels, 2, width), f32),
            dma((6,)),
            dma((3,)),
            dma((2,)),
            dma((2, 2)),
            dma((2, 2)),
            dma((2, levels)),
        ]
        + [dma((len(groups), len(groups[0][2])))] * 4
        + [dma((len(groups),))],
        compiler_params=pltpu.CompilerParams(
            collective_id=1, has_side_effects=True, vmem_limit_bytes=62 << 20
        ),
        cost_estimate=pl.CostEstimate(
            flops=36 * slots * width * width, bytes_accessed=40 << 20, transcendentals=3 * parents * width
        ),
    )(
        child_feats,
        importance.reshape(-1, 128),
        board_mask.reshape(-1, 128),
        parent_slot.reshape(-1, 128),
        send_counts,
        parent_feats,
        proj_weight,
        q_weight,
        q_bias.reshape(1, -1),
        w_weight,
        w_bias.reshape(1, -1),
        emb_cotangent,
    )
    return widen(emb, grad_child, grad_parent, total, biases)


def solution(mesh):
    rows = P(("hop", "par"), None)
    flat = P(("hop", "par"))
    fused = mesh.shape["hop"] == 16 and mesh.shape["par"] == 2
    return jax.shard_map(
        fused_body if fused else plain_body,
        mesh=mesh,
        in_specs=(rows, flat, flat, flat, rows, rows, P(), P(), P(), P(), P(), rows),
        out_specs=(rows, rows, rows, P(), P(), P(), P(), P()),
        check_vma=False,
    )
```

```python
import functools

import jax
import jax.numpy as jnp
from jax import lax
from jax.experimental import pallas as pl
from jax.experimental.pallas import tpu as pltpu
from jax.sharding import PartitionSpec as P

MESH = pl.DeviceIdType.MESH
CORE = -1


def times_transpose(left, right):
    return lax.dot_general(
        left, right, (((1,), (1,)), ((), ())), preferred_element_type=jnp.float32
    )


def contract_rows(left, right):
    return lax.dot_general(
        left, right, (((0,), (0,)), ((), ())), preferred_element_type=jnp.float32
    )


def silu_slope(value):
    sigma = jax.nn.sigmoid(value)
    return sigma * (1.0 + value * (1.0 - sigma))


def send_rows(payload, hop_count, par_count, slot_cap, feature_width):
    parcel = payload.reshape(hop_count * par_count, slot_cap, feature_width)
    arrived = lax.all_to_all(parcel, ("hop", "par"), split_axis=0, concat_axis=0, tiled=True)
    return arrived.reshape(payload.shape)


def halving_orders(hop_count, rows):
    bits = hop_count.bit_length() - 1
    if bits == 4:
        x, y, z0, z1 = range(4)
        base = [[x, y, z0, z1], [y, x, z0, z1], [z0, x, y, z1], [x, y, z0, z1]]
        base += [[y, x, z0, z1], [z0, y, x, z1], [x, y, z0, z1], [y, x, z0, z1]]
    else:
        base = [[(first + k) % bits for k in range(bits)] for first in range(0, bits, 2)]
    groups = 1
    while groups * 2 <= len(base) and rows // (groups * 2) // (hop_count * 2) >= 16:
        groups *= 2
    return [[CORE] + order for order in base[:groups]]


def own_bit(hop, core, bit):
    return core if bit == CORE else lax.rem(hop // (1 << bit), 2)


def partner(hop, core, bit):
    if bit == CORE:
        return (hop, 1 - core)
    return (hop + (1 - 2 * own_bit(hop, core, bit)) * (1 << bit), core)


def sum_kernel(orders, part_ref, sum_ref, held, inbox, send_sem, recv_sem, out_sem, in_sem):
    hop, core = lax.axis_index("hop"), lax.axis_index("par")
    groups, levels = len(orders), len(orders[0])
    rows = part_ref.shape[0] // groups
    barrier = pltpu.get_barrier_semaphore()
    for bit in range(CORE, levels - 1):
        pl.semaphore_signal(barrier, inc=1, device_id=partner(hop, core, bit), device_id_type=MESH)
    held[...] = part_ref[...]
    pl.semaphore_wait(barrier, levels)

    start = [jnp.int32(group * rows) for group in range(groups)]
    kept = [[None] * levels for _ in range(groups)]
    places = [rows - (rows >> level) for level in range(levels)]
    down, up = {}, {}

    def halve(group, level):
        bit = orders[group][level]
        half = rows >> (level + 1)
        mine = own_bit(hop, core, bit)
        away = pl.multiple_of(start[group] + (1 - mine) * half, half)
        copy = pltpu.make_async_remote_copy(
            src_ref=held.at[pl.ds(away, half)],
            dst_ref=inbox.at[group, pl.ds(places[level], half)],
            send_sem=send_sem.at[group, level],
            recv_sem=recv_sem.at[group, level],
            device_id=partner(hop, core, bit),
            device_id_type=MESH,
        )
        copy.start()
        down[group, level] = copy
        start[group] = start[group] + mine * half
        kept[group][level] = start[group]

    def double(group, level):
        half = rows >> (level + 1)
        part = pl.ds(pl.multiple_of(kept[group][level], half), half)
        copy = pltpu.make_async_remote_copy(
            src_ref=sum_ref.at[part],
            dst_ref=sum_ref.at[part],
            send_sem=out_sem.at[group, level],
            recv_sem=in_sem.at[group, level],
            device_id=partner(hop, core, orders[group][level]),
            device_id_type=MESH,
        )
        copy.start()
        up[group, level] = copy

    for group in range(groups):
        halve(group, 0)
    for level in range(levels):
        for group in range(groups):
            half = rows >> (level + 1)
            part = pl.ds(pl.multiple_of(kept[group][level], half), half)
            down[group, level].wait_recv()
            total = held[part] + inbox[group, pl.ds(places[level], half)]
            if level < levels - 1:
                held[part] = total
                halve(group, level + 1)
            else:
                sum_ref[part] = total
                double(group, level)
    for level in range(levels - 1, -1, -1):
        for group in range(groups):
            up[group, level].wait_recv()
            if level > 0:
                double(group, level - 1)
    for level in range(levels):
        for group in range(groups):
            down[group, level].wait_send()
            up[group, level].wait_send()


def sum_over_devices(part, hop_count):
    rows, columns = part.shape
    orders = halving_orders(hop_count, rows)
    groups, levels = len(orders), len(orders[0])
    semaphores = pltpu.SemaphoreType.DMA((groups, levels))
    return pl.pallas_call(
        functools.partial(sum_kernel, orders),
        name="weight_gradient_sum",
        out_shape=jax.ShapeDtypeStruct((rows, columns), part.dtype),
        in_specs=[pl.BlockSpec(memory_space=pltpu.VMEM)],
        out_specs=pl.BlockSpec(memory_space=pltpu.VMEM),
        scratch_shapes=[
            pltpu.VMEM((rows, columns), part.dtype),
            pltpu.VMEM((groups, rows // groups, columns), part.dtype),
            semaphores,
            semaphores,
            semaphores,
            semaphores,
        ],
        compiler_params=pltpu.CompilerParams(
            collective_id=0, has_side_effects=True, vmem_limit_bytes=48 << 20
        ),
    )(part)


def plain_body(
    child_feats,
    board_mask,
    importance,
    parent_slot,
    send_counts,
    parent_feats,
    proj_weight,
    q_weight,
    q_bias,
    w_weight,
    w_bias,
    emb_cotangent,
):
    slot_rows, feature_width = child_feats.shape
    hop_count = lax.axis_size("hop")
    par_count = lax.axis_size("par")
    shard_count = hop_count * par_count
    slot_cap = slot_rows // shard_count
    live_slots = (
        (jnp.arange(slot_cap)[None, :] < send_counts[0][:, None])
        .astype(jnp.float32)
        .reshape(slot_rows)
    )
    weight_live = importance * live_slots
    is_board = board_mask[:, None] == 1
    projected = jnp.dot(child_feats, proj_weight, preferred_element_type=jnp.float32)
    merged = jnp.where(is_board, projected, child_feats.astype(jnp.float32)).astype(jnp.bfloat16)
    pre_act = jnp.dot(merged, q_weight, preferred_element_type=jnp.float32) + q_bias
    message = (weight_live[:, None] * jax.nn.silu(pre_act)).astype(jnp.bfloat16)
    edge_info = jnp.stack([weight_live, parent_slot.astype(jnp.float32)]).reshape(
        2, shard_count, slot_cap
    )
    got_info = lax.all_to_all(edge_info, ("hop", "par"), split_axis=1, concat_axis=1, tiled=True)
    got_weight = got_info[0].reshape(slot_rows)
    got_slot = got_info[1].reshape(slot_rows).astype(jnp.int32)
    arrived = send_rows(message, hop_count, par_count, slot_cap, feature_width)
    parent_rows = parent_feats.shape[0]
    owner_table = got_slot[None, :] == jnp.arange(parent_rows, dtype=jnp.int32)[:, None]
    gathered = jnp.dot(
        owner_table.astype(jnp.bfloat16), arrived, preferred_element_type=jnp.float32
    )
    weight_sum = jnp.sum(jnp.where(owner_table, got_weight[None, :], 0.0), axis=1)
    divisor = jnp.maximum(weight_sum, 1.0)
    neighbor_mean = (gathered / divisor[:, None]).astype(jnp.bfloat16)
    joined = jnp.concatenate([parent_feats, neighbor_mean], axis=1)
    pre_norm = jnp.dot(joined, w_weight, preferred_element_type=jnp.float32) + w_bias
    act_out = jax.nn.silu(pre_norm)
    inv_norm = lax.rsqrt(jnp.sum(act_out * act_out, axis=1, keepdims=True) + 1e-06)
    embedding = act_out * inv_norm
    grad_emb = inv_norm * (
        emb_cotangent - embedding * jnp.sum(emb_cotangent * embedding, axis=1, keepdims=True)
    )
    grad_pre = (grad_emb * silu_slope(pre_norm)).astype(jnp.bfloat16)
    grad_w = contract_rows(joined, grad_pre)
    grad_wbias = jnp.sum(grad_pre.astype(jnp.float32), axis=0)
    grad_cat = times_transpose(grad_pre, w_weight)
    grad_parent = grad_cat[:, :feature_width]
    grad_mean = grad_cat[:, feature_width:] / divisor[:, None]
    return_rows = jnp.take(grad_mean, got_slot, axis=0).astype(jnp.bfloat16)
    grad_message = send_rows(return_rows, hop_count, par_count, slot_cap, feature_width)
    grad_act = weight_live[:, None] * grad_message.astype(jnp.float32)
    grad_preact = (grad_act * silu_slope(pre_act)).astype(jnp.bfloat16)
    grad_q = contract_rows(merged, grad_preact)
    grad_qbias = jnp.sum(grad_preact.astype(jnp.float32), axis=0)
    grad_merged = times_transpose(grad_preact, q_weight)
    grad_board = jnp.where(is_board, grad_merged, 0.0).astype(jnp.bfloat16)
    grad_proj = contract_rows(child_feats, grad_board)
    grad_child = (
        jnp.where(is_board, 0.0, grad_merged) + times_transpose(grad_board, proj_weight)
    ).astype(jnp.bfloat16)
    part = jnp.concatenate([grad_w, grad_q, grad_proj]).astype(jnp.bfloat16)
    summed = sum_over_devices(part, hop_count)
    summed = summed.astype(jnp.float32)
    grad_qbias, grad_wbias = lax.psum((grad_qbias, grad_wbias), ("hop", "par"))
    w_rows, q_rows = grad_w.shape[0], grad_q.shape[0]
    return (
        embedding,
        grad_child,
        grad_parent,
        summed[w_rows + q_rows :],
        summed[w_rows : w_rows + q_rows],
        grad_qbias,
        summed[:w_rows],
        grad_wbias,
    )


TILE = 512
BLOCK = 128


def columns(index, width=TILE):
    return pl.ds(pl.multiple_of(index * width, width), width)


def mm(left, right):
    return jnp.dot(left, right, preferred_element_type=jnp.float32)


def sigmoid(value):
    return 0.5 * jnp.tanh(0.5 * value) + 0.5


def spread(column, width):
    return jnp.concatenate([column] * (width // column.shape[1]), axis=1)


class Sums:
    def __init__(self, hop, core, groups, held, inbox, total, sems):
        self.hop, self.core, self.groups = hop, core, groups
        self.held, self.inbox, self.total = held, inbox, total
        self.send, self.recv, self.out, self.into, self.own = sems
        self.levels = len(groups[0][2])
        low, high = own_bit(hop, core, 2), own_bit(hop, core, 3)
        self.is_inner = low != high
        self.high = high
        place = 0
        self.plans = []
        for first, rows, order in groups:
            start, size, inner, steps = jnp.int32(first), rows, False, []
            for kind in order:
                if kind == "i":
                    step = (kind, start, start, size, place, inner)
                    inner = True
                else:
                    size //= 2
                    mine = high if kind == "m" else own_bit(hop, core, "cxypq".index(kind) - 1)
                    step = (kind, start + (1 - mine) * size, start + mine * size, size, place, inner)
                    start = start + mine * size
                    inner = inner or kind == "m"
                steps.append(step)
                place += size
            self.plans.append(steps)

    def other(self, kind):
        if kind == "m":
            return (self.hop + (1 - 2 * self.high) * 4, self.core)
        return partner(self.hop, self.core, "cxypq".index(kind.replace("i", "p")) - 1)

    def when(self, role, what):
        if role is None:
            what()
        else:
            pl.when(self.is_inner if role == "inner" else jnp.logical_not(self.is_inner))(what)

    def roles(self, group, level, upward):
        kind, _, _, _, _, inner = self.plans[group][level]
        if kind == "i":
            return ("inner", "outer") if upward else ("outer", "inner")
        role = "inner" if inner or kind == "m" else None
        return role, role

    def rows(self, start, size):
        return pl.ds(pl.multiple_of(start, size), size)

    def down(self, group, level):
        kind, away, _, size, place, _ = self.plans[group][level]
        return pltpu.make_async_remote_copy(
            src_ref=self.held.at[self.rows(away, size)],
            dst_ref=self.inbox.at[pl.ds(place, size)],
            send_sem=self.send.at[group, level],
            recv_sem=self.recv.at[group, level],
            device_id=self.other(kind),
            device_id_type=MESH,
        )

    def up(self, group, level):
        kind, _, kept, size, _, _ = self.plans[group][level]
        source = self.held if level == self.levels - 1 else self.total
        part = self.rows(kept, size)
        return pltpu.make_async_remote_copy(
            src_ref=source.at[part],
            dst_ref=self.total.at[part],
            send_sem=self.out.at[group, level],
            recv_sem=self.into.at[group, level],
            device_id=self.other(kind),
            device_id_type=MESH,
        )

    def own_copy(self, group):
        _, _, kept, size, _, _ = self.plans[group][-1]
        part = self.rows(kept, size)
        return pltpu.make_async_copy(self.held.at[part], self.total.at[part], self.own.at[group])

    def halve(self, group, level):
        self.when(self.roles(group, level, False)[0], lambda: self.down(group, level).start())

    def double(self, group, level):
        self.when(self.roles(group, level, True)[0], lambda: self.up(group, level).start())

    def fold(self, group, level):
        _, _, kept, size, place, _ = self.plans[group][level]

        def add():
            self.down(group, level).wait_recv()
            part = self.rows(kept, size)
            self.held[part] = self.held[part] + self.inbox[pl.ds(place, size)]
            if level == self.levels - 1:
                self.own_copy(group).start()
                self.up(group, level).start()

        self.when(self.roles(group, level, False)[1], add)
        if level < self.levels - 1:
            self.halve(group, level + 1)

    def gather(self, group, level):
        def take():
            if level == self.levels - 1:
                self.own_copy(group).wait()
            self.up(group, level).wait_recv()

        self.when(self.roles(group, level, True)[1], take)
        if level > 0:
            self.double(group, level - 1)

    def finish(self):
        for group in range(len(self.groups)):
            for level in range(self.levels):
                self.when(
                    self.roles(group, level, False)[0], lambda: self.down(group, level).wait_send()
                )
                self.when(self.roles(group, level, True)[0], lambda: self.up(group, level).wait_send())


def layer_kernel(
    groups,
    child_in,
    importance,
    board,
    slot,
    counts,
    parent_in,
    proj_in,
    q_in,
    q_bias,
    w_in,
    w_bias,
    cot_in,
    emb,
    message,
    parent,
    total,
    bias_out,
    child,
    proj,
    q,
    w,
    cot,
    merged,
    scaled_slope,
    arrived,
    moved,
    pre,
    table_rows,
    grad_pre,
    grad_moved,
    back_out,
    back_in,
    held,
    inbox,
    weight_col,
    board_col,
    shrink,
    slot_shrink,
    got_weight,
    got_slot,
    info_out,
    info_in,
    bias_held,
    bias_in,
    load_sem,
    info_sem,
    msg_sem,
    back_sem,
    bias_sem,
    sum_send,
    sum_recv,
    sum_out,
    sum_in,
    sum_own,
):
    hop, core = lax.axis_index("hop"), lax.axis_index("par")
    me = hop * 2 + core
    slots, width = child.shape
    parents = parent.shape[0]
    devices = counts.shape[1]
    cap = slots // devices
    half = slots // 2
    levels = bias_held.shape[0]
    tiles = width // TILE
    upper = own_bit(hop, core, levels - 2)
    sides = (1 - upper, upper)
    f32, bf16 = jnp.float32, jnp.bfloat16

    def other_hop(flips):
        to_hop = hop
        for bit in range(levels - 1):
            if (flips >> bit) & 1:
                to_hop = to_hop + (1 - 2 * own_bit(hop, core, bit)) * (1 << bit)
        return to_hop

    def targets(first, last):
        away = [(other_hop(flips), to_core) for to_core in range(2) for flips in range(last - 1, max(first, 1) - 1, -1)]
        return away + ([(hop, 1 - core)] if first == 0 else [])

    def rows_of(device):
        return pl.ds(pl.multiple_of(device * cap, cap), cap)

    def side_rows(side):
        return pl.ds(pl.multiple_of(side * half, half), half)

    loads = []
    for index, (source, place) in enumerate(
        ((child_in, child), (proj_in, proj), (q_in, q), (parent_in, parent), (w_in, w), (cot_in, cot))
    ):
        loads.append(pltpu.make_async_copy(source, place, load_sem.at[index]))
    for copy in loads[:3]:
        copy.start()

    barrier = pltpu.get_barrier_semaphore()
    for to in targets(0, devices // 2):
        pl.semaphore_signal(barrier, inc=1, device_id=to, device_id_type=MESH)

    lane = lax.broadcasted_iota(jnp.int32, (128, 128), 1)
    down = lax.broadcasted_iota(jnp.int32, (128, 128), 0)
    eye = lane == down
    place = lax.rem(down, cap)

    def column(row):
        return jnp.sum(jnp.where(eye, jnp.broadcast_to(row, (128, 128)), 0.0), axis=1, keepdims=True)

    count_row = counts[...].astype(f32)
    for part in range(slots // 128):
        owner = lax.broadcasted_iota(jnp.int32, (128, devices), 0) // cap + part * (128 // cap)
        is_owner = owner == lax.broadcasted_iota(jnp.int32, (128, devices), 1)
        live = jnp.sum(
            jnp.where(is_owner, jnp.broadcast_to(count_row, (128, devices)), 0.0), axis=1, keepdims=True
        )
        weight = jnp.broadcast_to(column(importance[part : part + 1, :]), (128, 128))
        weight = jnp.where(place.astype(f32) < live, weight, 0.0)
        slot_at = jnp.broadcast_to(column(slot[part : part + 1, :].astype(f32)), (128, 128))
        at = slice(part * 128, (part + 1) * 128)
        weight_col[at, :] = weight
        board_col[at, :] = jnp.broadcast_to(column(board[part : part + 1, :].astype(f32)), (128, 128))
        info = jnp.where(lane == place, weight, 0.0) + jnp.where(lane == place + cap, slot_at, 0.0)
        for owner_at in range(128 // cap):
            info_out[part * (128 // cap) + owner_at] = jnp.sum(
                info[owner_at * cap : (owner_at + 1) * cap, :], axis=0, keepdims=True
            )

    def send_info():
        pl.semaphore_wait(barrier, devices - 1)

        for to_hop, to_core in targets(0, devices // 2):
            pltpu.make_async_remote_copy(
                src_ref=info_out.at[to_hop * 2 + to_core],
                dst_ref=info_in.at[me],
                send_sem=info_sem.at[0],
                recv_sem=info_sem.at[1],
                device_id=(to_hop, to_core),
                device_id_type=MESH,
            ).start()
        pltpu.make_async_copy(info_out.at[me], info_in.at[me], info_sem.at[1]).start()

    def send_side(source, place_ref, sem, side_index):
        quarter = devices // 4
        for to_hop, to_core in targets(quarter, 2 * quarter) if side_index == 0 else targets(0, quarter):
            pltpu.make_async_remote_copy(
                src_ref=source.at[rows_of(to_hop * 2 + to_core)],
                dst_ref=place_ref.at[rows_of(me)],
                send_sem=sem.at[0, side_index],
                recv_sem=sem.at[1, side_index],
                device_id=(to_hop, to_core),
                device_id_type=MESH,
            ).start()
        if side_index == 1:
            pltpu.make_async_copy(
                source.at[rows_of(me)], place_ref.at[rows_of(me)], sem.at[1, side_index]
            ).start()

    def wait_side(place_ref, sem, side_index):
        rows = side_rows(sides[side_index])
        pltpu.make_async_copy(place_ref.at[rows], place_ref.at[rows], sem.at[1, side_index]).wait()

    def wait_sent(source, sem):
        for side_index, rows in ((0, half), (1, half - cap)):
            part = source.at[pl.ds(0, rows)]
            pltpu.make_async_copy(part, part, sem.at[0, side_index]).wait()

    loads[0].wait()
    loads[1].wait()
    for side_index, side in enumerate(sides):
        rows = side_rows(side)
        boards = spread(board_col[rows, :], TILE) == 1.0

        @pl.loop(0, tiles)
        def _(tile):
            projected = mm(child[rows, :], proj[:, columns(tile)])
            raw = child[rows, columns(tile)]
            merged[rows, columns(tile)] = jnp.where(boards, projected, raw.astype(f32)).astype(bf16)

        if side_index == 0:
            loads[2].wait()
            for copy in loads[3:]:
                copy.start()
        weights = spread(weight_col[rows, :], TILE)

        @pl.loop(0, tiles)
        def _(tile):
            value = mm(merged[rows, :], q[:, columns(tile)]) + q_bias[:, columns(tile)]
            gate = sigmoid(value)
            act = value * gate
            message[rows, columns(tile)] = (weights * act).astype(bf16)
            scaled_slope[rows, columns(tile)] = weights * (gate + act * (1.0 - gate))

        if side_index == 0:
            send_info()
        send_side(message, arrived, msg_sem, side_index)

    loads[3].wait()
    loads[4].wait()

    @pl.loop(0, tiles)
    def _(tile):
        pre[:, columns(tile)] = mm(parent[...], w[pl.ds(0, width), columns(tile)]) + w_bias[:, columns(tile)]

    info_all = pltpu.make_async_copy(info_in, info_in, info_sem.at[1])
    info_all.wait()
    lane16 = lax.broadcasted_iota(jnp.int32, (cap, 128), 1)
    down16 = lax.broadcasted_iota(jnp.int32, (cap, 128), 0)
    for device in range(devices):
        got = jnp.broadcast_to(info_in[device], (cap, 128))
        at = slice(device * cap, (device + 1) * cap)
        got_weight[at, :] = jnp.broadcast_to(
            jnp.sum(jnp.where(lane16 == down16, got, 0.0), axis=1, keepdims=True), (cap, 128)
        )
        got_slot[at, :] = jnp.broadcast_to(
            jnp.sum(jnp.where(lane16 == down16 + cap, got, 0.0), axis=1, keepdims=True), (cap, 128)
        )

    for part in range(parents // 128):
        want = (lax.broadcasted_iota(jnp.int32, (128, 128), 1) + part * 128).astype(f32)
        weight_sum = jnp.zeros((1, 128), f32)
        for block in range(slots // 128):
            at = slice(block * 128, (block + 1) * 128)
            hit = got_slot[at, :] == want
            table_rows[at, part * 128 : (part + 1) * 128] = jnp.where(hit, 1.0, 0.0).astype(bf16)
            weight_sum = weight_sum + jnp.sum(jnp.where(hit, got_weight[at, :], 0.0), axis=0, keepdims=True)
        inverse = 1.0 / jnp.maximum(weight_sum, 1.0)
        shrink[part * 128 : (part + 1) * 128, :] = jnp.broadcast_to(column(inverse), (128, 128))
        for block in range(slots // 128):
            at = slice(block * 128, (block + 1) * 128)
            hit = got_slot[at, :] == want
            term = jnp.where(hit, jnp.broadcast_to(inverse, (128, 128)), 0.0)
            if part == 0:
                slot_shrink[at, :] = term
            else:
                slot_shrink[at, :] = slot_shrink[at, :] + term
    for block in range(slots // 128):
        at = slice(block * 128, (block + 1) * 128)
        slot_shrink[at, :] = jnp.broadcast_to(
            jnp.sum(slot_shrink[at, :], axis=1, keepdims=True), (128, 128)
        )

    def add_messages(side_index):
        rows = side_rows(sides[side_index])

        @pl.loop(0, tiles)
        def _(tile):
            moved[rows, columns(tile)] = mm(arrived[rows, :], w[pl.ds(width, width), columns(tile)]).astype(bf16)

        @pl.loop(0, tiles)
        def _(tile):
            pre[:, columns(tile)] = pre[:, columns(tile)] + spread(shrink[...], TILE) * contract_rows(
                table_rows[rows, :], moved[rows, columns(tile)]
            )

    wait_side(arrived, msg_sem, 1)
    add_messages(1)
    loads[5].wait()
    wait_side(arrived, msg_sem, 0)
    add_messages(0)

    @pl.loop(0, parents // BLOCK)
    def _(block):
        at = columns(block, BLOCK)
        value = pre[at, :]
        turn = cot[at, :]
        gate = sigmoid(value)
        act = value * gate
        inv = lax.rsqrt(jnp.sum(act * act, axis=1, keepdims=True) + 1e-06)
        share = jnp.sum(turn * act, axis=1, keepdims=True) * (inv * inv * inv)
        emb[at, :] = (act * inv).astype(bf16)
        grad_pre[at, :] = ((turn * inv - act * share) * (gate + act * (1.0 - gate))).astype(bf16)

    for side_index, side in enumerate(sides):
        rows = side_rows(side)
        shrinks = spread(slot_shrink[rows, :], TILE)

        @pl.loop(0, tiles)
        def _(tile):
            grad_moved[rows, columns(tile)] = (
                shrinks * mm(table_rows[rows, :], grad_pre[:, columns(tile)])
            ).astype(bf16)

        @pl.loop(0, tiles)
        def _(tile):
            turned = w[pl.ds(pl.multiple_of(width + tile * TILE, TILE), TILE), :]
            back_out[rows, columns(tile)] = times_transpose(grad_moved[rows, :], turned).astype(bf16)

        send_side(back_out, back_in, back_sem, side_index)

    sums = Sums(hop, core, groups, held, inbox, total, (sum_send, sum_recv, sum_out, sum_in, sum_own))
    w_groups = [g for g, (first, _, _) in enumerate(groups) if first < 2 * width]
    q_groups = [g for g, (first, _, _) in enumerate(groups) if 2 * width <= first < 3 * width]
    p_groups = [g for g, (first, _, _) in enumerate(groups) if first >= 3 * width]

    @pl.loop(0, tiles)
    def _(tile):
        held[pl.ds(0, width), columns(tile)] = contract_rows(parent[...], grad_pre[:, columns(tile)]).astype(bf16)

    for group in w_groups[: len(w_groups) // 2]:
        sums.halve(group, 0)

    @pl.loop(0, tiles)
    def _(tile):
        held[pl.ds(width, width), columns(tile)] = contract_rows(
            arrived[...], grad_moved[:, columns(tile)]
        ).astype(bf16)

    for group in w_groups[len(w_groups) // 2 :]:
        sums.halve(group, 0)
    bias_held[0, 0:1, :] = mm(jnp.ones((16, parents), bf16), grad_pre[...])[0:1, :]

    def parent_gradient():
        @pl.loop(0, tiles)
        def _(tile):
            parent[:, columns(tile)] = times_transpose(grad_pre[...], w[columns(tile), :]).astype(bf16)

        wait_sent(message, msg_sem)

    def child_front(side_index):
        rows = side_rows(sides[side_index])

        @pl.loop(0, tiles)
        def _(tile):
            grad_moved[rows, columns(tile)] = (
                scaled_slope[rows, columns(tile)] * back_in[rows, columns(tile)].astype(f32)
            ).astype(bf16)

    def weight_sums(side_index, left, grads, partial, base):
        rows = side_rows(sides[side_index])

        @pl.loop(0, tiles)
        def _(tile):
            value = contract_rows(left[rows, :], grads[rows, columns(tile)])
            if side_index == 1:
                partial[:, columns(tile)] = value
            else:
                held[pl.ds(base, width), columns(tile)] = (value + partial[:, columns(tile)]).astype(bf16)

    def child_middle(side_index):
        rows = side_rows(sides[side_index])
        boards = spread(board_col[rows, :], TILE) == 1.0

        @pl.loop(0, tiles)
        def _(tile):
            value = times_transpose(grad_moved[rows, :], q[columns(tile), :])
            moved[rows, columns(tile)] = jnp.where(boards, value, 0.0).astype(bf16)
            scaled_slope[rows, columns(tile)] = jnp.where(boards, 0.0, value)

    def child_end(side_index):
        rows = side_rows(sides[side_index])

        @pl.loop(0, tiles)
        def _(tile):
            value = times_transpose(moved[rows, :], proj[columns(tile), :])
            message[rows, columns(tile)] = (scaled_slope[rows, columns(tile)] + value).astype(bf16)

    bias_copies = []

    def send_bias(level):
        copy = pltpu.make_async_remote_copy(
            src_ref=bias_held.at[level],
            dst_ref=bias_in.at[level],
            send_sem=bias_sem.at[0, level],
            recv_sem=bias_sem.at[1, level],
            device_id=partner(hop, core, level - 1),
            device_id_type=MESH,
        )
        copy.start()
        bias_copies.append(copy)

    def fold_bias(level):
        bias_copies[level].wait_recv()
        both = bias_held[level] + bias_in[level]
        if level < levels - 1:
            bias_held[level + 1] = both
            send_bias(level + 1)
        else:
            bias_out[...] = both

    def near_children():
        child_front(1)
        weight_sums(1, merged, grad_moved, pre, 2 * width)
        child_middle(1)
        weight_sums(1, child, moved, cot, 3 * width)
        child_end(1)

    def far_q():
        child_front(0)
        weight_sums(0, merged, grad_moved, pre, 2 * width)

    def far_p():
        child_middle(0)
        weight_sums(0, child, moved, cot, 3 * width)

    def send_q():
        for group in q_groups:
            sums.halve(group, 0)
        bias_held[0, 1:2, :] = mm(jnp.ones((16, slots), bf16), grad_moved[...])[0:1, :]
        send_bias(0)

    def far_end():
        child_end(0)

    main = [
        parent_gradient,
        lambda: wait_side(back_in, back_sem, 1),
        near_children,
        lambda: wait_side(back_in, back_sem, 0),
        far_q,
        send_q,
        far_p,
        lambda: [sums.halve(group, 0) for group in p_groups],
        far_end,
    ]
    done = [0] * (len(groups) + 1)
    for turn in SCHEDULE:
        at = done[turn]
        done[turn] += 1
        if turn == 0:
            main[at]()
        elif at < sums.levels:
            sums.fold(turn - 1, at)
            if turn - 1 == q_groups[0]:
                fold_bias(at)
        else:
            sums.gather(turn - 1, 2 * sums.levels - 1 - at)

    sums.finish()
    for copy in bias_copies:
        copy.wait_send()
    wait_sent(back_out, back_sem)
    sent = info_out.at[pl.ds(0, devices - 1)]
    pltpu.make_async_copy(sent, sent, info_sem.at[0]).wait()


GROUPS = [("cxyim", 2), ("cyxim", 2), ("cxyim", 2), ("cyxim", 2), ("cxyim", 4), ("cyxim", 4), ("cxyim", 4), ("cyxim", 4), ("cxyim", 4), ("cyxim", 4), ("cxyim", 4), ("cyxim", 4)]
SCHEDULE = [
    3, 4, 0, 1, 2, 0, 0, 3, 4, 0, 0, 0, 1, 2, 3, 4, 0, 5, 6, 0, 11, 12, 9, 10, 3, 4, 0, 1, 2, 7, 8, 3, 4, 5, 6, 1,
    2, 11, 12, 3, 4, 9, 10, 5, 6, 1, 2, 7, 8, 11, 12, 3, 4, 9, 10, 7, 8, 5, 6, 1, 2, 3, 4, 11, 12, 1, 2, 9, 10, 5, 6, 7,
    8, 5, 6, 11, 12, 1, 2, 5, 6, 9, 10, 11, 12, 7, 8, 9, 10, 11, 12, 3, 4, 9, 10, 7, 8, 7, 8, 5, 6, 11, 12, 1, 2, 9, 10, 5,
    6, 7, 8, 3, 4, 11, 12, 9, 10, 7, 8, 5, 6, 1, 2, 11, 12, 9, 10, 7, 8,
]


def sum_groups(width):
    groups, first = [], 0
    for order, share in GROUPS:
        groups.append((first, width // share, order))
        first += width // share
    return groups


def inbox_rows(groups):
    total = 0
    for _, size, order in groups:
        for kind in order:
            size = size if kind == "i" else size // 2
            total += size
    return total


def widen_kernel(
    emb,
    child,
    parent,
    total,
    biases,
    emb_out,
    child_out,
    parent_out,
    proj_out,
    q_out,
    q_bias_out,
    w_out,
    w_bias_out,
    narrow,
    wide,
    read_sem,
    write_sem,
    child_sem,
):
    slots, rows, width = narrow.shape
    through = pltpu.make_async_copy(child, child_out, child_sem)
    pieces = []
    for source, place in ((parent, parent_out), (emb, emb_out)):
        for first in range(0, place.shape[0], rows):
            pieces.append((source, first, place, first))
    base = 0
    for place in (w_out, q_out, proj_out):
        for first in range(0, place.shape[0], rows):
            pieces.append((total, base + first, place, first))
        base += place.shape[0]
    near = [True for source, _, _, _ in pieces]

    def read(index):
        source, first, _, _ = pieces[index]
        slot = index % slots
        return pltpu.make_async_copy(source.at[pl.ds(first, rows)], narrow.at[slot], read_sem.at[slot])

    def write(index):
        _, _, place, first = pieces[index]
        slot = index % slots
        return pltpu.make_async_copy(wide.at[slot], place.at[pl.ds(first, rows)], write_sem.at[slot])

    far = [index for index in range(len(pieces)) if not near[index]]
    for index in far[:slots]:
        read(index).start()
    for index in range(len(pieces)):
        source, first, _, _ = pieces[index]
        if index >= slots:
            write(index - slots).wait()
        if near[index]:
            value = source[first : first + rows, :]
        else:
            read(index).wait()
            value = narrow[index % slots]
        wide[index % slots] = value.astype(jnp.float32)
        write(index).start()
        if not near[index] and index + slots < len(pieces):
            read(index + slots).start()
    through.start()
    w_bias_out[...] = biases[0, :]
    q_bias_out[...] = biases[1, :]
    for index in range(len(pieces) - slots, len(pieces)):
        write(index).wait()
    through.wait()


def widen(emb, child, parent, total, biases):
    width = emb.shape[1]
    slots, rows = 4, 512
    shape, f32 = jax.ShapeDtypeStruct, jnp.float32
    hbm = pl.BlockSpec(memory_space=pl.ANY)
    vmem = pl.BlockSpec(memory_space=pltpu.VMEM)
    return pl.pallas_call(
        widen_kernel,
        name="widen",
        out_shape=(
            shape(emb.shape, f32),
            shape(child.shape, child.dtype),
            shape(parent.shape, f32),
            shape((width, width), f32),
            shape((width, width), f32),
            shape((width,), f32),
            shape((2 * width, width), f32),
            shape((width,), f32),
        ),
        in_specs=[vmem, vmem, vmem, vmem, vmem],
        out_specs=(hbm, hbm, hbm, hbm, hbm, vmem, hbm, vmem),
        scratch_shapes=[
            pltpu.VMEM((slots, rows, width), child.dtype),
            pltpu.VMEM((slots, rows, width), f32),
            pltpu.SemaphoreType.DMA((slots,)),
            pltpu.SemaphoreType.DMA((slots,)),
            pltpu.SemaphoreType.DMA,
        ],
        compiler_params=pltpu.CompilerParams(vmem_limit_bytes=36 << 20),
    )(emb, child, parent, total, biases)


def fused_body(
    child_feats,
    board_mask,
    importance,
    parent_slot,
    send_counts,
    parent_feats,
    proj_weight,
    q_weight,
    q_bias,
    w_weight,
    w_bias,
    emb_cotangent,
):
    slots, width = child_feats.shape
    parents = parent_feats.shape[0]
    devices = send_counts.shape[1]
    groups = sum_groups(width)
    levels = devices.bit_length() - 1
    f32, bf16 = jnp.float32, jnp.bfloat16
    vmem = pl.BlockSpec(memory_space=pltpu.VMEM)
    hbm = pl.BlockSpec(memory_space=pl.ANY)
    dma = pltpu.SemaphoreType.DMA
    shape = jax.ShapeDtypeStruct
    emb, grad_child, grad_parent, total, biases = pl.pallas_call(
        functools.partial(layer_kernel, groups),
        name="layer",
        out_shape=(
            pltpu.VMEM((parents, width), bf16),
            pltpu.VMEM((slots, width), bf16),
            pltpu.VMEM((parents, width), bf16),
            pltpu.VMEM((4 * width, width), bf16),
            shape((2, width), f32),
        ),
        in_specs=[hbm, vmem, vmem, vmem, vmem, hbm, hbm, hbm, vmem, hbm, vmem, hbm],
        out_specs=(vmem, vmem, vmem, vmem, vmem),
        scratch_shapes=[
            pltpu.VMEM((slots, width), bf16),
            pltpu.VMEM((width, width), bf16),
            pltpu.VMEM((width, width), bf16),
            pltpu.VMEM((2 * width, width), bf16),
            pltpu.VMEM((parents, width), f32),
            pltpu.VMEM((slots, width), bf16),
            pltpu.VMEM((slots, width), f32),
            pltpu.VMEM((slots, width), bf16),
            pltpu.VMEM((slots, width), bf16),
            pltpu.VMEM((parents, width), f32),
            pltpu.VMEM((slots, parents), bf16),
            pltpu.VMEM((parents, width), bf16),
            pltpu.VMEM((slots, width), bf16),
            pltpu.VMEM((slots, width), bf16),
            pltpu.VMEM((slots, width), bf16),
            pltpu.VMEM((4 * width, width), bf16),
            pltpu.VMEM((inbox_rows(groups), width), bf16),
            pltpu.VMEM((slots, 128), f32),
            pltpu.VMEM((slots, 128), f32),
            pltpu.VMEM((parents, 128), f32),
            pltpu.VMEM((slots, 128), f32),
            pltpu.VMEM((slots, 128), f32),
            pltpu.VMEM((slots, 128), f32),
            pltpu.VMEM((devices, 1, 128), f32),
            pltpu.VMEM((devices, 1, 128), f32),
            pltpu.VMEM((levels, 2, width), f32),
            pltpu.VMEM((levels, 2, width), f32),
            dma((6,)),
            dma((2,)),
            dma((2, 2)),
            dma((2, 2)),
            dma((2, levels)),
        ]
        + [dma((len(groups), len(groups[0][2])))] * 4
        + [dma((len(groups),))],
        compiler_params=pltpu.CompilerParams(
            collective_id=1, has_side_effects=True, vmem_limit_bytes=50 << 20
        ),
        cost_estimate=pl.CostEstimate(
            flops=36 * slots * width * width, bytes_accessed=40 << 20, transcendentals=3 * parents * width
        ),
    )(
        child_feats,
        importance.reshape(-1, 128),
        board_mask.reshape(-1, 128),
        parent_slot.reshape(-1, 128),
        send_counts,
        parent_feats,
        proj_weight,
        q_weight,
        q_bias.reshape(1, -1),
        w_weight,
        w_bias.reshape(1, -1),
        emb_cotangent,
    )
    return widen(emb, grad_child, grad_parent, total, biases)


def solution(mesh):
    rows = P(("hop", "par"), None)
    flat = P(("hop", "par"))
    fused = mesh.shape["hop"] == 16 and mesh.shape["par"] == 2
    return jax.shard_map(
        fused_body if fused else plain_body,
        mesh=mesh,
        in_specs=(rows, flat, flat, flat, rows, rows, P(), P(), P(), P(), P(), rows),
        out_specs=(rows, rows, rows, P(), P(), P(), P(), P()),
        check_vma=False,
    )
```

```python
import functools

import jax
import jax.numpy as jnp
from jax import lax
from jax.experimental import pallas as pl
from jax.experimental.pallas import tpu as pltpu
from jax.sharding import PartitionSpec as P

MESH = pl.DeviceIdType.MESH
CORE = -1


def times_transpose(left, right):
    return lax.dot_general(
        left, right, (((1,), (1,)), ((), ())), preferred_element_type=jnp.float32
    )


def contract_rows(left, right):
    return lax.dot_general(
        left, right, (((0,), (0,)), ((), ())), preferred_element_type=jnp.float32
    )


def silu_slope(value):
    sigma = jax.nn.sigmoid(value)
    return sigma * (1.0 + value * (1.0 - sigma))


def send_rows(payload, hop_count, par_count, slot_cap, feature_width):
    parcel = payload.reshape(hop_count * par_count, slot_cap, feature_width)
    arrived = lax.all_to_all(parcel, ("hop", "par"), split_axis=0, concat_axis=0, tiled=True)
    return arrived.reshape(payload.shape)


def halving_orders(hop_count, rows):
    bits = hop_count.bit_length() - 1
    if bits == 4:
        x, y, z0, z1 = range(4)
        base = [[x, y, z0, z1], [y, x, z0, z1], [z0, x, y, z1], [x, y, z0, z1]]
        base += [[y, x, z0, z1], [z0, y, x, z1], [x, y, z0, z1], [y, x, z0, z1]]
    else:
        base = [[(first + k) % bits for k in range(bits)] for first in range(0, bits, 2)]
    groups = 1
    while groups * 2 <= len(base) and rows // (groups * 2) // (hop_count * 2) >= 16:
        groups *= 2
    return [[CORE] + order for order in base[:groups]]


def own_bit(hop, core, bit):
    return core if bit == CORE else lax.rem(hop // (1 << bit), 2)


def partner(hop, core, bit):
    if bit == CORE:
        return (hop, 1 - core)
    return (hop + (1 - 2 * own_bit(hop, core, bit)) * (1 << bit), core)


def sum_kernel(orders, part_ref, sum_ref, held, inbox, send_sem, recv_sem, out_sem, in_sem):
    hop, core = lax.axis_index("hop"), lax.axis_index("par")
    groups, levels = len(orders), len(orders[0])
    rows = part_ref.shape[0] // groups
    barrier = pltpu.get_barrier_semaphore()
    for bit in range(CORE, levels - 1):
        pl.semaphore_signal(barrier, inc=1, device_id=partner(hop, core, bit), device_id_type=MESH)
    held[...] = part_ref[...]
    pl.semaphore_wait(barrier, levels)

    start = [jnp.int32(group * rows) for group in range(groups)]
    kept = [[None] * levels for _ in range(groups)]
    places = [rows - (rows >> level) for level in range(levels)]
    down, up = {}, {}

    def halve(group, level):
        bit = orders[group][level]
        half = rows >> (level + 1)
        mine = own_bit(hop, core, bit)
        away = pl.multiple_of(start[group] + (1 - mine) * half, half)
        copy = pltpu.make_async_remote_copy(
            src_ref=held.at[pl.ds(away, half)],
            dst_ref=inbox.at[group, pl.ds(places[level], half)],
            send_sem=send_sem.at[group, level],
            recv_sem=recv_sem.at[group, level],
            device_id=partner(hop, core, bit),
            device_id_type=MESH,
        )
        copy.start()
        down[group, level] = copy
        start[group] = start[group] + mine * half
        kept[group][level] = start[group]

    def double(group, level):
        half = rows >> (level + 1)
        part = pl.ds(pl.multiple_of(kept[group][level], half), half)
        copy = pltpu.make_async_remote_copy(
            src_ref=sum_ref.at[part],
            dst_ref=sum_ref.at[part],
            send_sem=out_sem.at[group, level],
            recv_sem=in_sem.at[group, level],
            device_id=partner(hop, core, orders[group][level]),
            device_id_type=MESH,
        )
        copy.start()
        up[group, level] = copy

    for group in range(groups):
        halve(group, 0)
    for level in range(levels):
        for group in range(groups):
            half = rows >> (level + 1)
            part = pl.ds(pl.multiple_of(kept[group][level], half), half)
            down[group, level].wait_recv()
            total = held[part] + inbox[group, pl.ds(places[level], half)]
            if level < levels - 1:
                held[part] = total
                halve(group, level + 1)
            else:
                sum_ref[part] = total
                double(group, level)
    for level in range(levels - 1, -1, -1):
        for group in range(groups):
            up[group, level].wait_recv()
            if level > 0:
                double(group, level - 1)
    for level in range(levels):
        for group in range(groups):
            down[group, level].wait_send()
            up[group, level].wait_send()


def sum_over_devices(part, hop_count):
    rows, columns = part.shape
    orders = halving_orders(hop_count, rows)
    groups, levels = len(orders), len(orders[0])
    semaphores = pltpu.SemaphoreType.DMA((groups, levels))
    return pl.pallas_call(
        functools.partial(sum_kernel, orders),
        name="weight_gradient_sum",
        out_shape=jax.ShapeDtypeStruct((rows, columns), part.dtype),
        in_specs=[pl.BlockSpec(memory_space=pltpu.VMEM)],
        out_specs=pl.BlockSpec(memory_space=pltpu.VMEM),
        scratch_shapes=[
            pltpu.VMEM((rows, columns), part.dtype),
            pltpu.VMEM((groups, rows // groups, columns), part.dtype),
            semaphores,
            semaphores,
            semaphores,
            semaphores,
        ],
        compiler_params=pltpu.CompilerParams(
            collective_id=0, has_side_effects=True, vmem_limit_bytes=48 << 20
        ),
    )(part)


def plain_body(
    child_feats,
    board_mask,
    importance,
    parent_slot,
    send_counts,
    parent_feats,
    proj_weight,
    q_weight,
    q_bias,
    w_weight,
    w_bias,
    emb_cotangent,
):
    slot_rows, feature_width = child_feats.shape
    hop_count = lax.axis_size("hop")
    par_count = lax.axis_size("par")
    shard_count = hop_count * par_count
    slot_cap = slot_rows // shard_count
    live_slots = (
        (jnp.arange(slot_cap)[None, :] < send_counts[0][:, None])
        .astype(jnp.float32)
        .reshape(slot_rows)
    )
    weight_live = importance * live_slots
    is_board = board_mask[:, None] == 1
    projected = jnp.dot(child_feats, proj_weight, preferred_element_type=jnp.float32)
    merged = jnp.where(is_board, projected, child_feats.astype(jnp.float32)).astype(jnp.bfloat16)
    pre_act = jnp.dot(merged, q_weight, preferred_element_type=jnp.float32) + q_bias
    message = (weight_live[:, None] * jax.nn.silu(pre_act)).astype(jnp.bfloat16)
    edge_info = jnp.stack([weight_live, parent_slot.astype(jnp.float32)]).reshape(
        2, shard_count, slot_cap
    )
    got_info = lax.all_to_all(edge_info, ("hop", "par"), split_axis=1, concat_axis=1, tiled=True)
    got_weight = got_info[0].reshape(slot_rows)
    got_slot = got_info[1].reshape(slot_rows).astype(jnp.int32)
    arrived = send_rows(message, hop_count, par_count, slot_cap, feature_width)
    parent_rows = parent_feats.shape[0]
    owner_table = got_slot[None, :] == jnp.arange(parent_rows, dtype=jnp.int32)[:, None]
    gathered = jnp.dot(
        owner_table.astype(jnp.bfloat16), arrived, preferred_element_type=jnp.float32
    )
    weight_sum = jnp.sum(jnp.where(owner_table, got_weight[None, :], 0.0), axis=1)
    divisor = jnp.maximum(weight_sum, 1.0)
    neighbor_mean = (gathered / divisor[:, None]).astype(jnp.bfloat16)
    joined = jnp.concatenate([parent_feats, neighbor_mean], axis=1)
    pre_norm = jnp.dot(joined, w_weight, preferred_element_type=jnp.float32) + w_bias
    act_out = jax.nn.silu(pre_norm)
    inv_norm = lax.rsqrt(jnp.sum(act_out * act_out, axis=1, keepdims=True) + 1e-06)
    embedding = act_out * inv_norm
    grad_emb = inv_norm * (
        emb_cotangent - embedding * jnp.sum(emb_cotangent * embedding, axis=1, keepdims=True)
    )
    grad_pre = (grad_emb * silu_slope(pre_norm)).astype(jnp.bfloat16)
    grad_w = contract_rows(joined, grad_pre)
    grad_wbias = jnp.sum(grad_pre.astype(jnp.float32), axis=0)
    grad_cat = times_transpose(grad_pre, w_weight)
    grad_parent = grad_cat[:, :feature_width]
    grad_mean = grad_cat[:, feature_width:] / divisor[:, None]
    return_rows = jnp.take(grad_mean, got_slot, axis=0).astype(jnp.bfloat16)
    grad_message = send_rows(return_rows, hop_count, par_count, slot_cap, feature_width)
    grad_act = weight_live[:, None] * grad_message.astype(jnp.float32)
    grad_preact = (grad_act * silu_slope(pre_act)).astype(jnp.bfloat16)
    grad_q = contract_rows(merged, grad_preact)
    grad_qbias = jnp.sum(grad_preact.astype(jnp.float32), axis=0)
    grad_merged = times_transpose(grad_preact, q_weight)
    grad_board = jnp.where(is_board, grad_merged, 0.0).astype(jnp.bfloat16)
    grad_proj = contract_rows(child_feats, grad_board)
    grad_child = (
        jnp.where(is_board, 0.0, grad_merged) + times_transpose(grad_board, proj_weight)
    ).astype(jnp.bfloat16)
    part = jnp.concatenate([grad_w, grad_q, grad_proj]).astype(jnp.bfloat16)
    summed = sum_over_devices(part, hop_count)
    summed = summed.astype(jnp.float32)
    grad_qbias, grad_wbias = lax.psum((grad_qbias, grad_wbias), ("hop", "par"))
    w_rows, q_rows = grad_w.shape[0], grad_q.shape[0]
    return (
        embedding,
        grad_child,
        grad_parent,
        summed[w_rows + q_rows :],
        summed[w_rows : w_rows + q_rows],
        grad_qbias,
        summed[:w_rows],
        grad_wbias,
    )


TILE = 512
BLOCK = 128


def columns(index, width=TILE):
    return pl.ds(pl.multiple_of(index * width, width), width)


def mm(left, right):
    return jnp.dot(left, right, preferred_element_type=jnp.float32)


def sigmoid(value):
    return 0.5 * jnp.tanh(0.5 * value) + 0.5


def spread(column, width):
    return jnp.concatenate([column] * (width // column.shape[1]), axis=1)


class Sums:
    def __init__(self, hop, core, groups, held, inbox, total, sems):
        self.hop, self.core, self.groups = hop, core, groups
        self.held, self.inbox, self.total = held, inbox, total
        self.send, self.recv, self.out, self.into = sems
        self.levels = len(groups[0][2])
        low, high = own_bit(hop, core, 2), own_bit(hop, core, 3)
        self.is_inner = low != high
        self.high = high
        place = 0
        self.plans = []
        for first, rows, order in groups:
            start, size, inner, steps = jnp.int32(first), rows, False, []
            for kind in order:
                if kind == "i":
                    step = (kind, start, start, size, place, inner)
                    inner = True
                else:
                    size //= 2
                    mine = high if kind == "m" else own_bit(hop, core, "cxypq".index(kind) - 1)
                    step = (kind, start + (1 - mine) * size, start + mine * size, size, place, inner)
                    start = start + mine * size
                    inner = inner or kind == "m"
                steps.append(step)
                place += size
            self.plans.append(steps)

    def other(self, kind):
        if kind == "m":
            return (self.hop + (1 - 2 * self.high) * 4, self.core)
        return partner(self.hop, self.core, "cxypq".index(kind.replace("i", "p")) - 1)

    def when(self, role, what):
        if role is None:
            what()
        else:
            pl.when(self.is_inner if role == "inner" else jnp.logical_not(self.is_inner))(what)

    def roles(self, group, level, upward):
        kind, _, _, _, _, inner = self.plans[group][level]
        if kind == "i":
            return ("inner", "outer") if upward else ("outer", "inner")
        role = "inner" if inner or kind == "m" else None
        return role, role

    def rows(self, start, size):
        return pl.ds(pl.multiple_of(start, size), size)

    def down(self, group, level):
        kind, away, _, size, place, _ = self.plans[group][level]
        return pltpu.make_async_remote_copy(
            src_ref=self.held.at[self.rows(away, size)],
            dst_ref=self.inbox.at[pl.ds(place, size)],
            send_sem=self.send.at[group, level],
            recv_sem=self.recv.at[group, level],
            device_id=self.other(kind),
            device_id_type=MESH,
        )

    def up(self, group, level):
        kind, _, kept, size, _, _ = self.plans[group][level]
        part = self.rows(kept, size)
        return pltpu.make_async_remote_copy(
            src_ref=self.total.at[part],
            dst_ref=self.total.at[part],
            send_sem=self.out.at[group, level],
            recv_sem=self.into.at[group, level],
            device_id=self.other(kind),
            device_id_type=MESH,
        )

    def halve(self, group, level):
        self.when(self.roles(group, level, False)[0], lambda: self.down(group, level).start())

    def double(self, group, level):
        self.when(self.roles(group, level, True)[0], lambda: self.up(group, level).start())

    def fold(self, group, level):
        _, _, kept, size, place, _ = self.plans[group][level]

        def add():
            self.down(group, level).wait_recv()
            part = self.rows(kept, size)
            done = self.total if level == self.levels - 1 else self.held
            done[part] = self.held[part] + self.inbox[pl.ds(place, size)]
            if level == self.levels - 1:
                self.up(group, level).start()

        self.when(self.roles(group, level, False)[1], add)
        if level < self.levels - 1:
            self.halve(group, level + 1)

    def gather(self, group, level):
        self.when(self.roles(group, level, True)[1], lambda: self.up(group, level).wait_recv())
        if level > 0:
            self.double(group, level - 1)

    def finish(self):
        for group in range(len(self.groups)):
            for level in range(self.levels):
                self.when(
                    self.roles(group, level, False)[0], lambda: self.down(group, level).wait_send()
                )
                self.when(self.roles(group, level, True)[0], lambda: self.up(group, level).wait_send())


def layer_kernel(
    groups,
    child_in,
    importance_in,
    board_in,
    slot_in,
    counts_in,
    parent_in,
    proj_in,
    q_in,
    q_bias_in,
    w_in,
    w_bias_in,
    cot_in,
    emb,
    message,
    parent,
    total,
    bias_out,
    child,
    proj,
    q,
    w,
    cot,
    merged,
    scaled_slope,
    arrived,
    moved,
    pre,
    table_rows,
    grad_pre,
    grad_moved,
    back_out,
    back_in,
    held,
    inbox,
    weight_col,
    board_col,
    shrink,
    slot_shrink,
    got_weight,
    got_slot,
    info_out,
    info_in,
    bias_held,
    bias_in,
    importance,
    board,
    slot,
    counts,
    q_bias,
    w_bias,
    load_sem,
    small_sem,
    info_sem,
    msg_sem,
    back_sem,
    bias_sem,
    sum_send,
    sum_recv,
    sum_out,
    sum_in,
):
    hop, core = lax.axis_index("hop"), lax.axis_index("par")
    me = hop * 2 + core
    slots, width = child.shape
    parents = parent.shape[0]
    devices = counts.shape[1]
    cap = slots // devices
    half = slots // 2
    levels = bias_held.shape[0]
    tiles = width // TILE
    upper = own_bit(hop, core, levels - 2)
    sides = (1 - upper, upper)
    f32, bf16 = jnp.float32, jnp.bfloat16

    def other_hop(flips):
        to_hop = hop
        for bit in range(levels - 1):
            if (flips >> bit) & 1:
                to_hop = to_hop + (1 - 2 * own_bit(hop, core, bit)) * (1 << bit)
        return to_hop

    def targets(first, last):
        away = [(other_hop(flips), to_core) for to_core in range(2) for flips in range(last - 1, max(first, 1) - 1, -1)]
        return away + ([(hop, 1 - core)] if first == 0 else [])

    def rows_of(device):
        return pl.ds(pl.multiple_of(device * cap, cap), cap)

    def side_rows(side):
        return pl.ds(pl.multiple_of(side * half, half), half)

    loads = []
    for index, (source, place) in enumerate(
        ((child_in, child), (proj_in, proj), (q_in, q), (parent_in, parent), (w_in, w), (cot_in, cot))
    ):
        loads.append(pltpu.make_async_copy(source, place, load_sem.at[index]))
    small = []
    for index, (source, place) in enumerate(
        (
            (importance_in, importance),
            (board_in, board),
            (slot_in, slot),
            (counts_in, counts),
            (q_bias_in, q_bias),
            (w_bias_in, w_bias),
        )
    ):
        small.append(pltpu.make_async_copy(source, place, small_sem.at[index]))
    for copy in small + loads[:3]:
        copy.start()

    barrier = pltpu.get_barrier_semaphore()
    for to in targets(0, devices // 2):
        pl.semaphore_signal(barrier, inc=1, device_id=to, device_id_type=MESH)

    lane = lax.broadcasted_iota(jnp.int32, (128, 128), 1)
    down = lax.broadcasted_iota(jnp.int32, (128, 128), 0)
    eye = lane == down
    place = lax.rem(down, cap)

    def column(row):
        return jnp.sum(jnp.where(eye, jnp.broadcast_to(row, (128, 128)), 0.0), axis=1, keepdims=True)

    for copy in small:
        copy.wait()
    count_row = counts[...].astype(f32)
    for part in range(slots // 128):
        owner = lax.broadcasted_iota(jnp.int32, (128, devices), 0) // cap + part * (128 // cap)
        is_owner = owner == lax.broadcasted_iota(jnp.int32, (128, devices), 1)
        live = jnp.sum(
            jnp.where(is_owner, jnp.broadcast_to(count_row, (128, devices)), 0.0), axis=1, keepdims=True
        )
        weight = jnp.broadcast_to(column(importance[part : part + 1, :]), (128, 128))
        weight = jnp.where(place.astype(f32) < live, weight, 0.0)
        slot_at = jnp.broadcast_to(column(slot[part : part + 1, :].astype(f32)), (128, 128))
        at = slice(part * 128, (part + 1) * 128)
        weight_col[at, :] = weight
        board_col[at, :] = jnp.broadcast_to(column(board[part : part + 1, :].astype(f32)), (128, 128))
        info = jnp.where(lane == place, weight, 0.0) + jnp.where(lane == place + cap, slot_at, 0.0)
        for owner_at in range(128 // cap):
            info_out[part * (128 // cap) + owner_at] = jnp.sum(
                info[owner_at * cap : (owner_at + 1) * cap, :], axis=0, keepdims=True
            )

    quarter = devices // 4

    def targets_of(side_index):
        return targets(quarter, 2 * quarter) if side_index == 0 else targets(0, quarter)

    def send_info(side_index):
        for to_hop, to_core in targets_of(side_index):
            pltpu.make_async_remote_copy(
                src_ref=info_out.at[to_hop * 2 + to_core],
                dst_ref=info_in.at[me],
                send_sem=info_sem.at[0],
                recv_sem=info_sem.at[1],
                device_id=(to_hop, to_core),
                device_id_type=MESH,
            ).start()
        if side_index == 1:
            pltpu.make_async_copy(info_out.at[me], info_in.at[me], info_sem.at[1]).start()

    def send_side(source, place_ref, sem, side_index):
        for to_hop, to_core in targets_of(side_index):
            pltpu.make_async_remote_copy(
                src_ref=source.at[rows_of(to_hop * 2 + to_core)],
                dst_ref=place_ref.at[rows_of(me)],
                send_sem=sem.at[0, side_index],
                recv_sem=sem.at[1, side_index],
                device_id=(to_hop, to_core),
                device_id_type=MESH,
            ).start()
        if side_index == 1:
            pltpu.make_async_copy(
                source.at[rows_of(me)], place_ref.at[rows_of(me)], sem.at[1, side_index]
            ).start()

    def wait_side(place_ref, sem, side_index):
        rows = side_rows(sides[side_index])
        pltpu.make_async_copy(place_ref.at[rows], place_ref.at[rows], sem.at[1, side_index]).wait()

    def wait_sent(source, sem):
        for side_index, rows in ((0, half), (1, half - cap)):
            part = source.at[pl.ds(0, rows)]
            pltpu.make_async_copy(part, part, sem.at[0, side_index]).wait()

    loads[0].wait()
    loads[1].wait()
    for side_index, side in enumerate(sides):
        rows = side_rows(side)
        boards = spread(board_col[rows, :], TILE) == 1.0

        @pl.loop(0, tiles)
        def _(tile):
            projected = mm(child[rows, :], proj[:, columns(tile)])
            raw = child[rows, columns(tile)]
            merged[rows, columns(tile)] = jnp.where(boards, projected, raw.astype(f32)).astype(bf16)

        if side_index == 0:
            loads[2].wait()
            for copy in loads[3:]:
                copy.start()
        weights = spread(weight_col[rows, :], TILE)

        @pl.loop(0, tiles)
        def _(tile):
            value = mm(merged[rows, :], q[:, columns(tile)]) + q_bias[:, columns(tile)]
            gate = sigmoid(value)
            act = value * gate
            message[rows, columns(tile)] = (weights * act).astype(bf16)
            scaled_slope[rows, columns(tile)] = weights * (gate + act * (1.0 - gate))

        if side_index == 0:
            pl.semaphore_wait(barrier, devices - 1)
        send_info(side_index)
        send_side(message, arrived, msg_sem, side_index)

    loads[3].wait()
    loads[4].wait()

    @pl.loop(0, tiles)
    def _(tile):
        pre[:, columns(tile)] = mm(parent[...], w[pl.ds(0, width), columns(tile)]) + w_bias[:, columns(tile)]

    info_all = pltpu.make_async_copy(info_in, info_in, info_sem.at[1])
    info_all.wait()
    lane16 = lax.broadcasted_iota(jnp.int32, (cap, 128), 1)
    down16 = lax.broadcasted_iota(jnp.int32, (cap, 128), 0)
    for device in range(devices):
        got = jnp.broadcast_to(info_in[device], (cap, 128))
        at = slice(device * cap, (device + 1) * cap)
        got_weight[at, :] = jnp.broadcast_to(
            jnp.sum(jnp.where(lane16 == down16, got, 0.0), axis=1, keepdims=True), (cap, 128)
        )
        got_slot[at, :] = jnp.broadcast_to(
            jnp.sum(jnp.where(lane16 == down16 + cap, got, 0.0), axis=1, keepdims=True), (cap, 128)
        )

    for part in range(parents // 128):
        want = (lax.broadcasted_iota(jnp.int32, (128, 128), 1) + part * 128).astype(f32)
        weight_sum = jnp.zeros((1, 128), f32)
        for block in range(slots // 128):
            at = slice(block * 128, (block + 1) * 128)
            hit = got_slot[at, :] == want
            table_rows[at, part * 128 : (part + 1) * 128] = jnp.where(hit, 1.0, 0.0).astype(bf16)
            weight_sum = weight_sum + jnp.sum(jnp.where(hit, got_weight[at, :], 0.0), axis=0, keepdims=True)
        inverse = 1.0 / jnp.maximum(weight_sum, 1.0)
        shrink[part * 128 : (part + 1) * 128, :] = jnp.broadcast_to(column(inverse), (128, 128))
        for block in range(slots // 128):
            at = slice(block * 128, (block + 1) * 128)
            hit = got_slot[at, :] == want
            term = jnp.where(hit, jnp.broadcast_to(inverse, (128, 128)), 0.0)
            if part == 0:
                slot_shrink[at, :] = term
            else:
                slot_shrink[at, :] = slot_shrink[at, :] + term
    for block in range(slots // 128):
        at = slice(block * 128, (block + 1) * 128)
        slot_shrink[at, :] = jnp.broadcast_to(
            jnp.sum(slot_shrink[at, :], axis=1, keepdims=True), (128, 128)
        )

    def add_messages(side_index):
        rows = side_rows(sides[side_index])

        @pl.loop(0, tiles)
        def _(tile):
            moved[rows, columns(tile)] = mm(arrived[rows, :], w[pl.ds(width, width), columns(tile)]).astype(bf16)

        @pl.loop(0, tiles)
        def _(tile):
            pre[:, columns(tile)] = pre[:, columns(tile)] + spread(shrink[...], TILE) * contract_rows(
                table_rows[rows, :], moved[rows, columns(tile)]
            )

    wait_side(arrived, msg_sem, 1)
    add_messages(1)
    loads[5].wait()
    wait_side(arrived, msg_sem, 0)
    add_messages(0)

    @pl.loop(0, parents // BLOCK)
    def _(block):
        at = columns(block, BLOCK)
        value = pre[at, :]
        turn = cot[at, :]
        gate = sigmoid(value)
        act = value * gate
        inv = lax.rsqrt(jnp.sum(act * act, axis=1, keepdims=True) + 1e-06)
        share = jnp.sum(turn * act, axis=1, keepdims=True) * (inv * inv * inv)
        emb[at, :] = (act * inv).astype(bf16)
        grad_pre[at, :] = ((turn * inv - act * share) * (gate + act * (1.0 - gate))).astype(bf16)

    for side_index, side in enumerate(sides):
        rows = side_rows(side)
        shrinks = spread(slot_shrink[rows, :], TILE)

        @pl.loop(0, tiles)
        def _(tile):
            grad_moved[rows, columns(tile)] = (
                shrinks * mm(table_rows[rows, :], grad_pre[:, columns(tile)])
            ).astype(bf16)

        @pl.loop(0, tiles)
        def _(tile):
            turned = w[pl.ds(pl.multiple_of(width + tile * TILE, TILE), TILE), :]
            back_out[rows, columns(tile)] = times_transpose(grad_moved[rows, :], turned).astype(bf16)

        send_side(back_out, back_in, back_sem, side_index)

    sums = Sums(hop, core, groups, held, inbox, total, (sum_send, sum_recv, sum_out, sum_in))
    w_groups = [g for g, (first, _, _) in enumerate(groups) if first < 2 * width]
    q_groups = [g for g, (first, _, _) in enumerate(groups) if 2 * width <= first < 3 * width]
    p_groups = [g for g, (first, _, _) in enumerate(groups) if first >= 3 * width]

    @pl.loop(0, tiles)
    def _(tile):
        held[pl.ds(0, width), columns(tile)] = contract_rows(parent[...], grad_pre[:, columns(tile)]).astype(bf16)

    for group in w_groups[: len(w_groups) // 2]:
        sums.halve(group, 0)

    @pl.loop(0, tiles)
    def _(tile):
        held[pl.ds(width, width), columns(tile)] = contract_rows(
            arrived[...], grad_moved[:, columns(tile)]
        ).astype(bf16)

    for group in w_groups[len(w_groups) // 2 :]:
        sums.halve(group, 0)
    bias_held[0, 0:1, :] = mm(jnp.ones((16, parents), bf16), grad_pre[...])[0:1, :]

    def parent_gradient():
        @pl.loop(0, tiles)
        def _(tile):
            parent[:, columns(tile)] = times_transpose(grad_pre[...], w[columns(tile), :]).astype(bf16)

        wait_sent(message, msg_sem)

    def child_front(side_index):
        rows = side_rows(sides[side_index])

        @pl.loop(0, tiles)
        def _(tile):
            grad_moved[rows, columns(tile)] = (
                scaled_slope[rows, columns(tile)] * back_in[rows, columns(tile)].astype(f32)
            ).astype(bf16)

    def weight_sums(side_index, left, grads, partial, base):
        rows = side_rows(sides[side_index])

        @pl.loop(0, tiles)
        def _(tile):
            value = contract_rows(left[rows, :], grads[rows, columns(tile)])
            if side_index == 1:
                partial[:, columns(tile)] = value
            else:
                held[pl.ds(base, width), columns(tile)] = (value + partial[:, columns(tile)]).astype(bf16)

    def child_middle(side_index):
        rows = side_rows(sides[side_index])
        boards = spread(board_col[rows, :], TILE) == 1.0

        @pl.loop(0, tiles)
        def _(tile):
            value = times_transpose(grad_moved[rows, :], q[columns(tile), :])
            moved[rows, columns(tile)] = jnp.where(boards, value, 0.0).astype(bf16)
            scaled_slope[rows, columns(tile)] = jnp.where(boards, 0.0, value)

    def child_end(side_index):
        rows = side_rows(sides[side_index])

        @pl.loop(0, tiles)
        def _(tile):
            value = times_transpose(moved[rows, :], proj[columns(tile), :])
            message[rows, columns(tile)] = (scaled_slope[rows, columns(tile)] + value).astype(bf16)

    bias_copies = []

    def send_bias(level):
        copy = pltpu.make_async_remote_copy(
            src_ref=bias_held.at[level],
            dst_ref=bias_in.at[level],
            send_sem=bias_sem.at[0, level],
            recv_sem=bias_sem.at[1, level],
            device_id=partner(hop, core, level - 1),
            device_id_type=MESH,
        )
        copy.start()
        bias_copies.append(copy)

    def fold_bias(level):
        bias_copies[level].wait_recv()
        both = bias_held[level] + bias_in[level]
        if level < levels - 1:
            bias_held[level + 1] = both
            send_bias(level + 1)
        else:
            bias_out[...] = both

    def near_children():
        child_front(1)
        weight_sums(1, merged, grad_moved, pre, 2 * width)
        child_middle(1)
        weight_sums(1, child, moved, cot, 3 * width)
        child_end(1)

    def far_q():
        child_front(0)
        weight_sums(0, merged, grad_moved, pre, 2 * width)

    def far_p():
        child_middle(0)
        weight_sums(0, child, moved, cot, 3 * width)

    def send_q():
        for group in q_groups:
            sums.halve(group, 0)
        bias_held[0, 1:2, :] = mm(jnp.ones((16, slots), bf16), grad_moved[...])[0:1, :]
        send_bias(0)

    def far_end():
        child_end(0)

    main = [
        parent_gradient,
        lambda: wait_side(back_in, back_sem, 1),
        near_children,
        lambda: wait_side(back_in, back_sem, 0),
        far_q,
        send_q,
        far_p,
        lambda: [sums.halve(group, 0) for group in p_groups],
        far_end,
    ]
    done = [0] * (len(groups) + 1)
    for turn in SCHEDULE:
        at = done[turn]
        done[turn] += 1
        if turn == 0:
            main[at]()
        elif at < sums.levels:
            sums.fold(turn - 1, at)
            if turn - 1 == q_groups[0]:
                fold_bias(at)
        else:
            sums.gather(turn - 1, 2 * sums.levels - 1 - at)

    sums.finish()
    for copy in bias_copies:
        copy.wait_send()
    wait_sent(back_out, back_sem)
    sent = info_out.at[pl.ds(0, devices - 1)]
    pltpu.make_async_copy(sent, sent, info_sem.at[0]).wait()


GROUPS = [("cxyim", 2), ("cyxim", 2), ("cxyim", 2), ("cyxim", 2), ("cxyim", 4), ("cyxim", 4), ("cxyim", 4), ("cyxim", 4), ("cxyim", 4), ("cyxim", 4), ("cxyim", 4), ("cyxim", 4)]
SCHEDULE = [
    1, 2, 0, 3, 4, 1, 0, 2, 0, 0, 0, 0, 4, 3, 1, 2, 0, 5, 0, 7, 8, 1, 2, 6, 4, 0, 7, 1, 5, 8, 2, 6, 11, 4, 12, 3,
    10, 7, 2, 6, 9, 1, 3, 11, 5, 12, 4, 10, 3, 9, 2, 8, 7, 1, 6, 11, 5, 12, 3, 8, 9, 4, 11, 10, 1, 2, 8, 3, 7, 4, 9, 6,
    5, 7, 12, 10, 5, 2, 6, 1, 9, 12, 4, 3, 11, 10, 5, 6, 9, 1, 8, 8, 12, 11, 7, 5, 12, 6, 9, 10, 7, 11, 3, 2, 5, 12, 10, 4,
    9, 8, 12, 11, 6, 10, 9, 7, 3, 8, 4, 6, 9, 12, 11, 10, 5, 8, 10, 11, 7,
]


def sum_groups(width):
    groups, first = [], 0
    for order, share in GROUPS:
        groups.append((first, width // share, order))
        first += width // share
    return groups


def inbox_rows(groups):
    total = 0
    for _, size, order in groups:
        for kind in order:
            size = size if kind == "i" else size // 2
            total += size
    return total


def widen_kernel(
    emb,
    child,
    parent,
    total,
    biases,
    emb_out,
    child_out,
    parent_out,
    proj_out,
    q_out,
    q_bias_out,
    w_out,
    w_bias_out,
    wide,
    w_bias,
    q_bias,
    write_sem,
    other_sem,
):
    slots, rows, width = wide.shape
    w_bias[...] = biases[0, :]
    q_bias[...] = biases[1, :]
    others = [
        pltpu.make_async_copy(source, place, other_sem.at[index])
        for index, (source, place) in enumerate(((child, child_out), (w_bias, w_bias_out), (q_bias, q_bias_out)))
    ]
    for copy in others:
        copy.start()
    pieces = []
    for source, place in ((parent, parent_out), (emb, emb_out)):
        for first in range(0, place.shape[0], rows):
            pieces.append((source, first, place, first))
    base = 0
    for place in (w_out, q_out, proj_out):
        for first in range(0, place.shape[0], rows):
            pieces.append((total, base + first, place, first))
        base += place.shape[0]
    def write(index):
        _, _, place, first = pieces[index]
        slot = index % slots
        return pltpu.make_async_copy(wide.at[slot], place.at[pl.ds(first, rows)], write_sem.at[slot])

    for index, (source, first, _, _) in enumerate(pieces):
        if index >= slots:
            write(index - slots).wait()
        wide[index % slots] = source[first : first + rows, :].astype(jnp.float32)
        write(index).start()
    for index in range(len(pieces) - slots, len(pieces)):
        write(index).wait()
    for copy in others:
        copy.wait()


def widen(emb, child, parent, total, biases):
    width = emb.shape[1]
    slots, rows = 8, 256
    shape, f32 = jax.ShapeDtypeStruct, jnp.float32
    hbm = pl.BlockSpec(memory_space=pl.ANY)
    vmem = pl.BlockSpec(memory_space=pltpu.VMEM)
    return pl.pallas_call(
        widen_kernel,
        name="widen",
        out_shape=(
            shape(emb.shape, f32),
            shape(child.shape, child.dtype),
            shape(parent.shape, f32),
            shape((width, width), f32),
            shape((width, width), f32),
            shape((width,), f32),
            shape((2 * width, width), f32),
            shape((width,), f32),
        ),
        in_specs=[vmem, vmem, vmem, vmem, vmem],
        out_specs=(hbm,) * 8,
        scratch_shapes=[
            pltpu.VMEM((slots, rows, width), f32),
            pltpu.VMEM((width,), f32),
            pltpu.VMEM((width,), f32),
            pltpu.SemaphoreType.DMA((slots,)),
            pltpu.SemaphoreType.DMA((3,)),
        ],
        compiler_params=pltpu.CompilerParams(vmem_limit_bytes=36 << 20),
    )(emb, child, parent, total, biases)


def fused_body(
    child_feats,
    board_mask,
    importance,
    parent_slot,
    send_counts,
    parent_feats,
    proj_weight,
    q_weight,
    q_bias,
    w_weight,
    w_bias,
    emb_cotangent,
):
    slots, width = child_feats.shape
    parents = parent_feats.shape[0]
    devices = send_counts.shape[1]
    groups = sum_groups(width)
    levels = devices.bit_length() - 1
    f32, bf16 = jnp.float32, jnp.bfloat16
    vmem = pl.BlockSpec(memory_space=pltpu.VMEM)
    hbm = pl.BlockSpec(memory_space=pl.ANY)
    dma = pltpu.SemaphoreType.DMA
    shape = jax.ShapeDtypeStruct
    emb, grad_child, grad_parent, total, biases = pl.pallas_call(
        functools.partial(layer_kernel, groups),
        name="layer",
        out_shape=(
            pltpu.VMEM((parents, width), bf16),
            pltpu.VMEM((slots, width), bf16),
            pltpu.VMEM((parents, width), bf16),
            pltpu.VMEM((4 * width, width), bf16),
            pltpu.VMEM((2, width), f32),
        ),
        in_specs=[hbm] * 12,
        out_specs=(vmem, vmem, vmem, vmem, vmem),
        scratch_shapes=[
            pltpu.VMEM((slots, width), bf16),
            pltpu.VMEM((width, width), bf16),
            pltpu.VMEM((width, width), bf16),
            pltpu.VMEM((2 * width, width), bf16),
            pltpu.VMEM((parents, width), f32),
            pltpu.VMEM((slots, width), bf16),
            pltpu.VMEM((slots, width), f32),
            pltpu.VMEM((slots, width), bf16),
            pltpu.VMEM((slots, width), bf16),
            pltpu.VMEM((parents, width), f32),
            pltpu.VMEM((slots, parents), bf16),
            pltpu.VMEM((parents, width), bf16),
            pltpu.VMEM((slots, width), bf16),
            pltpu.VMEM((slots, width), bf16),
            pltpu.VMEM((slots, width), bf16),
            pltpu.VMEM((4 * width, width), bf16),
            pltpu.VMEM((inbox_rows(groups), width), bf16),
            pltpu.VMEM((slots, 128), f32),
            pltpu.VMEM((slots, 128), f32),
            pltpu.VMEM((parents, 128), f32),
            pltpu.VMEM((slots, 128), f32),
            pltpu.VMEM((slots, 128), f32),
            pltpu.VMEM((slots, 128), f32),
            pltpu.VMEM((devices, 1, 128), f32),
            pltpu.VMEM((devices, 1, 128), f32),
            pltpu.VMEM((levels, 2, width), f32),
            pltpu.VMEM((levels, 2, width), f32),
            pltpu.VMEM((slots // 128, 128), f32),
            pltpu.VMEM((slots // 128, 128), jnp.int32),
            pltpu.VMEM((slots // 128, 128), jnp.int32),
            pltpu.VMEM(send_counts.shape, jnp.int32),
            pltpu.VMEM((1, width), f32),
            pltpu.VMEM((1, width), f32),
            dma((6,)),
            dma((6,)),
            dma((2,)),
            dma((2, 2)),
            dma((2, 2)),
            dma((2, levels)),
        ]
        + [dma((len(groups), len(groups[0][2])))] * 4,
        compiler_params=pltpu.CompilerParams(
            collective_id=1, has_side_effects=True, vmem_limit_bytes=50 << 20
        ),
        cost_estimate=pl.CostEstimate(
            flops=36 * slots * width * width, bytes_accessed=40 << 20, transcendentals=3 * parents * width
        ),
    )(
        child_feats,
        importance.reshape(-1, 128),
        board_mask.reshape(-1, 128),
        parent_slot.reshape(-1, 128),
        send_counts,
        parent_feats,
        proj_weight,
        q_weight,
        q_bias.reshape(1, -1),
        w_weight,
        w_bias.reshape(1, -1),
        emb_cotangent,
    )
    return widen(emb, grad_child, grad_parent, total, biases)


def solution(mesh):
    rows = P(("hop", "par"), None)
    flat = P(("hop", "par"))
    fused = mesh.shape["hop"] == 16 and mesh.shape["par"] == 2
    return jax.shard_map(
        fused_body if fused else plain_body,
        mesh=mesh,
        in_specs=(rows, flat, flat, flat, rows, rows, P(), P(), P(), P(), P(), rows),
        out_specs=(rows, rows, rows, P(), P(), P(), P(), P()),
        check_vma=False,
    )
```

```python
import functools

import jax
import jax.numpy as jnp
from jax import lax
from jax.experimental import pallas as pl
from jax.experimental.pallas import tpu as pltpu
from jax.sharding import PartitionSpec as P

MESH = pl.DeviceIdType.MESH
CORE = -1


def times_transpose(left, right):
    return lax.dot_general(
        left, right, (((1,), (1,)), ((), ())), preferred_element_type=jnp.float32
    )


def contract_rows(left, right):
    return lax.dot_general(
        left, right, (((0,), (0,)), ((), ())), preferred_element_type=jnp.float32
    )


def silu_slope(value):
    sigma = jax.nn.sigmoid(value)
    return sigma * (1.0 + value * (1.0 - sigma))


def send_rows(payload, hop_count, par_count, slot_cap, feature_width):
    parcel = payload.reshape(hop_count * par_count, slot_cap, feature_width)
    arrived = lax.all_to_all(parcel, ("hop", "par"), split_axis=0, concat_axis=0, tiled=True)
    return arrived.reshape(payload.shape)


def halving_orders(hop_count, rows):
    bits = hop_count.bit_length() - 1
    if bits == 4:
        x, y, z0, z1 = range(4)
        base = [[x, y, z0, z1], [y, x, z0, z1], [z0, x, y, z1], [x, y, z0, z1]]
        base += [[y, x, z0, z1], [z0, y, x, z1], [x, y, z0, z1], [y, x, z0, z1]]
    else:
        base = [[(first + k) % bits for k in range(bits)] for first in range(0, bits, 2)]
    groups = 1
    while groups * 2 <= len(base) and rows // (groups * 2) // (hop_count * 2) >= 16:
        groups *= 2
    return [[CORE] + order for order in base[:groups]]


def own_bit(hop, core, bit):
    return core if bit == CORE else lax.rem(hop // (1 << bit), 2)


def partner(hop, core, bit):
    if bit == CORE:
        return (hop, 1 - core)
    return (hop + (1 - 2 * own_bit(hop, core, bit)) * (1 << bit), core)


def sum_kernel(orders, part_ref, sum_ref, held, inbox, send_sem, recv_sem, out_sem, in_sem):
    hop, core = lax.axis_index("hop"), lax.axis_index("par")
    groups, levels = len(orders), len(orders[0])
    rows = part_ref.shape[0] // groups
    barrier = pltpu.get_barrier_semaphore()
    for bit in range(CORE, levels - 1):
        pl.semaphore_signal(barrier, inc=1, device_id=partner(hop, core, bit), device_id_type=MESH)
    held[...] = part_ref[...]
    pl.semaphore_wait(barrier, levels)

    start = [jnp.int32(group * rows) for group in range(groups)]
    kept = [[None] * levels for _ in range(groups)]
    places = [rows - (rows >> level) for level in range(levels)]
    down, up = {}, {}

    def halve(group, level):
        bit = orders[group][level]
        half = rows >> (level + 1)
        mine = own_bit(hop, core, bit)
        away = pl.multiple_of(start[group] + (1 - mine) * half, half)
        copy = pltpu.make_async_remote_copy(
            src_ref=held.at[pl.ds(away, half)],
            dst_ref=inbox.at[group, pl.ds(places[level], half)],
            send_sem=send_sem.at[group, level],
            recv_sem=recv_sem.at[group, level],
            device_id=partner(hop, core, bit),
            device_id_type=MESH,
        )
        copy.start()
        down[group, level] = copy
        start[group] = start[group] + mine * half
        kept[group][level] = start[group]

    def double(group, level):
        half = rows >> (level + 1)
        part = pl.ds(pl.multiple_of(kept[group][level], half), half)
        copy = pltpu.make_async_remote_copy(
            src_ref=sum_ref.at[part],
            dst_ref=sum_ref.at[part],
            send_sem=out_sem.at[group, level],
            recv_sem=in_sem.at[group, level],
            device_id=partner(hop, core, orders[group][level]),
            device_id_type=MESH,
        )
        copy.start()
        up[group, level] = copy

    for group in range(groups):
        halve(group, 0)
    for level in range(levels):
        for group in range(groups):
            half = rows >> (level + 1)
            part = pl.ds(pl.multiple_of(kept[group][level], half), half)
            down[group, level].wait_recv()
            total = held[part] + inbox[group, pl.ds(places[level], half)]
            if level < levels - 1:
                held[part] = total
                halve(group, level + 1)
            else:
                sum_ref[part] = total
                double(group, level)
    for level in range(levels - 1, -1, -1):
        for group in range(groups):
            up[group, level].wait_recv()
            if level > 0:
                double(group, level - 1)
    for level in range(levels):
        for group in range(groups):
            down[group, level].wait_send()
            up[group, level].wait_send()


def sum_over_devices(part, hop_count):
    rows, columns = part.shape
    orders = halving_orders(hop_count, rows)
    groups, levels = len(orders), len(orders[0])
    semaphores = pltpu.SemaphoreType.DMA((groups, levels))
    return pl.pallas_call(
        functools.partial(sum_kernel, orders),
        name="weight_gradient_sum",
        out_shape=jax.ShapeDtypeStruct((rows, columns), part.dtype),
        in_specs=[pl.BlockSpec(memory_space=pltpu.VMEM)],
        out_specs=pl.BlockSpec(memory_space=pltpu.VMEM),
        scratch_shapes=[
            pltpu.VMEM((rows, columns), part.dtype),
            pltpu.VMEM((groups, rows // groups, columns), part.dtype),
            semaphores,
            semaphores,
            semaphores,
            semaphores,
        ],
        compiler_params=pltpu.CompilerParams(
            collective_id=0, has_side_effects=True, vmem_limit_bytes=48 << 20
        ),
    )(part)


def plain_body(
    child_feats,
    board_mask,
    importance,
    parent_slot,
    send_counts,
    parent_feats,
    proj_weight,
    q_weight,
    q_bias,
    w_weight,
    w_bias,
    emb_cotangent,
):
    slot_rows, feature_width = child_feats.shape
    hop_count = lax.axis_size("hop")
    par_count = lax.axis_size("par")
    shard_count = hop_count * par_count
    slot_cap = slot_rows // shard_count
    live_slots = (
        (jnp.arange(slot_cap)[None, :] < send_counts[0][:, None])
        .astype(jnp.float32)
        .reshape(slot_rows)
    )
    weight_live = importance * live_slots
    is_board = board_mask[:, None] == 1
    projected = jnp.dot(child_feats, proj_weight, preferred_element_type=jnp.float32)
    merged = jnp.where(is_board, projected, child_feats.astype(jnp.float32)).astype(jnp.bfloat16)
    pre_act = jnp.dot(merged, q_weight, preferred_element_type=jnp.float32) + q_bias
    message = (weight_live[:, None] * jax.nn.silu(pre_act)).astype(jnp.bfloat16)
    edge_info = jnp.stack([weight_live, parent_slot.astype(jnp.float32)]).reshape(
        2, shard_count, slot_cap
    )
    got_info = lax.all_to_all(edge_info, ("hop", "par"), split_axis=1, concat_axis=1, tiled=True)
    got_weight = got_info[0].reshape(slot_rows)
    got_slot = got_info[1].reshape(slot_rows).astype(jnp.int32)
    arrived = send_rows(message, hop_count, par_count, slot_cap, feature_width)
    parent_rows = parent_feats.shape[0]
    owner_table = got_slot[None, :] == jnp.arange(parent_rows, dtype=jnp.int32)[:, None]
    gathered = jnp.dot(
        owner_table.astype(jnp.bfloat16), arrived, preferred_element_type=jnp.float32
    )
    weight_sum = jnp.sum(jnp.where(owner_table, got_weight[None, :], 0.0), axis=1)
    divisor = jnp.maximum(weight_sum, 1.0)
    neighbor_mean = (gathered / divisor[:, None]).astype(jnp.bfloat16)
    joined = jnp.concatenate([parent_feats, neighbor_mean], axis=1)
    pre_norm = jnp.dot(joined, w_weight, preferred_element_type=jnp.float32) + w_bias
    act_out = jax.nn.silu(pre_norm)
    inv_norm = lax.rsqrt(jnp.sum(act_out * act_out, axis=1, keepdims=True) + 1e-06)
    embedding = act_out * inv_norm
    grad_emb = inv_norm * (
        emb_cotangent - embedding * jnp.sum(emb_cotangent * embedding, axis=1, keepdims=True)
    )
    grad_pre = (grad_emb * silu_slope(pre_norm)).astype(jnp.bfloat16)
    grad_w = contract_rows(joined, grad_pre)
    grad_wbias = jnp.sum(grad_pre.astype(jnp.float32), axis=0)
    grad_cat = times_transpose(grad_pre, w_weight)
    grad_parent = grad_cat[:, :feature_width]
    grad_mean = grad_cat[:, feature_width:] / divisor[:, None]
    return_rows = jnp.take(grad_mean, got_slot, axis=0).astype(jnp.bfloat16)
    grad_message = send_rows(return_rows, hop_count, par_count, slot_cap, feature_width)
    grad_act = weight_live[:, None] * grad_message.astype(jnp.float32)
    grad_preact = (grad_act * silu_slope(pre_act)).astype(jnp.bfloat16)
    grad_q = contract_rows(merged, grad_preact)
    grad_qbias = jnp.sum(grad_preact.astype(jnp.float32), axis=0)
    grad_merged = times_transpose(grad_preact, q_weight)
    grad_board = jnp.where(is_board, grad_merged, 0.0).astype(jnp.bfloat16)
    grad_proj = contract_rows(child_feats, grad_board)
    grad_child = (
        jnp.where(is_board, 0.0, grad_merged) + times_transpose(grad_board, proj_weight)
    ).astype(jnp.bfloat16)
    part = jnp.concatenate([grad_w, grad_q, grad_proj]).astype(jnp.bfloat16)
    summed = sum_over_devices(part, hop_count)
    summed = summed.astype(jnp.float32)
    grad_qbias, grad_wbias = lax.psum((grad_qbias, grad_wbias), ("hop", "par"))
    w_rows, q_rows = grad_w.shape[0], grad_q.shape[0]
    return (
        embedding,
        grad_child,
        grad_parent,
        summed[w_rows + q_rows :],
        summed[w_rows : w_rows + q_rows],
        grad_qbias,
        summed[:w_rows],
        grad_wbias,
    )


TILE = 512
WIDE = 1024
BLOCK = 128


def columns(index, width=TILE):
    return pl.ds(pl.multiple_of(index * width, width), width)


def mm(left, right):
    return jnp.dot(left, right, preferred_element_type=jnp.float32)


def sigmoid(value):
    return 0.5 * jnp.tanh(0.5 * value) + 0.5


def spread(column, width):
    return jnp.concatenate([column] * (width // column.shape[1]), axis=1)


class Sums:
    def __init__(self, hop, core, groups, held, inbox, total, sems):
        self.hop, self.core, self.groups = hop, core, groups
        self.held, self.inbox, self.total = held, inbox, total
        self.send, self.recv, self.out, self.into = sems
        self.levels = len(groups[0][2])
        low, high = own_bit(hop, core, 2), own_bit(hop, core, 3)
        self.is_inner = low != high
        self.high = high
        place = 0
        self.plans = []
        for first, rows, order in groups:
            start, size, inner, steps = jnp.int32(first), rows, False, []
            for kind in order:
                if kind == "i":
                    step = (kind, start, start, size, place, inner)
                    inner = True
                else:
                    size //= 2
                    mine = high if kind == "m" else own_bit(hop, core, "cxypq".index(kind) - 1)
                    step = (kind, start + (1 - mine) * size, start + mine * size, size, place, inner)
                    start = start + mine * size
                    inner = inner or kind == "m"
                steps.append(step)
                place += size
            self.plans.append(steps)

    def other(self, kind):
        if kind == "m":
            return (self.hop + (1 - 2 * self.high) * 4, self.core)
        return partner(self.hop, self.core, "cxypq".index(kind.replace("i", "p")) - 1)

    def when(self, role, what):
        if role is None:
            what()
        else:
            pl.when(self.is_inner if role == "inner" else jnp.logical_not(self.is_inner))(what)

    def roles(self, group, level, upward):
        kind, _, _, _, _, inner = self.plans[group][level]
        if kind == "i":
            return ("inner", "outer") if upward else ("outer", "inner")
        role = "inner" if inner or kind == "m" else None
        return role, role

    def rows(self, start, size):
        return pl.ds(pl.multiple_of(start, size), size)

    def down(self, group, level):
        kind, away, _, size, place, _ = self.plans[group][level]
        return pltpu.make_async_remote_copy(
            src_ref=self.held.at[self.rows(away, size)],
            dst_ref=self.inbox.at[pl.ds(place, size)],
            send_sem=self.send.at[group, level],
            recv_sem=self.recv.at[group, level],
            device_id=self.other(kind),
            device_id_type=MESH,
        )

    def up(self, group, level):
        kind, _, kept, size, _, _ = self.plans[group][level]
        part = self.rows(kept, size)
        return pltpu.make_async_remote_copy(
            src_ref=self.total.at[part],
            dst_ref=self.total.at[part],
            send_sem=self.out.at[group, level],
            recv_sem=self.into.at[group, level],
            device_id=self.other(kind),
            device_id_type=MESH,
        )

    def halve(self, group, level):
        self.when(self.roles(group, level, False)[0], lambda: self.down(group, level).start())

    def double(self, group, level):
        self.when(self.roles(group, level, True)[0], lambda: self.up(group, level).start())

    def fold(self, group, level):
        _, _, kept, size, place, _ = self.plans[group][level]

        def add():
            self.down(group, level).wait_recv()
            part = self.rows(kept, size)
            done = self.total if level == self.levels - 1 else self.held
            done[part] = self.held[part] + self.inbox[pl.ds(place, size)]
            if level == self.levels - 1:
                self.up(group, level).start()

        self.when(self.roles(group, level, False)[1], add)
        if level < self.levels - 1:
            self.halve(group, level + 1)

    def gather(self, group, level):
        self.when(self.roles(group, level, True)[1], lambda: self.up(group, level).wait_recv())
        if level > 0:
            self.double(group, level - 1)

    def finish(self):
        for group in range(len(self.groups)):
            for level in range(self.levels):
                self.when(
                    self.roles(group, level, False)[0], lambda: self.down(group, level).wait_send()
                )
                self.when(self.roles(group, level, True)[0], lambda: self.up(group, level).wait_send())


def layer_kernel(
    groups,
    child_in,
    importance_in,
    board_in,
    slot_in,
    counts_in,
    parent_in,
    proj_in,
    q_in,
    q_bias_in,
    w_in,
    w_bias_in,
    cot_in,
    emb,
    message,
    parent,
    total,
    bias_out,
    child,
    proj,
    q,
    w,
    cot,
    merged,
    scaled_slope,
    arrived,
    moved,
    pre,
    table_rows,
    grad_pre,
    grad_moved,
    back_out,
    back_in,
    held,
    inbox,
    weight_col,
    board_col,
    shrink,
    slot_shrink,
    got_weight,
    got_slot,
    info_out,
    info_in,
    bias_held,
    bias_in,
    importance,
    board,
    slot,
    counts,
    q_bias,
    w_bias,
    load_sem,
    small_sem,
    info_sem,
    msg_sem,
    back_sem,
    bias_sem,
    sum_send,
    sum_recv,
    sum_out,
    sum_in,
):
    hop, core = lax.axis_index("hop"), lax.axis_index("par")
    me = hop * 2 + core
    slots, width = child.shape
    parents = parent.shape[0]
    devices = counts.shape[1]
    cap = slots // devices
    half = slots // 2
    levels = bias_held.shape[0]
    tiles = width // TILE
    wides = width // WIDE
    upper = own_bit(hop, core, levels - 2)
    sides = (1 - upper, upper)
    f32, bf16 = jnp.float32, jnp.bfloat16

    def other_hop(flips):
        to_hop = hop
        for bit in range(levels - 1):
            if (flips >> bit) & 1:
                to_hop = to_hop + (1 - 2 * own_bit(hop, core, bit)) * (1 << bit)
        return to_hop

    def targets(first, last):
        away = [(other_hop(flips), to_core) for to_core in range(2) for flips in range(last - 1, max(first, 1) - 1, -1)]
        return away + ([(hop, 1 - core)] if first == 0 else [])

    def rows_of(device):
        return pl.ds(pl.multiple_of(device * cap, cap), cap)

    def side_rows(side):
        return pl.ds(pl.multiple_of(side * half, half), half)

    loads = []
    for index, (source, place) in enumerate(
        ((child_in, child), (proj_in, proj), (q_in, q), (parent_in, parent), (w_in, w), (cot_in, cot))
    ):
        loads.append(pltpu.make_async_copy(source, place, load_sem.at[index]))
    small = []
    for index, (source, place) in enumerate(
        (
            (importance_in, importance),
            (board_in, board),
            (slot_in, slot),
            (counts_in, counts),
            (q_bias_in, q_bias),
            (w_bias_in, w_bias),
        )
    ):
        small.append(pltpu.make_async_copy(source, place, small_sem.at[index]))
    for copy in small + loads[:3]:
        copy.start()

    barrier = pltpu.get_barrier_semaphore()
    for to in targets(0, devices // 2):
        pl.semaphore_signal(barrier, inc=1, device_id=to, device_id_type=MESH)

    lane = lax.broadcasted_iota(jnp.int32, (128, 128), 1)
    down = lax.broadcasted_iota(jnp.int32, (128, 128), 0)
    eye = lane == down
    place = lax.rem(down, cap)

    def column(row):
        return jnp.sum(jnp.where(eye, jnp.broadcast_to(row, (128, 128)), 0.0), axis=1, keepdims=True)

    for copy in small:
        copy.wait()
    count_row = counts[...].astype(f32)
    for part in range(slots // 128):
        owner = lax.broadcasted_iota(jnp.int32, (128, devices), 0) // cap + part * (128 // cap)
        is_owner = owner == lax.broadcasted_iota(jnp.int32, (128, devices), 1)
        live = jnp.sum(
            jnp.where(is_owner, jnp.broadcast_to(count_row, (128, devices)), 0.0), axis=1, keepdims=True
        )
        weight = jnp.broadcast_to(column(importance[part : part + 1, :]), (128, 128))
        weight = jnp.where(place.astype(f32) < live, weight, 0.0)
        slot_at = jnp.broadcast_to(column(slot[part : part + 1, :].astype(f32)), (128, 128))
        at = slice(part * 128, (part + 1) * 128)
        weight_col[at, :] = weight
        board_col[at, :] = jnp.broadcast_to(column(board[part : part + 1, :].astype(f32)), (128, 128))
        info = jnp.where(lane == place, weight, 0.0) + jnp.where(lane == place + cap, slot_at, 0.0)
        for owner_at in range(128 // cap):
            info_out[part * (128 // cap) + owner_at] = jnp.sum(
                info[owner_at * cap : (owner_at + 1) * cap, :], axis=0, keepdims=True
            )

    quarter = devices // 4

    def targets_of(side_index):
        return targets(quarter, 2 * quarter) if side_index == 0 else targets(0, quarter)

    def send_info(side_index):
        for to_hop, to_core in targets_of(side_index):
            pltpu.make_async_remote_copy(
                src_ref=info_out.at[to_hop * 2 + to_core],
                dst_ref=info_in.at[me],
                send_sem=info_sem.at[0],
                recv_sem=info_sem.at[1],
                device_id=(to_hop, to_core),
                device_id_type=MESH,
            ).start()
        if side_index == 1:
            pltpu.make_async_copy(info_out.at[me], info_in.at[me], info_sem.at[1]).start()

    def send_side(source, place_ref, sem, side_index):
        for to_hop, to_core in targets_of(side_index):
            pltpu.make_async_remote_copy(
                src_ref=source.at[rows_of(to_hop * 2 + to_core)],
                dst_ref=place_ref.at[rows_of(me)],
                send_sem=sem.at[0, side_index],
                recv_sem=sem.at[1, side_index],
                device_id=(to_hop, to_core),
                device_id_type=MESH,
            ).start()
        if side_index == 1:
            pltpu.make_async_copy(
                source.at[rows_of(me)], place_ref.at[rows_of(me)], sem.at[1, side_index]
            ).start()

    def wait_side(place_ref, sem, side_index):
        rows = side_rows(sides[side_index])
        pltpu.make_async_copy(place_ref.at[rows], place_ref.at[rows], sem.at[1, side_index]).wait()

    def wait_sent(source, sem):
        for side_index, rows in ((0, half), (1, half - cap)):
            part = source.at[pl.ds(0, rows)]
            pltpu.make_async_copy(part, part, sem.at[0, side_index]).wait()

    loads[0].wait()
    loads[1].wait()
    for side_index, side in enumerate(sides):
        rows = side_rows(side)
        boards = spread(board_col[rows, :], TILE) == 1.0

        @pl.loop(0, tiles)
        def _(tile):
            projected = mm(child[rows, :], proj[:, columns(tile)])
            raw = child[rows, columns(tile)]
            merged[rows, columns(tile)] = jnp.where(boards, projected, raw.astype(f32)).astype(bf16)

        if side_index == 0:
            loads[2].wait()
            for copy in loads[3:]:
                copy.start()
        weights = spread(weight_col[rows, :], TILE)

        @pl.loop(0, tiles)
        def _(tile):
            value = mm(merged[rows, :], q[:, columns(tile)]) + q_bias[:, columns(tile)]
            gate = sigmoid(value)
            act = value * gate
            message[rows, columns(tile)] = (weights * act).astype(bf16)
            scaled_slope[rows, columns(tile)] = weights * (gate + act * (1.0 - gate))

        if side_index == 0:
            pl.semaphore_wait(barrier, devices - 1)
        send_info(side_index)
        send_side(message, arrived, msg_sem, side_index)

    loads[3].wait()
    loads[4].wait()

    @pl.loop(0, tiles)
    def _(tile):
        pre[:, columns(tile)] = mm(parent[...], w[pl.ds(0, width), columns(tile)]) + w_bias[:, columns(tile)]

    info_all = pltpu.make_async_copy(info_in, info_in, info_sem.at[1])
    info_all.wait()
    lane16 = lax.broadcasted_iota(jnp.int32, (cap, 128), 1)
    down16 = lax.broadcasted_iota(jnp.int32, (cap, 128), 0)
    for device in range(devices):
        got = jnp.broadcast_to(info_in[device], (cap, 128))
        at = slice(device * cap, (device + 1) * cap)
        got_weight[at, :] = jnp.broadcast_to(
            jnp.sum(jnp.where(lane16 == down16, got, 0.0), axis=1, keepdims=True), (cap, 128)
        )
        got_slot[at, :] = jnp.broadcast_to(
            jnp.sum(jnp.where(lane16 == down16 + cap, got, 0.0), axis=1, keepdims=True), (cap, 128)
        )

    for part in range(parents // 128):
        want = (lax.broadcasted_iota(jnp.int32, (128, 128), 1) + part * 128).astype(f32)
        weight_sum = jnp.zeros((1, 128), f32)
        for block in range(slots // 128):
            at = slice(block * 128, (block + 1) * 128)
            hit = got_slot[at, :] == want
            table_rows[at, part * 128 : (part + 1) * 128] = jnp.where(hit, 1.0, 0.0).astype(bf16)
            weight_sum = weight_sum + jnp.sum(jnp.where(hit, got_weight[at, :], 0.0), axis=0, keepdims=True)
        inverse = 1.0 / jnp.maximum(weight_sum, 1.0)
        shrink[part * 128 : (part + 1) * 128, :] = jnp.broadcast_to(column(inverse), (128, 128))
        for block in range(slots // 128):
            at = slice(block * 128, (block + 1) * 128)
            hit = got_slot[at, :] == want
            term = jnp.where(hit, jnp.broadcast_to(inverse, (128, 128)), 0.0)
            if part == 0:
                slot_shrink[at, :] = term
            else:
                slot_shrink[at, :] = slot_shrink[at, :] + term
    for block in range(slots // 128):
        at = slice(block * 128, (block + 1) * 128)
        slot_shrink[at, :] = jnp.broadcast_to(
            jnp.sum(slot_shrink[at, :], axis=1, keepdims=True), (128, 128)
        )

    def add_messages(side_index):
        rows = side_rows(sides[side_index])

        @pl.loop(0, tiles)
        def _(tile):
            moved[rows, columns(tile)] = mm(arrived[rows, :], w[pl.ds(width, width), columns(tile)]).astype(bf16)

        @pl.loop(0, tiles)
        def _(tile):
            pre[:, columns(tile)] = pre[:, columns(tile)] + spread(shrink[...], TILE) * contract_rows(
                table_rows[rows, :], moved[rows, columns(tile)]
            )

    wait_side(arrived, msg_sem, 1)
    add_messages(1)
    loads[5].wait()
    wait_side(arrived, msg_sem, 0)
    add_messages(0)

    @pl.loop(0, parents // BLOCK)
    def _(block):
        at = columns(block, BLOCK)
        value = pre[at, :]
        turn = cot[at, :]
        gate = sigmoid(value)
        act = value * gate
        inv = lax.rsqrt(jnp.sum(act * act, axis=1, keepdims=True) + 1e-06)
        share = jnp.sum(turn * act, axis=1, keepdims=True) * (inv * inv * inv)
        emb[at, :] = (act * inv).astype(bf16)
        grad_pre[at, :] = ((turn * inv - act * share) * (gate + act * (1.0 - gate))).astype(bf16)

    for side_index, side in enumerate(sides):
        rows = side_rows(side)
        shrinks = spread(slot_shrink[rows, :], WIDE)

        @pl.loop(0, wides)
        def _(tile):
            grad_moved[rows, columns(tile, WIDE)] = (
                shrinks * mm(table_rows[rows, :], grad_pre[:, columns(tile, WIDE)])
            ).astype(bf16)

        @pl.loop(0, wides)
        def _(tile):
            turned = w[pl.ds(pl.multiple_of(width + tile * WIDE, WIDE), WIDE), :]
            back_out[rows, columns(tile, WIDE)] = times_transpose(grad_moved[rows, :], turned).astype(bf16)

        send_side(back_out, back_in, back_sem, side_index)

    sums = Sums(hop, core, groups, held, inbox, total, (sum_send, sum_recv, sum_out, sum_in))
    w_groups = [g for g, (first, _, _) in enumerate(groups) if first < 2 * width]
    q_groups = [g for g, (first, _, _) in enumerate(groups) if 2 * width <= first < 3 * width]
    p_groups = [g for g, (first, _, _) in enumerate(groups) if first >= 3 * width]

    @pl.loop(0, tiles)
    def _(tile):
        held[pl.ds(0, width), columns(tile)] = contract_rows(parent[...], grad_pre[:, columns(tile)]).astype(bf16)

    for group in w_groups[: len(w_groups) // 2]:
        sums.halve(group, 0)

    @pl.loop(0, tiles)
    def _(tile):
        held[pl.ds(width, width), columns(tile)] = contract_rows(
            arrived[...], grad_moved[:, columns(tile)]
        ).astype(bf16)

    for group in w_groups[len(w_groups) // 2 :]:
        sums.halve(group, 0)
    bias_held[0, 0:1, :] = mm(jnp.ones((16, parents), bf16), grad_pre[...])[0:1, :]

    def parent_gradient():
        @pl.loop(0, tiles)
        def _(tile):
            parent[:, columns(tile)] = times_transpose(grad_pre[...], w[columns(tile), :]).astype(bf16)

        wait_sent(message, msg_sem)

    def child_front(side_index):
        rows = side_rows(sides[side_index])

        @pl.loop(0, tiles)
        def _(tile):
            grad_moved[rows, columns(tile)] = (
                scaled_slope[rows, columns(tile)] * back_in[rows, columns(tile)].astype(f32)
            ).astype(bf16)

    def weight_sums(side_index, left, grads, partial, base):
        rows = side_rows(sides[side_index])

        @pl.loop(0, tiles)
        def _(tile):
            value = contract_rows(left[rows, :], grads[rows, columns(tile)])
            if side_index == 1:
                partial[:, columns(tile)] = value
            else:
                held[pl.ds(base, width), columns(tile)] = (value + partial[:, columns(tile)]).astype(bf16)

    def child_middle(side_index):
        rows = side_rows(sides[side_index])
        boards = spread(board_col[rows, :], TILE) == 1.0

        @pl.loop(0, tiles)
        def _(tile):
            value = times_transpose(grad_moved[rows, :], q[columns(tile), :])
            moved[rows, columns(tile)] = jnp.where(boards, value, 0.0).astype(bf16)
            scaled_slope[rows, columns(tile)] = jnp.where(boards, 0.0, value)

    def child_end(side_index):
        rows = side_rows(sides[side_index])

        @pl.loop(0, tiles)
        def _(tile):
            value = times_transpose(moved[rows, :], proj[columns(tile), :])
            message[rows, columns(tile)] = (scaled_slope[rows, columns(tile)] + value).astype(bf16)

    bias_copies = []

    def send_bias(level):
        copy = pltpu.make_async_remote_copy(
            src_ref=bias_held.at[level],
            dst_ref=bias_in.at[level],
            send_sem=bias_sem.at[0, level],
            recv_sem=bias_sem.at[1, level],
            device_id=partner(hop, core, level - 1),
            device_id_type=MESH,
        )
        copy.start()
        bias_copies.append(copy)

    def fold_bias(level):
        bias_copies[level].wait_recv()
        both = bias_held[level] + bias_in[level]
        if level < levels - 1:
            bias_held[level + 1] = both
            send_bias(level + 1)
        else:
            bias_out[...] = both

    def near_children():
        child_front(1)
        weight_sums(1, merged, grad_moved, pre, 2 * width)
        child_middle(1)
        weight_sums(1, child, moved, cot, 3 * width)
        child_end(1)

    def far_q():
        child_front(0)
        weight_sums(0, merged, grad_moved, pre, 2 * width)

    def far_p():
        child_middle(0)
        weight_sums(0, child, moved, cot, 3 * width)

    def send_q():
        for group in q_groups:
            sums.halve(group, 0)
        bias_held[0, 1:2, :] = mm(jnp.ones((16, slots), bf16), grad_moved[...])[0:1, :]
        send_bias(0)

    def far_end():
        child_end(0)

    main = [
        parent_gradient,
        lambda: wait_side(back_in, back_sem, 1),
        near_children,
        lambda: wait_side(back_in, back_sem, 0),
        far_q,
        send_q,
        far_p,
        lambda: [sums.halve(group, 0) for group in p_groups],
        far_end,
    ]
    done = [0] * (len(groups) + 1)
    for turn in SCHEDULE:
        at = done[turn]
        done[turn] += 1
        if turn == 0:
            main[at]()
        elif at < sums.levels:
            sums.fold(turn - 1, at)
            if turn - 1 == q_groups[0]:
                fold_bias(at)
        else:
            sums.gather(turn - 1, 2 * sums.levels - 1 - at)

    sums.finish()
    for copy in bias_copies:
        copy.wait_send()
    wait_sent(back_out, back_sem)
    sent = info_out.at[pl.ds(0, devices - 1)]
    pltpu.make_async_copy(sent, sent, info_sem.at[0]).wait()


GROUPS = [("cxyim", 2), ("cyxim", 2), ("cxyim", 2), ("cyxim", 2), ("cxyim", 4), ("cyxim", 4), ("cxyim", 4), ("cyxim", 4), ("cxyim", 4), ("cyxim", 4), ("cxyim", 4), ("cyxim", 4)]
SCHEDULE = [
    1, 2, 0, 3, 4, 1, 0, 2, 0, 0, 0, 0, 4, 3, 1, 2, 0, 5, 0, 7, 8, 1, 2, 6, 4, 0, 7, 1, 5, 8, 2, 6, 11, 4, 12, 3,
    10, 7, 2, 6, 9, 1, 3, 11, 5, 12, 4, 10, 3, 9, 2, 8, 7, 1, 6, 11, 5, 12, 3, 8, 9, 4, 11, 10, 1, 2, 8, 3, 7, 4, 9, 6,
    5, 7, 12, 10, 5, 2, 6, 1, 9, 12, 4, 3, 11, 10, 5, 6, 9, 1, 8, 8, 12, 11, 7, 5, 12, 6, 9, 10, 7, 11, 3, 2, 5, 12, 10, 4,
    9, 8, 12, 11, 6, 10, 9, 7, 3, 8, 4, 6, 9, 12, 11, 10, 5, 8, 10, 11, 7,
]


def sum_groups(width):
    groups, first = [], 0
    for order, share in GROUPS:
        groups.append((first, width // share, order))
        first += width // share
    return groups


def inbox_rows(groups):
    total = 0
    for _, size, order in groups:
        for kind in order:
            size = size if kind == "i" else size // 2
            total += size
    return total


def widen_kernel(
    emb,
    child,
    parent,
    total,
    biases,
    emb_out,
    child_out,
    parent_out,
    proj_out,
    q_out,
    q_bias_out,
    w_out,
    w_bias_out,
    wide,
    w_bias,
    q_bias,
    write_sem,
    other_sem,
):
    slots, rows, width = wide.shape
    w_bias[...] = biases[0, :]
    q_bias[...] = biases[1, :]
    others = [
        pltpu.make_async_copy(source, place, other_sem.at[index])
        for index, (source, place) in enumerate(((child, child_out), (w_bias, w_bias_out), (q_bias, q_bias_out)))
    ]
    for copy in others:
        copy.start()
    pieces = []
    for source, place in ((parent, parent_out), (emb, emb_out)):
        for first in range(0, place.shape[0], rows):
            pieces.append((source, first, place, first))
    base = 0
    for place in (w_out, q_out, proj_out):
        for first in range(0, place.shape[0], rows):
            pieces.append((total, base + first, place, first))
        base += place.shape[0]
    def write(index):
        _, _, place, first = pieces[index]
        slot = index % slots
        return pltpu.make_async_copy(wide.at[slot], place.at[pl.ds(first, rows)], write_sem.at[slot])

    for index, (source, first, _, _) in enumerate(pieces):
        if index >= slots:
            write(index - slots).wait()
        wide[index % slots] = source[first : first + rows, :].astype(jnp.float32)
        write(index).start()
    for index in range(len(pieces) - slots, len(pieces)):
        write(index).wait()
    for copy in others:
        copy.wait()


def widen(emb, child, parent, total, biases):
    width = emb.shape[1]
    slots, rows = 8, 256
    shape, f32 = jax.ShapeDtypeStruct, jnp.float32
    hbm = pl.BlockSpec(memory_space=pl.ANY)
    vmem = pl.BlockSpec(memory_space=pltpu.VMEM)
    return pl.pallas_call(
        widen_kernel,
        name="widen",
        out_shape=(
            shape(emb.shape, f32),
            shape(child.shape, child.dtype),
            shape(parent.shape, f32),
            shape((width, width), f32),
            shape((width, width), f32),
            shape((width,), f32),
            shape((2 * width, width), f32),
            shape((width,), f32),
        ),
        in_specs=[vmem, vmem, vmem, vmem, vmem],
        out_specs=(hbm,) * 8,
        scratch_shapes=[
            pltpu.VMEM((slots, rows, width), f32),
            pltpu.VMEM((width,), f32),
            pltpu.VMEM((width,), f32),
            pltpu.SemaphoreType.DMA((slots,)),
            pltpu.SemaphoreType.DMA((3,)),
        ],
        compiler_params=pltpu.CompilerParams(vmem_limit_bytes=36 << 20),
    )(emb, child, parent, total, biases)


def fused_body(
    child_feats,
    board_mask,
    importance,
    parent_slot,
    send_counts,
    parent_feats,
    proj_weight,
    q_weight,
    q_bias,
    w_weight,
    w_bias,
    emb_cotangent,
):
    slots, width = child_feats.shape
    parents = parent_feats.shape[0]
    devices = send_counts.shape[1]
    groups = sum_groups(width)
    levels = devices.bit_length() - 1
    f32, bf16 = jnp.float32, jnp.bfloat16
    vmem = pl.BlockSpec(memory_space=pltpu.VMEM)
    hbm = pl.BlockSpec(memory_space=pl.ANY)
    dma = pltpu.SemaphoreType.DMA
    shape = jax.ShapeDtypeStruct
    emb, grad_child, grad_parent, total, biases = pl.pallas_call(
        functools.partial(layer_kernel, groups),
        name="layer",
        out_shape=(
            pltpu.VMEM((parents, width), bf16),
            pltpu.VMEM((slots, width), bf16),
            pltpu.VMEM((parents, width), bf16),
            pltpu.VMEM((4 * width, width), bf16),
            pltpu.VMEM((2, width), f32),
        ),
        in_specs=[hbm] * 12,
        out_specs=(vmem, vmem, vmem, vmem, vmem),
        scratch_shapes=[
            pltpu.VMEM((slots, width), bf16),
            pltpu.VMEM((width, width), bf16),
            pltpu.VMEM((width, width), bf16),
            pltpu.VMEM((2 * width, width), bf16),
            pltpu.VMEM((parents, width), f32),
            pltpu.VMEM((slots, width), bf16),
            pltpu.VMEM((slots, width), f32),
            pltpu.VMEM((slots, width), bf16),
            pltpu.VMEM((slots, width), bf16),
            pltpu.VMEM((parents, width), f32),
            pltpu.VMEM((slots, parents), bf16),
            pltpu.VMEM((parents, width), bf16),
            pltpu.VMEM((slots, width), bf16),
            pltpu.VMEM((slots, width), bf16),
            pltpu.VMEM((slots, width), bf16),
            pltpu.VMEM((4 * width, width), bf16),
            pltpu.VMEM((inbox_rows(groups), width), bf16),
            pltpu.VMEM((slots, 128), f32),
            pltpu.VMEM((slots, 128), f32),
            pltpu.VMEM((parents, 128), f32),
            pltpu.VMEM((slots, 128), f32),
            pltpu.VMEM((slots, 128), f32),
            pltpu.VMEM((slots, 128), f32),
            pltpu.VMEM((devices, 1, 128), f32),
            pltpu.VMEM((devices, 1, 128), f32),
            pltpu.VMEM((levels, 2, width), f32),
            pltpu.VMEM((levels, 2, width), f32),
            pltpu.VMEM((slots // 128, 128), f32),
            pltpu.VMEM((slots // 128, 128), jnp.int32),
            pltpu.VMEM((slots // 128, 128), jnp.int32),
            pltpu.VMEM(send_counts.shape, jnp.int32),
            pltpu.VMEM((1, width), f32),
            pltpu.VMEM((1, width), f32),
            dma((6,)),
            dma((6,)),
            dma((2,)),
            dma((2, 2)),
            dma((2, 2)),
            dma((2, levels)),
        ]
        + [dma((len(groups), len(groups[0][2])))] * 4,
        compiler_params=pltpu.CompilerParams(
            collective_id=1, has_side_effects=True, vmem_limit_bytes=50 << 20
        ),
        cost_estimate=pl.CostEstimate(
            flops=36 * slots * width * width, bytes_accessed=40 << 20, transcendentals=3 * parents * width
        ),
    )(
        child_feats,
        importance.reshape(-1, 128),
        board_mask.reshape(-1, 128),
        parent_slot.reshape(-1, 128),
        send_counts,
        parent_feats,
        proj_weight,
        q_weight,
        q_bias.reshape(1, -1),
        w_weight,
        w_bias.reshape(1, -1),
        emb_cotangent,
    )
    return widen(emb, grad_child, grad_parent, total, biases)


def solution(mesh):
    rows = P(("hop", "par"), None)
    flat = P(("hop", "par"))
    fused = mesh.shape["hop"] == 16 and mesh.shape["par"] == 2
    return jax.shard_map(
        fused_body if fused else plain_body,
        mesh=mesh,
        in_specs=(rows, flat, flat, flat, rows, rows, P(), P(), P(), P(), P(), rows),
        out_specs=(rows, rows, rows, P(), P(), P(), P(), P()),
        check_vma=False,
    )
```
